256 devices in a mesh: obj: 4 (over z_lo, core), plane: 4 (over y), tile: 16 (over x, z_hi).
Axes of the slice: x: 4, y: 4, z: 8 (z_hi: 4, z_lo: 2; z = z_hi * 2 + z_lo), core: 2. Of those that a mesh axis runs over, the one named last changes fastest.
Arguments:
- tokens: bfloat16 [8, 3, 32, 32, 1024], P('obj', None, 'plane', 'tile'), may hold values from -6 to 6
- gout: bfloat16 [8, 3, 128, 128, 128], P('obj', None, 'plane', 'tile'), may hold values from -6 to 6
- deconv_weight: bfloat16 [1024, 2048], replicated, may hold values from -0.1875 to 0.1875
- deconv_bias: float32 [128], replicated, may hold values from -4 to 4
- conv_kernels: bfloat16 [2, 1152, 128], replicated, may hold values from -0.1875 to 0.1875
- conv_biases: float32 [2, 128], replicated, may hold values from -4 to 4
Outputs:
- d_tokens: bfloat16 [8, 3, 32, 32, 1024], P('obj', None, 'plane', 'tile')
- d_deconv_weight: float32 [1024, 2048], P(('obj', 'plane', 'tile'))
- d_deconv_bias: float32 [128], replicated
- d_conv_kernels: float32 [2, 1152, 128], replicated
- d_conv_biases: float32 [2, 128], replicated
The draws below stay inside these ranges and needn't reach their ends.
All inputs are finite; a program needn't handle non-finite values.
Results may differ from the reference program's by a relative error of at most 0.01.
Values may be sent and summed in bfloat16 or wider, within the bound.
A program may use at most 128 MiB of HBM per device.

```python
import jax
import jax.numpy as jnp
from jax import lax

D = 1024
C = 128
LAYERS = 2
NOBJ = 8
TSIDE = 32
SIDE = 128


def levels(stream_key, shape, split, low, high):
    def one(position, shards_of):
        steps = jax.random.uniform(jax.random.fold_in(jax.random.fold_in(stream_key, 6), position), (shards_of,), jnp.float32, low / len(split), high / len(split))
        return jnp.repeat(jnp.exp(steps), shape[position] // shards_of).reshape((-1,) + (1,) * (len(shape) - position - 1))

    gain = one(*split[0])
    for cut in split[1:]:
        gain = gain * one(*cut)
    return gain


def noise(rng, dims, scale, bound, cuts=(), held_as=jnp.bfloat16):
    result = scale * jax.random.normal(rng, dims, jnp.float32)
    if cuts:
        result = result * levels(rng, dims, cuts, -0.22, 0.18)
    return jnp.clip(result, -bound, bound).astype(held_as)


def setup_inputs(seed: int = 0) -> dict:
    splits = jax.random.split(jax.random.key(seed), 7)
    tokens = noise(splits[0], (NOBJ, 3, TSIDE, TSIDE, D), 1.0, 6.0, ((0, 4), (2, 4), (3, 16)))
    gout = noise(splits[1], (NOBJ, 3, SIDE, SIDE, C), 1.0, 6.0, ((0, 4), (2, 4), (3, 16)))
    deconv_weight = noise(splits[2], (D, 16 * C), D ** -0.5, 0.1875)
    deconv_bias = noise(splits[3], (C,), 1.0, 4.0, (), jnp.float32)
    conv_kernels = noise(splits[4], (LAYERS, 9 * C, C), (9 * C) ** -0.5, 0.1875)
    conv_biases = noise(splits[5], (LAYERS, C), 0.7, 4.0, (), jnp.float32)
    return dict(tokens=tokens, gout=gout, deconv_weight=deconv_weight, deconv_bias=deconv_bias, conv_kernels=conv_kernels, conv_biases=conv_biases)


def columns(padded, height, breadth, flipped):
    pieces = []
    for tap_y in range(3):
        for tap_x in range(3):
            shift_y = 2 - tap_y if flipped else tap_y
            shift_x = 2 - tap_x if flipped else tap_x
            pieces.append(padded[..., shift_y:shift_y + height, shift_x:shift_x + breadth, :])
    return jnp.concatenate(pieces, axis=-1)

def convolve(padded, kernel, height, breadth, flipped):
    gathered = columns(padded, height, breadth, flipped)
    products = jnp.dot(gathered.reshape(-1, gathered.shape[-1]), kernel, preferred_element_type=jnp.float32)
    return products.reshape(padded.shape[:-3] + (height, breadth, kernel.shape[1]))

def upsample(tokens_here, weight, offsets):
    planes, tok_rows, tok_cols, fan_width = tokens_here.shape
    products = jnp.dot(tokens_here.reshape(-1, fan_width), weight, preferred_element_type=jnp.float32)
    products = products.reshape(planes, tok_rows, tok_cols, 4, 4, -1).transpose(0, 1, 3, 2, 4, 5)
    return products.reshape(planes, 4 * tok_rows, 4 * tok_cols, -1) + offsets

def tap_layout(gradient):
    planes, height, breadth, channels = gradient.shape
    blocks = gradient.reshape(planes, height // 4, 4, breadth // 4, 4, channels).transpose(0, 1, 3, 2, 4, 5)
    return blocks.reshape(-1, 16 * channels)

def contexts(row_sum, col_sum, extent):
    row_mean = row_sum / extent
    col_mean = col_sum / extent
    row_ctx = jnp.stack([row_mean[1], row_mean[0], col_mean[0]])
    col_ctx = jnp.stack([row_mean[2], col_mean[2], col_mean[1]])
    return (row_ctx, col_ctx)

def adjoint_contexts(row_sum, col_sum, extent):
    row_adjoint = jnp.stack([row_sum[1], row_sum[0], col_sum[0]])
    col_adjoint = jnp.stack([row_sum[2], col_sum[2], col_sum[1]])
    return (row_adjoint / extent, col_adjoint / extent)

def flip_kernel(kernel):
    channels = kernel.shape[1]
    return kernel.reshape(9, channels, channels).transpose(0, 2, 1).reshape(9 * channels, channels)

def one_object(tokens_here, grad_out, weight, offsets, kernels, kernel_bias):
    hidden = upsample(tokens_here, weight, offsets)
    planes, height, breadth, channels = hidden.shape
    extent = height
    stored = []
    for layer_index in range(kernels.shape[0]):
        row_ctx, col_ctx = contexts(lax.optimization_barrier(jnp.sum(hidden, 2)), lax.optimization_barrier(jnp.sum(hidden, 1)), extent)
        preact = hidden + row_ctx[:, :, None, :] + col_ctx[:, None, :, :]
        activated = jax.nn.silu(preact).astype(jnp.bfloat16)
        padded = jnp.pad(activated, ((0, 0), (1, 1), (1, 1), (0, 0)))
        kernel = kernels[layer_index]
        conv_out = lax.map(lambda single: convolve(single, kernel, height, breadth, False), padded)
        hidden = hidden + conv_out + kernel_bias[layer_index]
        stored.append((preact, padded))
    gradient = grad_out.astype(jnp.float32)
    kernel_grads = []
    bias_grads = []
    for layer_index in reversed(range(kernels.shape[0])):
        preact, padded = stored[layer_index]
        grad_bf = gradient.astype(jnp.bfloat16)
        bias_grads.insert(0, lax.optimization_barrier(jnp.sum(gradient, (0, 1, 2))))
        grad_pad = jnp.pad(grad_bf, ((0, 0), (1, 1), (1, 1), (0, 0)))
        flipped = flip_kernel(kernels[layer_index])
        act_grad = lax.map(lambda single: convolve(single, flipped, height, breadth, True), grad_pad)

        def plane_kernel_grad(object_pair):
            gathered = columns(object_pair[0], height, breadth, False)
            return lax.dot_general(gathered.reshape(-1, gathered.shape[-1]), object_pair[1].reshape(-1, channels), (((0,), (0,)), ((), ())), preferred_element_type=jnp.float32)
        kernel_grads.insert(0, lax.optimization_barrier(jnp.sum(lax.map(plane_kernel_grad, (padded, grad_bf)), 0)))
        sigmoid_pre = jax.nn.sigmoid(preact)
        pre_grad = act_grad * sigmoid_pre * (1.0 + preact * (1.0 - sigmoid_pre))
        row_adjoint, col_adjoint = adjoint_contexts(lax.optimization_barrier(jnp.sum(pre_grad, 2)), lax.optimization_barrier(jnp.sum(pre_grad, 1)), extent)
        gradient = gradient + pre_grad + row_adjoint[:, :, None, :] + col_adjoint[:, None, :, :]
    grad_bf = gradient.astype(jnp.bfloat16)
    tap_grads = tap_layout(grad_bf)
    tok_grad = lax.dot_general(tap_grads, weight, (((1,), (1,)), ((), ())), preferred_element_type=jnp.float32)
    tok_grad = tok_grad.astype(jnp.bfloat16).reshape(tokens_here.shape)
    tok_flat = tokens_here.reshape(-1, tokens_here.shape[-1])
    weight_grad = lax.dot_general(tok_flat, tap_grads, (((0,), (0,)), ((), ())), preferred_element_type=jnp.float32)
    return (tok_grad, weight_grad, lax.optimization_barrier(jnp.sum(gradient, (0, 1, 2))), jnp.stack(kernel_grads), jnp.stack(bias_grads))

def reference(tokens, gout, deconv_weight, deconv_bias, conv_kernels, conv_biases):
    results = lax.map(lambda object_pair: one_object(object_pair[0], object_pair[1], deconv_weight, deconv_bias, conv_kernels, conv_biases), (tokens, gout))
    return (results[0], lax.optimization_barrier(jnp.sum(results[1], 0)), lax.optimization_barrier(jnp.sum(results[2], 0)), lax.optimization_barrier(jnp.sum(results[3], 0)), lax.optimization_barrier(jnp.sum(results[4], 0)))
```

```python
import jax
import jax.numpy as jnp
from jax import lax
from jax.experimental import pallas as pl
from jax.experimental.pallas import tpu as pltpu
from jax.sharding import PartitionSpec as P

MESH = pl.DeviceIdType.MESH
F32 = jnp.float32
BF16 = jnp.bfloat16
IMAGES = 6
ROWS = 32
COLS = 8
CELLS = ROWS * COLS
TOTAL = IMAGES * CELLS
PADDED = (ROWS + 2) * COLS

HALO = (
    (-1, 0, ("row", 0), ("row", 1)),
    (1, 0, ("row", 1), ("row", 0)),
    (0, -1, ("col", 0), ("col", 1)),
    (0, 1, ("col", 1), ("col", 0)),
    (-1, -1, ("row", 0), ("corner", 3)),
    (-1, 1, ("row", 0), ("corner", 2)),
    (1, -1, ("row", 1), ("corner", 1)),
    (1, 1, ("row", 1), ("corner", 0)),
)


def both(first, second):
    return jnp.logical_and(first, second)


def kernel(
    x_ref, g_ref, w_ref, db_ref, k_ref, cb_ref,
    dtok_ref, dw_ref, dk_ref, bias_ref,
    hid, pre0, pre1, act0, act1, grad, nat, dzed, kcat, col,
    centre, leftpad, rightpad, rowpart, colpart, rowband, colband,
    rowhalf, rowtwo, colzero,
    zs, zr, m1s, m1r, m2s, m2r, m3s, m3r, m4s, m4r,
    zsem, m1sem, m2sem, m3ss, m3rs, m4ss, m4rs,
    hsrow, hscol, hrrow, hrcol, hrcor, hss, hrs,
    xg, xsem, tg, gg, tsem, dwk, dws, dwr, dwsem, fin, fins, finr, finsem,
    dka, dks, dkr, dksem, dkbs, dkbr, dkbsem, dkcs, dkcr, dkcsem,
):
    obj, y, t = lax.axis_index("obj"), lax.axis_index("plane"), lax.axis_index("tile")
    x, z = t // 4, lax.rem(t, 4)
    mine = obj * 4 + y

    def group_a(d):
        other = lax.rem(mine + d, 16)
        return other, {"obj": other // 4, "plane": lax.rem(other, 4)}

    def group_b(d):
        other = lax.rem(t + d, 16)
        return other, {"tile": other}

    def send(src, dst, send_sem, recv_sem, where):
        copy = pltpu.make_async_remote_copy(
            src_ref=src, dst_ref=dst, send_sem=send_sem, recv_sem=recv_sem,
            device_id=where, device_id_type=MESH,
        )
        copy.start()

    def finish(ref, sem):
        pltpu.make_async_copy(ref, ref, sem).wait()

    hrrow[...] = jnp.zeros_like(hrrow)
    hrcol[...] = jnp.zeros_like(hrcol)
    hrcor[...] = jnp.zeros_like(hrcor)
    barrier = pltpu.get_barrier_semaphore()

    def greet(where):
        pl.semaphore_signal(barrier, inc=1, device_id=where, device_id_type=MESH)

    for d in range(1, 16):
        greet(group_a(d)[1])
        greet(group_b(d)[1])
    for dy in range(1, 4):
        for dx in range(1, 4):
            greet({"plane": lax.rem(y + dy, 4), "tile": lax.rem(x + dx, 4) * 4 + z})

    def inside(dy, dt):
        row_ok = both(y + dy >= 0, y + dy <= 3)
        return both(row_ok, both(t + dt >= 0, t + dt <= 15))

    diagonals = 0
    for dy, dt in ((-1, -1), (-1, 1), (1, -1), (1, 1)):
        ok = inside(dy, dt)

        @pl.when(ok)
        def _(dy=dy, dt=dt):
            greet({"plane": y + dy, "tile": t + dt})

        diagonals = diagonals + ok.astype(jnp.int32)

    for j in range(2):
        for part in range(4):
            products = jnp.dot(
                x_ref[j * 48:(j + 1) * 48, :], w_ref[:, part * 512:(part + 1) * 512],
                preferred_element_type=F32,
            )
            for b in range(4):
                hid[pl.ds(part * 8 + 4 * j + b, 48, stride=32), :] = (
                    products[:, b * 128:(b + 1) * 128] + db_ref[...]
                )
    for l in range(2):
        for tap in range(9):
            kcat[l, :, tap * 128:(tap + 1) * 128] = k_ref[l, tap * 128:(tap + 1) * 128, :]
    xg[mine] = x_ref[...]
    grad[...] = g_ref[...].astype(F32)

    pl.semaphore_wait(barrier, 39 + diagonals)

    partner = {"obj": lax.rem(obj + 2, 4)}
    send(xg.at[mine], xg.at[mine], xsem.at[0], xsem.at[1], partner)

    def halo_start(h, ref):
        for side, at in ((0, 0), (1, CELLS - COLS)):
            hsrow[h, side] = jnp.concatenate(
                [ref[i * CELLS + at:i * CELLS + at + COLS, :] for i in range(IMAGES)], axis=0
            ).astype(BF16)
        hscol[h, 0] = ref[pl.ds(0, IMAGES * ROWS, stride=COLS), :].astype(BF16)
        hscol[h, 1] = ref[pl.ds(COLS - 1, IMAGES * ROWS, stride=COLS), :].astype(BF16)
        sources = {"row": hsrow, "col": hscol}
        targets = {"row": hrrow, "col": hrcol, "corner": hrcor}
        for n, (dy, dt, src, dst) in enumerate(HALO):

            @pl.when(inside(dy, dt))
            def _(n=n, dy=dy, dt=dt, src=src, dst=dst):
                send(
                    sources[src[0]].at[h, src[1]], targets[dst[0]].at[h, dst[1]],
                    hss.at[h, n], hrs.at[h, n], {"plane": y + dy, "tile": t + dt},
                )

    def halo_finish(h, ref):
        sources = {"row": hsrow, "col": hscol}
        targets = {"row": hrrow, "col": hrcol, "corner": hrcor}
        for n, (dy, dt, src, dst) in enumerate(HALO):

            @pl.when(inside(-dy, -dt))
            def _(n=n, dst=dst):
                finish(targets[dst[0]].at[h, dst[1]], hrs.at[h, n])

            @pl.when(inside(dy, dt))
            def _(n=n, src=src):
                finish(sources[src[0]].at[h, src[1]], hss.at[h, n])

        top, bottom = hrrow[h, 0].astype(F32), hrrow[h, 1].astype(F32)
        left, right = hrcol[h, 0].astype(F32), hrcol[h, 1].astype(F32)
        corners = [hrcor[h, c].astype(F32) for c in range(4)]
        last = PADDED - COLS
        for i in range(IMAGES):
            base = i * PADDED
            centre[base:base + COLS, :] = top[i * COLS:(i + 1) * COLS]
            centre[base + COLS:base + COLS + CELLS, :] = ref[i * CELLS:(i + 1) * CELLS, :]
            centre[base + last:base + PADDED, :] = bottom[i * COLS:(i + 1) * COLS]
            leftpad[pl.ds(base + COLS, ROWS, stride=COLS), :] = left[i * ROWS:(i + 1) * ROWS]
            rightpad[pl.ds(base + 2 * COLS - 1, ROWS, stride=COLS), :] = right[i * ROWS:(i + 1) * ROWS]
            first, final = i * COLS, (i + 1) * COLS - 1
            leftpad[base:base + 1, :] = corners[0][final:final + 1]
            leftpad[base + last:base + last + 1, :] = corners[2][final:final + 1]
            rightpad[base + COLS - 1:base + COLS, :] = corners[1][first:first + 1]
            rightpad[base + PADDED - 1:base + PADDED, :] = corners[3][first:first + 1]

    def shifted(i, flipped):
        base = pl.multiple_of(i * PADDED, 8)
        middle = centre[pl.ds(base, PADDED), :]
        place = lax.rem(lax.broadcasted_iota(jnp.int32, (PADDED, 128), 0), COLS)
        before = jnp.where(place == 0, leftpad[pl.ds(base, PADDED), :], pltpu.roll(middle, 1, 0))
        after = jnp.where(
            place == COLS - 1, rightpad[pl.ds(base, PADDED), :], pltpu.roll(middle, PADDED - 1, 0)
        )
        for tx, padded in enumerate((before, middle, after)):
            for ty in range(3):
                tap = (2 - ty) * 3 + (2 - tx) if flipped else ty * 3 + tx
                col[:, tap * 128:(tap + 1) * 128] = padded[ty * COLS:ty * COLS + CELLS].astype(BF16)

    def pool(ph, ref):
        rows = ref[pl.ds(0, IMAGES * ROWS, stride=COLS), :]
        for v in range(1, COLS):
            rows = rows + ref[pl.ds(v, IMAGES * ROWS, stride=COLS), :]
        rowpart[...] = rows
        for i in range(IMAGES):
            colpart[i * COLS:(i + 1) * COLS, :] = jnp.sum(
                ref[i * CELLS:(i + 1) * CELLS, :].reshape(ROWS, COLS, 128), axis=0
            )
        common = jnp.concatenate(
            [rowpart[0:64, :], rowpart[96:160, :], colpart[0:8, :], colpart[24:32, :]], axis=0
        )
        for d in range(1, 4):
            zd = lax.rem(z + d, 4)
            chunk = [rowpart[pl.ds(pl.multiple_of(96 * o + 64 + 8 * zd, 8), 8), :] for o in range(2)]
            zs[ph, d - 1] = jnp.concatenate([common] + chunk, axis=0).astype(BF16)
            send(zs.at[ph, d - 1], zr.at[ph, d - 1], zsem.at[ph, 0], zsem.at[ph, 1], {"tile": x * 4 + zd})
        m2s[ph] = jnp.concatenate([colpart[8:24, :], colpart[32:48, :]], axis=0).astype(BF16)
        for d in range(1, 4):
            send(m2s.at[ph], m2r.at[ph, d - 1], m2sem.at[ph, 0], m2sem.at[ph, 1], {"plane": lax.rem(y + d, 4)})
        finish(zr.at[ph], zsem.at[ph, 1])
        half = common[:128]
        two = jnp.concatenate(
            [rowpart[pl.ds(pl.multiple_of(96 * o + 64 + 8 * z, 8), 8), :] for o in range(2)], axis=0
        )
        for o in range(2):
            colzero[pl.ds(pl.multiple_of(32 * o + 8 * z, 8), 8), :] = colpart[24 * o:24 * o + 8, :]
        for d in range(1, 4):
            got = zr[ph, d - 1].astype(F32)
            half = half + got[:128]
            two = two + got[144:160]
            source = lax.rem(z + 4 - d, 4)
            for o in range(2):
                colzero[pl.ds(pl.multiple_of(32 * o + 8 * source, 8), 8), :] = got[128 + 8 * o:136 + 8 * o]
        m1s[ph] = half.astype(BF16)
        m3s[ph] = colzero[...].astype(BF16)
        m4s[ph] = two.astype(BF16)
        same = x == y
        for d in range(1, 4):
            send(m1s.at[ph], m1r.at[ph, d - 1], m1sem.at[ph, 0], m1sem.at[ph, 1], {"tile": lax.rem(x + d, 4) * 4 + z})
        for k in range(4):

            @pl.when(jnp.logical_not(both(same, x == k)))
            def _(k=k):
                send(m3s.at[ph], m3r.at[ph, y], m3ss.at[ph, k], m3rs.at[ph, y], {"plane": x, "tile": k * 4 + z})
                send(m4s.at[ph], m4r.at[ph, x], m4ss.at[ph, k], m4rs.at[ph, x], {"plane": k, "tile": y * 4 + z})

        @pl.when(same)
        def _():
            m3r[ph, y] = m3s[ph]
            m4r[ph, x] = m4s[ph]

        finish(m2r.at[ph], m2sem.at[ph, 1])
        finish(m1r.at[ph], m1sem.at[ph, 1])
        for k in range(4):

            @pl.when(jnp.logical_not(both(same, x == k)))
            def _(k=k):
                finish(m3r.at[ph, k], m3rs.at[ph, k])
                finish(m4r.at[ph, k], m4rs.at[ph, k])
                finish(m3s.at[ph], m3ss.at[ph, k])
                finish(m4s.at[ph], m4ss.at[ph, k])

        finish(zs.at[ph], zsem.at[ph, 0])
        for d in range(3):
            pass
        finish(m1r.at[ph], m1sem.at[ph, 0])
        finish(m2r.at[ph], m2sem.at[ph, 0])
        one = jnp.concatenate([colpart[8:24, :], colpart[32:48, :]], axis=0)
        for d in range(3):
            half = half + m1r[ph, d].astype(F32)
            one = one + m2r[ph, d].astype(F32)
        zero = m3r[ph, 0].astype(F32)
        two = m4r[ph, 0].astype(F32)
        for k in range(1, 4):
            zero = zero + m3r[ph, k].astype(F32)
            two = two + m4r[ph, k].astype(F32)
        share = 1.0 / 128.0
        for o in range(2):
            rowband[96 * o:96 * o + 32, :] = half[64 * o + 32:64 * o + 64] * share
            rowband[96 * o + 32:96 * o + 64, :] = half[64 * o:64 * o + 32] * share
            rowband[96 * o + 64:96 * o + 96, :] = zero[32 * o:32 * o + 32] * share
            colband[24 * o:24 * o + 8, :] = two[8 * o:8 * o + 8] * share
            colband[24 * o + 8:24 * o + 16, :] = one[16 * o + 8:16 * o + 16] * share
            colband[24 * o + 16:24 * o + 24, :] = one[16 * o:16 * o + 8] * share

    def add_bands(dst, src):
        for i in range(IMAGES):
            rb = rowband[i * ROWS:(i + 1) * ROWS, :]
            for v in range(COLS):
                at = pl.ds(i * CELLS + v, ROWS, stride=COLS)
                cb = colband[i * COLS + v:i * COLS + v + 1, :]
                dst[at, :] = src[at, :] + rb + cb

    def per_image(body):
        def step(i, carry):
            body(i, pl.ds(pl.multiple_of(i * CELLS, CELLS), CELLS))
            return carry

        lax.fori_loop(0, IMAGES, step, 0)

    halo_start(0, grad)
    pool(0, hid)
    add_bands(pre0, hid)

    def silu0(i, at):
        value = pre0[at, :]
        rounded = (value * jax.nn.sigmoid(value)).astype(BF16)
        act0[at, :] = rounded
        nat[at, :] = rounded.astype(F32)

    per_image(silu0)
    halo_start(1, nat)
    finish(xg.at[mine], xsem.at[1])
    theirs = lax.rem(obj + 2, 4) * 4 + y
    for d in range(1, 4):
        for n, slot in enumerate((mine, theirs)):
            send(xg.at[slot], xg.at[slot], xsem.at[2], xsem.at[3], {"plane": lax.rem(y + d, 4)})
    halo_finish(1, nat)

    def forward(i, at):
        shifted(i, False)
        out = jnp.dot(col[...], k_ref[0], preferred_element_type=F32)
        hid[at, :] = hid[at, :] + out + cb_ref[0]

    per_image(forward)
    pool(1, hid)
    add_bands(pre1, hid)

    def silu1(i, at):
        value = pre1[at, :]
        act1[at, :] = (value * jax.nn.sigmoid(value)).astype(BF16)

    per_image(silu1)
    halo_finish(0, grad)

    def backward(layer, pre, act):
        dka[...] = jnp.zeros_like(dka)

        def body(i, at):
            shifted(i, True)
            da = lax.dot_general(
                col[...], kcat[layer], (((1,), (1,)), ((), ())), preferred_element_type=F32
            )
            dka[...] += lax.dot_general(
                act[at, :], col[...], (((0,), (0,)), ((), ())), preferred_element_type=F32
            )
            value = pre[at, :]
            s = jax.nn.sigmoid(value)
            dzed[at, :] = da * s * (1.0 + value * (1.0 - s))

        per_image(body)

    def total(ref):
        return jnp.sum(jnp.sum(ref[...].reshape(TOTAL // 8, 8, 128), axis=0), axis=0, keepdims=True)

    def kernel_grad_start(layer, extra):
        extras = jnp.concatenate(extra + [jnp.zeros((8 - len(extra), 128), F32)], axis=0)
        for g in range(16):
            rows = [dka[8 * g:8 * g + 8, tap * 128:(tap + 1) * 128] for tap in range(9)]
            dks[layer, g] = jnp.concatenate(rows + [extras], axis=0).astype(BF16)
        for d in range(1, 16):
            other, where = group_a(d)
            send(dks.at[layer, other], dkr.at[layer, mine], dksem.at[layer, 0], dksem.at[layer, 1], where)
        dkr[layer, mine] = dks[layer, mine]

    def fifteen(ref, sem):
        finish(ref.at[pl.ds(0, 15)], sem)

    def sum16(ref, layer):
        def step(n, acc):
            return acc + ref[layer, n].astype(F32)

        return lax.fori_loop(1, 16, step, ref[layer, 0].astype(F32))

    def kernel_grad_second(layer):
        fifteen(dkr.at[layer], dksem.at[layer, 1])
        fifteen(dks.at[layer], dksem.at[layer, 0])
        dkbs[layer] = sum16(dkr, layer).astype(BF16)
        for d in range(1, 16):
            send(dkbs.at[layer], dkbr.at[layer, t], dkbsem.at[layer, 0], dkbsem.at[layer, 1], group_b(d)[1])
        dkbr[layer, t] = dkbs[layer]

    def kernel_grad_third(layer):
        fifteen(dkbr.at[layer], dkbsem.at[layer, 1])
        fifteen(dkbr.at[layer], dkbsem.at[layer, 0])
        dkcs[layer] = sum16(dkbr, layer).astype(BF16)
        for d in range(1, 16):
            send(dkcs.at[layer], dkcr.at[layer, mine], dkcsem.at[layer, 0], dkcsem.at[layer, 1], group_a(d)[1])
        dkcr[layer, mine] = dkcs[layer]

    def kernel_grad_finish(layer):
        fifteen(dkcr.at[layer], dkcsem.at[layer, 1])
        fifteen(dkcr.at[layer], dkcsem.at[layer, 0])
        for g in range(16):
            got = dkcr[layer, g].astype(F32)
            for tap in range(9):
                dk_ref[layer, tap * 128 + 8 * g:tap * 128 + 8 * g + 8, :] = got[8 * tap:8 * tap + 8]
            if g == 0:
                bias_ref[layer * 8:layer * 8 + 8, :] = got[72:80]

    backward(1, pre1, act1)
    kernel_grad_start(1, [total(grad)])
    pool(2, dzed)
    finish(xg.at[pl.ds(0, 6)], xsem.at[3])
    finish(xg.at[pl.ds(0, 6)], xsem.at[2])
    sibling = {"obj": obj + 1 - 2 * lax.rem(obj, 2)}
    core = lax.rem(obj, 2)
    for half in range(2):
        held = xg.at[pl.ds(pl.multiple_of((core + 2 * half) * 4, 4), 4)]
        send(held, held, xsem.at[4], xsem.at[5], sibling)

    def join(i, at):
        grad[at, :] = grad[at, :] + dzed[at, :]

    per_image(join)
    add_bands(grad, grad)

    def rounded(i, at):
        nat[at, :] = grad[at, :].astype(BF16).astype(F32)

    per_image(rounded)
    halo_start(2, nat)
    kernel_grad_second(1)
    halo_finish(2, nat)
    backward(0, pre0, act0)
    sum_grad, sum_dz = total(grad), total(dzed)
    kernel_grad_start(0, [sum_grad, sum_grad + 3.0 * sum_dz])
    pool(3, dzed)
    per_image(join)
    add_bands(grad, grad)
    for a in range(4):
        for b in range(4):
            for j in range(2):
                tg[a * 4 + b, j * 48:(j + 1) * 48, :] = grad[
                    pl.ds(a * 8 + 4 * j + b, 48, stride=32), :
                ].astype(BF16)
    for d in range(1, 16):
        other, where = group_a(d)
        send(tg.at[other], gg.at[mine], tsem.at[0], tsem.at[1], where)
    gg[mine] = tg[mine]
    kernel_grad_second(0)
    kernel_grad_third(1)
    taps = jnp.concatenate([tg[n] for n in range(16)], axis=1)
    for part in range(4):
        dtok_ref[:, part * 256:(part + 1) * 256] = lax.dot_general(
            taps, w_ref[part * 256:(part + 1) * 256, :], (((1,), (1,)), ((), ())),
            preferred_element_type=F32,
        ).astype(BF16)
    finish(xg.at[mine], xsem.at[0])
    finish(xg.at[pl.ds(0, 8)], xsem.at[5])
    finish(xg.at[pl.ds(0, 8)], xsem.at[4])
    fifteen(gg, tsem.at[1])
    fifteen(tg, tsem.at[0])
    taken = gg[...].reshape(1536, 128)
    for part in range(4):
        product = lax.dot_general(
            taken, xg[:, :, part * 256:(part + 1) * 256].reshape(1536, 256),
            (((0,), (0,)), ((), ())), preferred_element_type=F32,
        )
        dwk[part * 256:(part + 1) * 256, :] = product.T
    for other in range(16):
        dws[other] = jnp.concatenate(
            [dwk[pl.ds(other * 4 + r, 16, stride=64), :] for r in range(4)], axis=0
        ).astype(BF16)
    for d in range(1, 16):
        other, where = group_b(d)
        send(dws.at[other], dwr.at[t], dwsem.at[0], dwsem.at[1], where)
    dwr[t] = dws[t]
    kernel_grad_third(0)
    kernel_grad_finish(1)
    fifteen(dwr, dwsem.at[1])
    fifteen(dws, dwsem.at[0])
    fin[...] = lax.fori_loop(
        1, 16, lambda n, acc: acc + dwr[n].astype(F32), dwr[0].astype(F32)
    )
    for other in range(16):
        fins[other, 0:4, :] = fin[pl.ds(other, 4, stride=16), :]
        fins[other, 4:8, :] = jnp.zeros((4, 128), F32)
    for d in range(1, 16):
        other, where = group_a(d)
        send(fins.at[other], finr.at[mine], finsem.at[0], finsem.at[1], where)
    finr[mine] = fins[mine]
    kernel_grad_finish(0)
    fifteen(finr, finsem.at[1])
    fifteen(fins, finsem.at[0])
    for n in range(16):
        dw_ref[:, n * 128:(n + 1) * 128] = finr[n, 0:4, :]


def scratch():
    dma = pltpu.SemaphoreType.DMA
    vmem = pltpu.VMEM
    full = (TOTAL, 128)
    padded = (IMAGES * PADDED, 128)
    return [
        vmem(full, F32), vmem(full, F32), vmem(full, F32), vmem(full, BF16), vmem(full, BF16),
        vmem(full, F32), vmem(full, F32), vmem(full, F32), vmem((2, 128, 1152), BF16), vmem((CELLS, 1152), BF16),
        vmem(padded, F32), vmem(padded, F32), vmem(padded, F32),
        vmem((192, 128), F32), vmem((48, 128), F32), vmem((192, 128), F32), vmem((48, 128), F32),
        vmem((128, 128), F32), vmem((16, 128), F32), vmem((64, 128), F32),
        vmem((4, 3, 160, 128), BF16), vmem((4, 3, 160, 128), BF16),
        vmem((4, 128, 128), BF16), vmem((4, 3, 128, 128), BF16),
        vmem((4, 32, 128), BF16), vmem((4, 3, 32, 128), BF16),
        vmem((4, 64, 128), BF16), vmem((4, 4, 64, 128), BF16),
        vmem((4, 16, 128), BF16), vmem((4, 4, 16, 128), BF16),
        dma((4, 2)), dma((4, 2)), dma((4, 2)), dma((4, 4)), dma((4, 4)), dma((4, 4)), dma((4, 4)),
        vmem((3, 2, 48, 128), BF16), vmem((3, 2, 192, 128), BF16),
        vmem((3, 2, 48, 128), BF16), vmem((3, 2, 192, 128), BF16), vmem((3, 4, 48, 128), BF16),
        dma((3, 8)), dma((3, 8)),
        vmem((16, 96, 1024), BF16), dma((6,)),
        vmem((16, 96, 128), BF16), vmem((16, 96, 128), BF16), dma((2,)),
        vmem((1024, 128), F32), vmem((16, 64, 128), BF16), vmem((16, 64, 128), BF16), dma((2,)),
        vmem((64, 128), F32), vmem((16, 8, 128), F32), vmem((16, 8, 128), F32), dma((2,)),
        vmem((128, 1152), F32), vmem((2, 16, 80, 128), BF16), vmem((2, 16, 80, 128), BF16), dma((2, 2)),
        vmem((2, 80, 128), BF16), vmem((2, 16, 80, 128), BF16), dma((2, 2)),
        vmem((2, 80, 128), BF16), vmem((2, 16, 80, 128), BF16), dma((2, 2)),
    ]


def per_device(tokens, gout, deconv_weight, deconv_bias, conv_kernels, conv_biases):
    flat = tokens.reshape(48, 2, 1024).transpose(1, 0, 2).reshape(96, 1024)
    here = pl.BlockSpec(memory_space=pltpu.VMEM)
    tok_grad, weight_grad, kernel_grads, biases = pl.pallas_call(
        kernel,
        out_shape=(
            jax.ShapeDtypeStruct((96, 1024), BF16),
            jax.ShapeDtypeStruct((4, 2048), F32),
            jax.ShapeDtypeStruct((2, 1152, 128), F32),
            jax.ShapeDtypeStruct((16, 128), F32),
        ),
        in_specs=[here] * 6,
        out_specs=(here,) * 4,
        scratch_shapes=scratch(),
        compiler_params=pltpu.CompilerParams(
            collective_id=0, has_side_effects=True, vmem_limit_bytes=56 * 1024 * 1024
        ),
        name="triplane",
    )(
        flat, gout.reshape(TOTAL, 128), deconv_weight, deconv_bias.reshape(1, 128),
        conv_kernels, conv_biases.reshape(2, 1, 128),
    )
    tok_out = tok_grad.reshape(2, 48, 1024).transpose(1, 0, 2).reshape(tokens.shape)
    return (
        tok_out, weight_grad, biases[1],
        kernel_grads, jnp.stack([biases[0], biases[8]]),
    )


def solution(mesh):
    split = P("obj", None, "plane", "tile", None)
    return jax.shard_map(
        per_device,
        mesh=mesh,
        in_specs=(split, split, P(), P(), P(), P()),
        out_specs=(split, P(("obj", "plane", "tile"), None), P(), P(), P()),
        check_vma=False,
    )
```

```python
import jax
import jax.numpy as jnp
from jax import lax
from jax.experimental import pallas as pl
from jax.experimental.pallas import tpu as pltpu
from jax.sharding import PartitionSpec as P

MESH = pl.DeviceIdType.MESH
F32 = jnp.float32
BF16 = jnp.bfloat16
IMAGES = 6
ROWS = 32
COLS = 8
CELLS = ROWS * COLS
TOTAL = IMAGES * CELLS
PADDED = (ROWS + 2) * COLS
HALF = 3 * CELLS

HALO = (
    (-1, 0, ("row", 0), ("row", 1)),
    (1, 0, ("row", 1), ("row", 0)),
    (0, -1, ("col", 0), ("col", 1)),
    (0, 1, ("col", 1), ("col", 0)),
    (-1, -1, ("row", 0), ("corner", 3)),
    (-1, 1, ("row", 0), ("corner", 2)),
    (1, -1, ("row", 1), ("corner", 1)),
    (1, 1, ("row", 1), ("corner", 0)),
)


def both(first, second):
    return jnp.logical_and(first, second)


def kernel(
    x_ref, g_ref, w_ref, db_ref, k_ref, cb_ref,
    dtok_ref, dw_ref, dk_ref, bias_ref,
    hid, pre0, pre1, act0, act1, grad, nat, dzed, kcat, col,
    centre, leftpad, rightpad, rowpart, colpart, rowband, colband,
    rowhalf, colzero,
    zs, zr, m1s, m1r, m2s, m2r, m3s, m3r, m4s, m4r,
    zsem, m1sem, m2sem, m3ss, m3rs, m4ss, m4rs,
    hsrow, hscol, hrrow, hrcol, hrcor, hss, hrs,
    xg, xsem, tg, gg, tsem, dwk, dws, dwr, dwsem, fin, fins, finr, finsem,
    dkf, dka, dks, dkr, dksem, dkbs, dkbr, dkbsem, dkcs, dkcr, dkcsem,
):
    obj, y, t = lax.axis_index("obj"), lax.axis_index("plane"), lax.axis_index("tile")
    x, z = t // 4, lax.rem(t, 4)
    mine = obj * 4 + y

    def group_a(d):
        other = lax.rem(mine + d, 16)
        return other, {"obj": other // 4, "plane": lax.rem(other, 4)}

    def group_b(d):
        other = lax.rem(t + d, 16)
        return other, {"tile": other}

    def send(src, dst, send_sem, recv_sem, where):
        copy = pltpu.make_async_remote_copy(
            src_ref=src, dst_ref=dst, send_sem=send_sem, recv_sem=recv_sem,
            device_id=where, device_id_type=MESH,
        )
        copy.start()

    def finish(ref, sem):
        pltpu.make_async_copy(ref, ref, sem).wait()

    hrrow[...] = jnp.zeros_like(hrrow)
    hrcol[...] = jnp.zeros_like(hrcol)
    hrcor[...] = jnp.zeros_like(hrcor)
    barrier = pltpu.get_barrier_semaphore()

    def greet(where):
        pl.semaphore_signal(barrier, inc=1, device_id=where, device_id_type=MESH)

    for d in range(1, 16):
        greet(group_a(d)[1])
        greet(group_b(d)[1])
    for dy in range(1, 4):
        for dx in range(1, 4):
            greet({"plane": lax.rem(y + dy, 4), "tile": lax.rem(x + dx, 4) * 4 + z})

    def inside(dy, dt):
        row_ok = both(y + dy >= 0, y + dy <= 3)
        return both(row_ok, both(t + dt >= 0, t + dt <= 15))

    diagonals = 0
    for dy, dt in ((-1, -1), (-1, 1), (1, -1), (1, 1)):
        ok = inside(dy, dt)

        @pl.when(ok)
        def _(dy=dy, dt=dt):
            greet({"plane": y + dy, "tile": t + dt})

        diagonals = diagonals + ok.astype(jnp.int32)

    for part in range(4):
        products = jnp.dot(
            x_ref[...], w_ref[:, part * 512:(part + 1) * 512], preferred_element_type=F32
        )
        for j in range(2):
            for b in range(4):
                hid[pl.ds(part * 8 + 4 * j + b, 48, stride=32), :] = (
                    products[j * 48:(j + 1) * 48, b * 128:(b + 1) * 128] + db_ref[...]
                )
    for l in range(2):
        for tap in range(9):
            kcat[l, :, tap * 128:(tap + 1) * 128] = k_ref[l, tap * 128:(tap + 1) * 128, :]
    xg[mine] = x_ref[...]
    grad[...] = g_ref[...].astype(F32)

    pl.semaphore_wait(barrier, 39 + diagonals)

    sources = {"row": hsrow, "col": hscol}
    targets = {"row": hrrow, "col": hrcol, "corner": hrcor}

    def halo_start(stage, o, ref):
        h = 2 * stage + o
        for side, at in ((0, 0), (1, CELLS - COLS)):
            edge = [ref[i * CELLS + at:i * CELLS + at + COLS, :] for i in range(3 * o, 3 * o + 3)]
            hsrow[h, side] = jnp.concatenate(edge + [jnp.zeros((8, 128), F32)], axis=0).astype(BF16)
        for side, at in ((0, 0), (1, COLS - 1)):
            hscol[h, side] = ref[pl.ds(o * HALF + at, 3 * ROWS, stride=COLS), :].astype(BF16)
        for n, (dy, dt, src, dst) in enumerate(HALO):

            @pl.when(inside(dy, dt))
            def _(n=n, dy=dy, dt=dt, src=src, dst=dst):
                send(
                    sources[src[0]].at[h, src[1]], targets[dst[0]].at[h, dst[1]],
                    hss.at[h, n], hrs.at[h, n], {"plane": y + dy, "tile": t + dt},
                )

    def halo_finish(stage, o, ref):
        h = 2 * stage + o
        for n, (dy, dt, src, dst) in enumerate(HALO):

            @pl.when(inside(-dy, -dt))
            def _(n=n, dst=dst):
                finish(targets[dst[0]].at[h, dst[1]], hrs.at[h, n])

            @pl.when(inside(dy, dt))
            def _(n=n, src=src):
                finish(sources[src[0]].at[h, src[1]], hss.at[h, n])

        top, bottom = hrrow[h, 0].astype(F32), hrrow[h, 1].astype(F32)
        left, right = hrcol[h, 0].astype(F32), hrcol[h, 1].astype(F32)
        corners = [hrcor[h, c].astype(F32) for c in range(4)]
        last = PADDED - COLS
        for p in range(3):
            i = 3 * o + p
            base = i * PADDED
            centre[base:base + COLS, :] = top[p * COLS:(p + 1) * COLS]
            centre[base + COLS:base + COLS + CELLS, :] = ref[i * CELLS:(i + 1) * CELLS, :]
            centre[base + last:base + PADDED, :] = bottom[p * COLS:(p + 1) * COLS]
            leftpad[pl.ds(base + COLS, ROWS, stride=COLS), :] = left[p * ROWS:(p + 1) * ROWS]
            rightpad[pl.ds(base + 2 * COLS - 1, ROWS, stride=COLS), :] = right[p * ROWS:(p + 1) * ROWS]
            first, final = p * COLS, (p + 1) * COLS - 1
            leftpad[base:base + 1, :] = corners[0][final:final + 1]
            leftpad[base + last:base + last + 1, :] = corners[2][final:final + 1]
            rightpad[base + COLS - 1:base + COLS, :] = corners[1][first:first + 1]
            rightpad[base + PADDED - 1:base + PADDED, :] = corners[3][first:first + 1]

    def shifted(i, flipped):
        base = pl.multiple_of(i * PADDED, 8)
        middle = centre[pl.ds(base, PADDED), :]
        place = lax.rem(lax.broadcasted_iota(jnp.int32, (PADDED, 128), 0), COLS)
        before = jnp.where(place == 0, leftpad[pl.ds(base, PADDED), :], pltpu.roll(middle, 1, 0))
        after = jnp.where(
            place == COLS - 1, rightpad[pl.ds(base, PADDED), :], pltpu.roll(middle, PADDED - 1, 0)
        )
        for tx, padded in enumerate((before, middle, after)):
            for ty in range(3):
                tap = (2 - ty) * 3 + (2 - tx) if flipped else ty * 3 + tx
                col[i, :, tap * 128:(tap + 1) * 128] = padded[ty * COLS:ty * COLS + CELLS].astype(BF16)

    same = x == y

    def pool_first(ph, o, ref):
        q = 2 * ph + o
        rows = ref[pl.ds(o * HALF, 3 * ROWS, stride=COLS), :]
        for v in range(1, COLS):
            rows = rows + ref[pl.ds(o * HALF + v, 3 * ROWS, stride=COLS), :]
        rowpart[o * 96:o * 96 + 96, :] = rows
        for i in range(3 * o, 3 * o + 3):
            colpart[i * COLS:(i + 1) * COLS, :] = jnp.sum(
                ref[i * CELLS:(i + 1) * CELLS, :].reshape(ROWS, COLS, 128), axis=0
            )
        common = jnp.concatenate([rows[0:64], colpart[24 * o:24 * o + 8, :]], axis=0)
        for d in range(1, 4):
            zd = lax.rem(z + d, 4)
            chunk = rowpart[pl.ds(pl.multiple_of(96 * o + 64 + 8 * zd, 8), 8), :]
            zs[q, d - 1] = jnp.concatenate([common, chunk], axis=0).astype(BF16)
            send(zs.at[q, d - 1], zr.at[q, d - 1], zsem.at[q, 0], zsem.at[q, 1], {"tile": x * 4 + zd})
        m2s[q] = colpart[24 * o + 8:24 * o + 24, :].astype(BF16)
        for d in range(1, 4):
            send(m2s.at[q], m2r.at[q, d - 1], m2sem.at[q, 0], m2sem.at[q, 1], {"plane": lax.rem(y + d, 4)})

    def pool_second(ph, o):
        q = 2 * ph + o
        finish(zr.at[q], zsem.at[q, 1])
        half = rowpart[o * 96:o * 96 + 64, :]
        two = rowpart[pl.ds(pl.multiple_of(96 * o + 64 + 8 * z, 8), 8), :]
        colzero[pl.ds(pl.multiple_of(32 * o + 8 * z, 8), 8), :] = colpart[24 * o:24 * o + 8, :]
        for d in range(1, 4):
            got = zr[q, d - 1].astype(F32)
            half = half + got[:64]
            two = two + got[72:80]
            source = lax.rem(z + 4 - d, 4)
            colzero[pl.ds(pl.multiple_of(32 * o + 8 * source, 8), 8), :] = got[64:72]
        rowhalf[o * 64:o * 64 + 64, :] = half
        m1s[q] = half.astype(BF16)
        m3s[q] = colzero[32 * o:32 * o + 32, :].astype(BF16)
        m4s[q] = jnp.concatenate([two, jnp.zeros((8, 128), F32)], axis=0).astype(BF16)
        for k in range(4):

            @pl.when(jnp.logical_not(both(same, x == k)))
            def _(k=k):
                send(m3s.at[q], m3r.at[q, y], m3ss.at[q, k], m3rs.at[q, y], {"plane": x, "tile": k * 4 + z})
                send(m4s.at[q], m4r.at[q, x], m4ss.at[q, k], m4rs.at[q, x], {"plane": k, "tile": y * 4 + z})

        for d in range(1, 4):
            send(m1s.at[q], m1r.at[q, d - 1], m1sem.at[q, 0], m1sem.at[q, 1], {"tile": lax.rem(x + d, 4) * 4 + z})

        @pl.when(same)
        def _():
            m3r[q, y] = m3s[q]
            m4r[q, x] = m4s[q]

    def pool_third(ph, o):
        q = 2 * ph + o
        finish(m2r.at[q], m2sem.at[q, 1])
        finish(m1r.at[q], m1sem.at[q, 1])
        for k in range(4):

            @pl.when(jnp.logical_not(both(same, x == k)))
            def _(k=k):
                finish(m3r.at[q, k], m3rs.at[q, k])
                finish(m4r.at[q, k], m4rs.at[q, k])
                finish(m3s.at[q], m3ss.at[q, k])
                finish(m4s.at[q], m4ss.at[q, k])

        finish(zs.at[q], zsem.at[q, 0])
        finish(m1r.at[q], m1sem.at[q, 0])
        finish(m2r.at[q], m2sem.at[q, 0])
        half = rowhalf[o * 64:o * 64 + 64, :]
        one = colpart[24 * o + 8:24 * o + 24, :]
        for d in range(3):
            half = half + m1r[q, d].astype(F32)
            one = one + m2r[q, d].astype(F32)
        zero = m3r[q, 0].astype(F32)
        two = m4r[q, 0].astype(F32)
        for k in range(1, 4):
            zero = zero + m3r[q, k].astype(F32)
            two = two + m4r[q, k].astype(F32)
        share = 1.0 / 128.0
        rowband[96 * o:96 * o + 32, :] = half[32:64] * share
        rowband[96 * o + 32:96 * o + 64, :] = half[0:32] * share
        rowband[96 * o + 64:96 * o + 96, :] = zero * share
        colband[24 * o:24 * o + 8, :] = two[0:8] * share
        colband[24 * o + 8:24 * o + 16, :] = one[8:16] * share
        colband[24 * o + 16:24 * o + 24, :] = one[0:8] * share

    def add_bands(dst, o, *srcs):
        for i in range(3 * o, 3 * o + 3):
            rb = rowband[i * ROWS:(i + 1) * ROWS, :]
            for v in range(COLS):
                at = pl.ds(i * CELLS + v, ROWS, stride=COLS)
                value = rb + colband[i * COLS + v:i * COLS + v + 1, :]
                for src in srcs:
                    value = value + src[at, :]
                dst[at, :] = value

    def per_image(o, body):
        def step(n, carry):
            i = n + 3 * o
            body(i, pl.ds(pl.multiple_of(i * CELLS, CELLS), CELLS))
            return carry

        lax.fori_loop(0, 3, step, 0)

    def silu0(i, at):
        value = pre0[at, :]
        rounded = (value * jax.nn.sigmoid(value)).astype(BF16)
        act0[at, :] = rounded
        nat[at, :] = rounded.astype(F32)

    def forward(i, at):
        shifted(i, False)
        out = jnp.dot(col[i], k_ref[0], preferred_element_type=F32)
        hid[at, :] = hid[at, :] + out + cb_ref[0]

    def act_grad(layer):
        def body(i, at):
            shifted(i, True)
            dzed[at, :] = lax.dot_general(
                col[i], kcat[layer], (((1,), (1,)), ((), ())), preferred_element_type=F32
            )

        return body

    def pre_grad1(i, at):
        value = pre1[at, :]
        s = jax.nn.sigmoid(value)
        act1[at, :] = (value * s).astype(BF16)
        dzed[at, :] = dzed[at, :] * s * (1.0 + value * (1.0 - s))

    def pre_grad0(i, at):
        value = pre0[at, :]
        s = jax.nn.sigmoid(value)
        dzed[at, :] = dzed[at, :] * s * (1.0 + value * (1.0 - s))

    def rounded(i, at):
        nat[at, :] = grad[at, :].astype(BF16).astype(F32)

    def kernel_grad(act):
        dka[...] = jnp.zeros_like(dka)

        def body(i, at):
            dka[...] += lax.dot_general(
                act[at, :], col[i], (((0,), (0,)), ((), ())), preferred_element_type=F32
            )

        for o in range(2):
            per_image(o, body)

    def total(ref):
        return jnp.sum(jnp.sum(ref[...].reshape(TOTAL // 8, 8, 128), axis=0), axis=0, keepdims=True)

    def kernel_grad_start(layer, extra):
        extras = jnp.concatenate(extra + [jnp.zeros((8 - len(extra), 128), F32)], axis=0)
        for g in range(16):
            rows = [dka[8 * g:8 * g + 8, tap * 128:(tap + 1) * 128] for tap in range(9)]
            dks[layer, g] = jnp.concatenate(rows + [extras], axis=0).astype(BF16)
        for d in range(1, 16):
            other, where = group_a(d)
            send(dks.at[layer, other], dkr.at[layer, mine], dksem.at[layer, 0], dksem.at[layer, 1], where)
        dkr[layer, mine] = dks[layer, mine]

    def fifteen(ref, sem):
        finish(ref.at[pl.ds(0, 15)], sem)

    def sum16(ref, layer):
        def step(n, acc):
            return acc + ref[layer, n].astype(F32)

        return lax.fori_loop(1, 16, step, ref[layer, 0].astype(F32))

    def kernel_grad_second(layer):
        fifteen(dkr.at[layer], dksem.at[layer, 1])
        fifteen(dks.at[layer], dksem.at[layer, 0])
        dkbs[layer] = sum16(dkr, layer).astype(BF16)
        for d in range(1, 16):
            send(dkbs.at[layer], dkbr.at[layer, t], dkbsem.at[layer, 0], dkbsem.at[layer, 1], group_b(d)[1])
        dkbr[layer, t] = dkbs[layer]

    def kernel_grad_third(layer):
        fifteen(dkbr.at[layer], dkbsem.at[layer, 1])
        fifteen(dkbr.at[layer], dkbsem.at[layer, 0])
        dkcs[layer] = sum16(dkbr, layer).astype(BF16)
        for d in range(1, 16):
            send(dkcs.at[layer], dkcr.at[layer, mine], dkcsem.at[layer, 0], dkcsem.at[layer, 1], group_a(d)[1])
        dkcr[layer, mine] = dkcs[layer]

    def kernel_grad_finish(layer):
        fifteen(dkcr.at[layer], dkcsem.at[layer, 1])
        fifteen(dkcr.at[layer], dkcsem.at[layer, 0])
        for g in range(16):
            got = dkcr[layer, g].astype(F32)
            dkf[g] = got[:72]
            if g == 0:
                bias_ref[layer * 8:layer * 8 + 8, :] = got[72:80]
        for tap in range(9):
            dk_ref[layer, tap * 128:(tap + 1) * 128, :] = (
                dkf[:, 8 * tap:8 * tap + 8, :].reshape(128, 128).astype(BF16)
            )

    objects = range(2)
    for o in objects:
        pool_first(0, o, hid)
    for o in objects:
        pool_second(0, o)
    partner = {"obj": lax.rem(obj + 2, 4)}
    send(xg.at[mine], xg.at[mine], xsem.at[0], xsem.at[1], partner)
    for o in objects:
        pool_third(0, o)
        add_bands(pre0, o, hid)
        per_image(o, silu0)
        halo_start(1, o, nat)
    for o in objects:
        halo_start(0, o, grad)
    for o in objects:
        halo_finish(1, o, nat)
        per_image(o, forward)
        pool_first(1, o, hid)
    finish(xg.at[mine], xsem.at[1])
    theirs = lax.rem(obj + 2, 4) * 4 + y

    def to_planes(slot):
        for d in range(1, 4):
            send(xg.at[slot], xg.at[slot], xsem.at[2], xsem.at[3], {"plane": lax.rem(y + d, 4)})

    to_planes(mine)
    halo_finish(0, 0, grad)
    per_image(0, act_grad(1))
    pool_second(1, 0)
    pool_second(1, 1)
    halo_finish(0, 1, grad)
    per_image(1, act_grad(1))
    for o in objects:
        pool_third(1, o)
        add_bands(pre1, o, hid)
        per_image(o, pre_grad1)
        pool_first(2, o, dzed)
    to_planes(theirs)
    kernel_grad(act1)
    kernel_grad_start(1, [total(grad)])
    for o in objects:
        pool_second(2, o)
    for o in objects:
        pool_third(2, o)
        add_bands(grad, o, grad, dzed)
        per_image(o, rounded)
        halo_start(2, o, nat)
    finish(xg.at[pl.ds(0, 6)], xsem.at[3])
    finish(xg.at[pl.ds(0, 6)], xsem.at[2])
    sum_grad = total(grad)
    for o in objects:
        halo_finish(2, o, nat)
        per_image(o, act_grad(0))
        per_image(o, pre_grad0)
        pool_first(3, o, dzed)
    sibling = {"obj": obj + 1 - 2 * lax.rem(obj, 2)}
    core = lax.rem(obj, 2)
    for half in range(2):
        held = xg.at[pl.ds(pl.multiple_of((core + 2 * half) * 4, 4), 4)]
        send(held, held, xsem.at[4], xsem.at[5], sibling)
    kernel_grad(act0)
    kernel_grad_start(0, [sum_grad, sum_grad + 3.0 * total(dzed)])
    for o in objects:
        pool_second(3, o)
    kernel_grad_second(1)
    for o in objects:
        pool_third(3, o)
        add_bands(grad, o, grad, dzed)
    for a in range(4):
        for b in range(4):
            for j in range(2):
                tg[a * 4 + b, j * 48:(j + 1) * 48, :] = grad[
                    pl.ds(a * 8 + 4 * j + b, 48, stride=32), :
                ].astype(BF16)
    for d in range(1, 16):
        other, where = group_a(d)
        send(tg.at[other], gg.at[mine], tsem.at[0], tsem.at[1], where)
    gg[mine] = tg[mine]
    kernel_grad_second(0)
    kernel_grad_third(1)
    taps = jnp.concatenate([tg[n] for n in range(16)], axis=1)
    for part in range(4):
        dtok_ref[:, part * 256:(part + 1) * 256] = lax.dot_general(
            taps, w_ref[part * 256:(part + 1) * 256, :], (((1,), (1,)), ((), ())),
            preferred_element_type=F32,
        ).astype(BF16)
    finish(xg.at[mine], xsem.at[0])
    finish(xg.at[pl.ds(0, 8)], xsem.at[5])
    finish(xg.at[pl.ds(0, 8)], xsem.at[4])
    fifteen(gg, tsem.at[1])
    fifteen(tg, tsem.at[0])
    taken = gg[...].reshape(1536, 128)
    for part in range(4):
        product = lax.dot_general(
            taken, xg[:, :, part * 256:(part + 1) * 256].reshape(1536, 256),
            (((0,), (0,)), ((), ())), preferred_element_type=F32,
        )
        dwk[part * 256:(part + 1) * 256, :] = product.T
    for other in range(16):
        dws[other] = jnp.concatenate(
            [dwk[pl.ds(other * 4 + r, 16, stride=64), :] for r in range(4)], axis=0
        ).astype(BF16)
    for d in range(1, 16):
        other, where = group_b(d)
        send(dws.at[other], dwr.at[t], dwsem.at[0], dwsem.at[1], where)
    dwr[t] = dws[t]
    kernel_grad_third(0)
    kernel_grad_finish(1)
    fifteen(dwr, dwsem.at[1])
    fifteen(dws, dwsem.at[0])
    fin[...] = lax.fori_loop(
        1, 16, lambda n, acc: acc + dwr[n].astype(F32), dwr[0].astype(F32)
    )
    for other in range(16):
        fins[other, 0:4, :] = fin[pl.ds(other, 4, stride=16), :]
        fins[other, 4:8, :] = jnp.zeros((4, 128), F32)
    for d in range(1, 16):
        other, where = group_a(d)
        send(fins.at[other], finr.at[mine], finsem.at[0], finsem.at[1], where)
    finr[mine] = fins[mine]
    kernel_grad_finish(0)
    fifteen(finr, finsem.at[1])
    fifteen(fins, finsem.at[0])
    for n in range(16):
        dw_ref[:, n * 128:(n + 1) * 128] = finr[n, 0:4, :]


def scratch():
    dma = pltpu.SemaphoreType.DMA
    vmem = pltpu.VMEM
    full = (TOTAL, 128)
    padded = (IMAGES * PADDED, 128)
    return [
        vmem(full, F32), vmem(full, F32), vmem(full, F32), vmem(full, BF16), vmem(full, BF16),
        vmem(full, F32), vmem(full, F32), vmem(full, F32), vmem((2, 128, 1152), BF16), vmem((IMAGES, CELLS, 1152), BF16),
        vmem(padded, F32), vmem(padded, F32), vmem(padded, F32),
        vmem((192, 128), F32), vmem((48, 128), F32), vmem((192, 128), F32), vmem((48, 128), F32),
        vmem((128, 128), F32), vmem((64, 128), F32),
        vmem((8, 3, 80, 128), BF16), vmem((8, 3, 80, 128), BF16),
        vmem((8, 64, 128), BF16), vmem((8, 3, 64, 128), BF16),
        vmem((8, 16, 128), BF16), vmem((8, 3, 16, 128), BF16),
        vmem((8, 32, 128), BF16), vmem((8, 4, 32, 128), BF16),
        vmem((8, 16, 128), BF16), vmem((8, 4, 16, 128), BF16),
        dma((8, 2)), dma((8, 2)), dma((8, 2)), dma((8, 4)), dma((8, 4)), dma((8, 4)), dma((8, 4)),
        vmem((6, 2, 32, 128), BF16), vmem((6, 2, 96, 128), BF16),
        vmem((6, 2, 32, 128), BF16), vmem((6, 2, 96, 128), BF16), vmem((6, 4, 32, 128), BF16),
        dma((6, 8)), dma((6, 8)),
        vmem((16, 96, 1024), BF16), dma((6,)),
        vmem((16, 96, 128), BF16), vmem((16, 96, 128), BF16), dma((2,)),
        vmem((1024, 128), F32), vmem((16, 64, 128), BF16), vmem((16, 64, 128), BF16), dma((2,)),
        vmem((64, 128), F32), vmem((16, 8, 128), F32), vmem((16, 8, 128), F32), dma((2,)),
        vmem((16, 72, 128), F32), vmem((128, 1152), F32), vmem((2, 16, 80, 128), BF16), vmem((2, 16, 80, 128), BF16), dma((2, 2)),
        vmem((2, 80, 128), BF16), vmem((2, 16, 80, 128), BF16), dma((2, 2)),
        vmem((2, 80, 128), BF16), vmem((2, 16, 80, 128), BF16), dma((2, 2)),
    ]


def per_device(tokens, gout, deconv_weight, deconv_bias, conv_kernels, conv_biases):
    flat = tokens.reshape(48, 2, 1024).transpose(1, 0, 2).reshape(96, 1024)
    here = pl.BlockSpec(memory_space=pltpu.VMEM)
    tok_grad, weight_grad, kernel_grads, biases = pl.pallas_call(
        kernel,
        out_shape=(
            jax.ShapeDtypeStruct((96, 1024), BF16),
            jax.ShapeDtypeStruct((4, 2048), F32),
            jax.ShapeDtypeStruct((2, 1152, 128), BF16),
            jax.ShapeDtypeStruct((16, 128), F32),
        ),
        in_specs=[here] * 6,
        out_specs=(here,) * 4,
        scratch_shapes=scratch(),
        compiler_params=pltpu.CompilerParams(
            collective_id=0, has_side_effects=True, vmem_limit_bytes=56 * 1024 * 1024
        ),
        name="triplane",
    )(
        flat, gout.reshape(TOTAL, 128), deconv_weight, deconv_bias.reshape(1, 128),
        conv_kernels, conv_biases.reshape(2, 1, 128),
    )
    tok_out = tok_grad.reshape(2, 48, 1024).transpose(1, 0, 2).reshape(tokens.shape)
    return (
        tok_out, weight_grad, biases[1],
        kernel_grads.astype(F32), jnp.stack([biases[0], biases[8]]),
    )


def solution(mesh):
    split = P("obj", None, "plane", "tile", None)
    return jax.shard_map(
        per_device,
        mesh=mesh,
        in_specs=(split, split, P(), P(), P(), P()),
        out_specs=(split, P(("obj", "plane", "tile"), None), P(), P(), P()),
        check_vma=False,
    )
```

```python
import jax
import jax.numpy as jnp
from jax import lax
from jax.experimental import pallas as pl
from jax.experimental.pallas import tpu as pltpu
from jax.sharding import PartitionSpec as P

MESH = pl.DeviceIdType.MESH
F32 = jnp.float32
BF16 = jnp.bfloat16
IMAGES = 6
ROWS = 32
COLS = 8
CELLS = ROWS * COLS
TOTAL = IMAGES * CELLS
PADDED = (ROWS + 2) * COLS
HALF = 3 * CELLS

HALO = (
    (-1, 0, ("row", 0), ("row", 1)),
    (1, 0, ("row", 1), ("row", 0)),
    (0, -1, ("col", 0), ("col", 1)),
    (0, 1, ("col", 1), ("col", 0)),
    (-1, -1, ("row", 0), ("corner", 3)),
    (-1, 1, ("row", 0), ("corner", 2)),
    (1, -1, ("row", 1), ("corner", 1)),
    (1, 1, ("row", 1), ("corner", 0)),
)


def both(first, second):
    return jnp.logical_and(first, second)


def kernel(
    x_ref, g_ref, w_hbm, db_ref, k_ref, cb_ref,
    dtok_ref, dw_ref, dk_ref, bias_ref,
    w_ref, wsem, hid, pre0, pre1, act0, act1, grad, nat, dzed, kcat, col,
    centre, leftpad, rightpad, rowpart, colpart, rowband, colband,
    rowhalf, colzero,
    zs, zr, m1s, m1r, m2s, m2r, m3s, m3r, m4s, m4r,
    zsem, m1sem, m2sem, m3ss, m3rs, m4ss, m4rs,
    hsrow, hscol, hrrow, hrcol, hrcor, hss, hrs,
    xg, xsem, tg, gg, tsem, dwk, dws, dwr, dwsem, fin, fins, finr, finsem,
    dkf, dkacc, dka, dks, dkr, dksem, dkbs, dkbr, dkbsem, dkms, dkmr, dkmsem, dkcs, dkcr, dkcsem,
):
    obj, y, t = lax.axis_index("obj"), lax.axis_index("plane"), lax.axis_index("tile")
    x, z = t // 4, lax.rem(t, 4)
    mine = obj * 4 + y

    def group_a(d):
        other = lax.rem(mine + d, 16)
        return other, {"obj": other // 4, "plane": lax.rem(other, 4)}

    def group_b(d):
        other = lax.rem(t + d, 16)
        return other, {"tile": other}

    def send(src, dst, send_sem, recv_sem, where):
        copy = pltpu.make_async_remote_copy(
            src_ref=src, dst_ref=dst, send_sem=send_sem, recv_sem=recv_sem,
            device_id=where, device_id_type=MESH,
        )
        copy.start()

    def finish(ref, sem):
        pltpu.make_async_copy(ref, ref, sem).wait()

    def weight_part(part):
        at = slice(part * 512, (part + 1) * 512)
        return pltpu.make_async_copy(w_hbm.at[:, at], w_ref.at[:, at], wsem.at[part])

    for part in range(4):
        weight_part(part).start()
    hrrow[...] = jnp.zeros_like(hrrow)
    hrcol[...] = jnp.zeros_like(hrcol)
    hrcor[...] = jnp.zeros_like(hrcor)
    barrier = pltpu.get_barrier_semaphore()

    def greet(where):
        pl.semaphore_signal(barrier, inc=1, device_id=where, device_id_type=MESH)

    for d in range(1, 16):
        greet(group_a(d)[1])
        greet(group_b(d)[1])
    for dy in range(1, 4):
        for dx in range(1, 4):
            greet({"plane": lax.rem(y + dy, 4), "tile": lax.rem(x + dx, 4) * 4 + z})

    def inside(dy, dt):
        row_ok = both(y + dy >= 0, y + dy <= 3)
        return both(row_ok, both(t + dt >= 0, t + dt <= 15))

    diagonals = 0
    for dy, dt in ((-1, -1), (-1, 1), (1, -1), (1, 1)):
        ok = inside(dy, dt)

        @pl.when(ok)
        def _(dy=dy, dt=dt):
            greet({"plane": y + dy, "tile": t + dt})

        diagonals = diagonals + ok.astype(jnp.int32)

    for l in range(2):
        for tap in range(9):
            kcat[l, :, tap * 128:(tap + 1) * 128] = k_ref[l, tap * 128:(tap + 1) * 128, :]
    xg[mine] = x_ref[...]
    grad[...] = g_ref[...].astype(F32)

    for part in range(4):
        weight_part(part).wait()
        products = jnp.dot(
            x_ref[...], w_ref[:, part * 512:(part + 1) * 512], preferred_element_type=F32
        )
        for j in range(2):
            for b in range(4):
                hid[pl.ds(part * 8 + 4 * j + b, 48, stride=32), :] = (
                    products[j * 48:(j + 1) * 48, b * 128:(b + 1) * 128] + db_ref[...]
                )
    pl.semaphore_wait(barrier, 39 + diagonals)

    sources = {"row": hsrow, "col": hscol}
    targets = {"row": hrrow, "col": hrcol, "corner": hrcor}

    def halo_start(stage, o, ref):
        h = 2 * stage + o
        for side, at in ((0, 0), (1, CELLS - COLS)):
            edge = [ref[i * CELLS + at:i * CELLS + at + COLS, :] for i in range(3 * o, 3 * o + 3)]
            hsrow[h, side] = jnp.concatenate(edge + [jnp.zeros((8, 128), F32)], axis=0).astype(BF16)
        for side, at in ((0, 0), (1, COLS - 1)):
            hscol[h, side] = ref[pl.ds(o * HALF + at, 3 * ROWS, stride=COLS), :].astype(BF16)
        for n, (dy, dt, src, dst) in enumerate(HALO):

            @pl.when(inside(dy, dt))
            def _(n=n, dy=dy, dt=dt, src=src, dst=dst):
                send(
                    sources[src[0]].at[h, src[1]], targets[dst[0]].at[h, dst[1]],
                    hss.at[h, n], hrs.at[h, n], {"plane": y + dy, "tile": t + dt},
                )

    def halo_finish(stage, o, ref):
        h = 2 * stage + o
        for n, (dy, dt, src, dst) in enumerate(HALO):

            @pl.when(inside(-dy, -dt))
            def _(n=n, dst=dst):
                finish(targets[dst[0]].at[h, dst[1]], hrs.at[h, n])

            @pl.when(inside(dy, dt))
            def _(n=n, src=src):
                finish(sources[src[0]].at[h, src[1]], hss.at[h, n])

        top, bottom = hrrow[h, 0].astype(F32), hrrow[h, 1].astype(F32)
        left, right = hrcol[h, 0].astype(F32), hrcol[h, 1].astype(F32)
        corners = [hrcor[h, c].astype(F32) for c in range(4)]
        last = PADDED - COLS
        for p in range(3):
            i = 3 * o + p
            base = i * PADDED
            centre[base:base + COLS, :] = top[p * COLS:(p + 1) * COLS]
            centre[base + COLS:base + COLS + CELLS, :] = ref[i * CELLS:(i + 1) * CELLS, :]
            centre[base + last:base + PADDED, :] = bottom[p * COLS:(p + 1) * COLS]
            leftpad[pl.ds(base + COLS, ROWS, stride=COLS), :] = left[p * ROWS:(p + 1) * ROWS]
            rightpad[pl.ds(base + 2 * COLS - 1, ROWS, stride=COLS), :] = right[p * ROWS:(p + 1) * ROWS]
            first, final = p * COLS, (p + 1) * COLS - 1
            leftpad[base:base + 1, :] = corners[0][final:final + 1]
            leftpad[base + last:base + last + 1, :] = corners[2][final:final + 1]
            rightpad[base + COLS - 1:base + COLS, :] = corners[1][first:first + 1]
            rightpad[base + PADDED - 1:base + PADDED, :] = corners[3][first:first + 1]

    def shifted(i, flipped):
        base = pl.multiple_of(i * PADDED, 8)
        middle = centre[pl.ds(base, PADDED), :]
        place = lax.rem(lax.broadcasted_iota(jnp.int32, (PADDED, 128), 0), COLS)
        before = jnp.where(place == 0, leftpad[pl.ds(base, PADDED), :], pltpu.roll(middle, 1, 0))
        after = jnp.where(
            place == COLS - 1, rightpad[pl.ds(base, PADDED), :], pltpu.roll(middle, PADDED - 1, 0)
        )
        for tx, padded in enumerate((before, middle, after)):
            for ty in range(3):
                tap = (2 - ty) * 3 + (2 - tx) if flipped else ty * 3 + tx
                col[i, :, tap * 128:(tap + 1) * 128] = padded[ty * COLS:ty * COLS + CELLS].astype(BF16)

    same = x == y

    def pool_first(ph, o, ref):
        q = 2 * ph + o
        rows = ref[pl.ds(o * HALF, 3 * ROWS, stride=COLS), :]
        for v in range(1, COLS):
            rows = rows + ref[pl.ds(o * HALF + v, 3 * ROWS, stride=COLS), :]
        rowpart[o * 96:o * 96 + 96, :] = rows
        for i in range(3 * o, 3 * o + 3):
            colpart[i * COLS:(i + 1) * COLS, :] = jnp.sum(
                ref[i * CELLS:(i + 1) * CELLS, :].reshape(ROWS, COLS, 128), axis=0
            )
        common = jnp.concatenate([rows[0:64], colpart[24 * o:24 * o + 8, :]], axis=0)
        for d in range(1, 4):
            zd = lax.rem(z + d, 4)
            chunk = rowpart[pl.ds(pl.multiple_of(96 * o + 64 + 8 * zd, 8), 8), :]
            zs[q, d - 1] = jnp.concatenate([common, chunk], axis=0).astype(BF16)
            send(zs.at[q, d - 1], zr.at[q, d - 1], zsem.at[q, 0], zsem.at[q, 1], {"tile": x * 4 + zd})
        m2s[q] = colpart[24 * o + 8:24 * o + 24, :].astype(BF16)
        for d in range(1, 4):
            send(m2s.at[q], m2r.at[q, d - 1], m2sem.at[q, 0], m2sem.at[q, 1], {"plane": lax.rem(y + d, 4)})

    def pool_second(ph, o):
        q = 2 * ph + o
        finish(zr.at[q], zsem.at[q, 1])
        half = rowpart[o * 96:o * 96 + 64, :]
        two = rowpart[pl.ds(pl.multiple_of(96 * o + 64 + 8 * z, 8), 8), :]
        colzero[pl.ds(pl.multiple_of(32 * o + 8 * z, 8), 8), :] = colpart[24 * o:24 * o + 8, :]
        for d in range(1, 4):
            got = zr[q, d - 1].astype(F32)
            half = half + got[:64]
            two = two + got[72:80]
            source = lax.rem(z + 4 - d, 4)
            colzero[pl.ds(pl.multiple_of(32 * o + 8 * source, 8), 8), :] = got[64:72]
        rowhalf[o * 64:o * 64 + 64, :] = half
        m1s[q] = half.astype(BF16)
        m3s[q] = colzero[32 * o:32 * o + 32, :].astype(BF16)
        m4s[q] = jnp.concatenate([two, jnp.zeros((8, 128), F32)], axis=0).astype(BF16)
        for k in range(4):

            @pl.when(jnp.logical_not(both(same, x == k)))
            def _(k=k):
                send(m3s.at[q], m3r.at[q, y], m3ss.at[q, k], m3rs.at[q, y], {"plane": x, "tile": k * 4 + z})
                send(m4s.at[q], m4r.at[q, x], m4ss.at[q, k], m4rs.at[q, x], {"plane": k, "tile": y * 4 + z})

        for d in range(1, 4):
            send(m1s.at[q], m1r.at[q, d - 1], m1sem.at[q, 0], m1sem.at[q, 1], {"tile": lax.rem(x + d, 4) * 4 + z})

        @pl.when(same)
        def _():
            m3r[q, y] = m3s[q]
            m4r[q, x] = m4s[q]

    def pool_third(ph, o):
        q = 2 * ph + o
        finish(m2r.at[q], m2sem.at[q, 1])
        finish(m1r.at[q], m1sem.at[q, 1])
        for k in range(4):

            @pl.when(jnp.logical_not(both(same, x == k)))
            def _(k=k):
                finish(m3r.at[q, k], m3rs.at[q, k])
                finish(m4r.at[q, k], m4rs.at[q, k])
                finish(m3s.at[q], m3ss.at[q, k])
                finish(m4s.at[q], m4ss.at[q, k])

        finish(zs.at[q], zsem.at[q, 0])
        finish(m1r.at[q], m1sem.at[q, 0])
        finish(m2r.at[q], m2sem.at[q, 0])
        half = rowhalf[o * 64:o * 64 + 64, :]
        one = colpart[24 * o + 8:24 * o + 24, :]
        for d in range(3):
            half = half + m1r[q, d].astype(F32)
            one = one + m2r[q, d].astype(F32)
        zero = m3r[q, 0].astype(F32)
        two = m4r[q, 0].astype(F32)
        for k in range(1, 4):
            zero = zero + m3r[q, k].astype(F32)
            two = two + m4r[q, k].astype(F32)
        share = 1.0 / 128.0
        rowband[96 * o:96 * o + 32, :] = half[32:64] * share
        rowband[96 * o + 32:96 * o + 64, :] = half[0:32] * share
        rowband[96 * o + 64:96 * o + 96, :] = zero * share
        colband[24 * o:24 * o + 8, :] = two[0:8] * share
        colband[24 * o + 8:24 * o + 16, :] = one[8:16] * share
        colband[24 * o + 16:24 * o + 24, :] = one[0:8] * share

    def add_bands(dst, o, *srcs):
        for i in range(3 * o, 3 * o + 3):
            rb = rowband[i * ROWS:(i + 1) * ROWS, :]
            for v in range(COLS):
                at = pl.ds(i * CELLS + v, ROWS, stride=COLS)
                value = rb + colband[i * COLS + v:i * COLS + v + 1, :]
                for src in srcs:
                    value = value + src[at, :]
                dst[at, :] = value

    def per_image(o, body):
        def step(n, carry):
            i = n + 3 * o
            body(i, pl.ds(pl.multiple_of(i * CELLS, CELLS), CELLS))
            return carry

        lax.fori_loop(0, 3, step, 0)

    def silu0(i, at):
        value = pre0[at, :]
        rounded = (value * jax.nn.sigmoid(value)).astype(BF16)
        act0[at, :] = rounded
        nat[at, :] = rounded.astype(F32)

    def forward(i, at):
        shifted(i, False)
        out = jnp.dot(col[i], k_ref[0], preferred_element_type=F32)
        hid[at, :] = hid[at, :] + out + cb_ref[0]

    def act_grad(layer):
        def body(i, at):
            shifted(i, True)
            dzed[at, :] = lax.dot_general(
                col[i], kcat[layer], (((1,), (1,)), ((), ())), preferred_element_type=F32
            )

        return body

    def pre_grad1(i, at):
        value = pre1[at, :]
        s = jax.nn.sigmoid(value)
        act1[at, :] = (value * s).astype(BF16)
        dzed[at, :] = dzed[at, :] * s * (1.0 + value * (1.0 - s))

    def pre_grad0(i, at):
        value = pre0[at, :]
        s = jax.nn.sigmoid(value)
        dzed[at, :] = dzed[at, :] * s * (1.0 + value * (1.0 - s))

    def rounded(i, at):
        nat[at, :] = grad[at, :].astype(BF16).astype(F32)

    def kernel_grad(act):
        dka[...] = jnp.zeros_like(dka)

        def body(i, at):
            dka[...] += lax.dot_general(
                act[at, :], col[i], (((0,), (0,)), ((), ())), preferred_element_type=F32
            )

        for o in range(2):
            per_image(o, body)

    def total(ref):
        return jnp.sum(jnp.sum(ref[...].reshape(TOTAL // 8, 8, 128), axis=0), axis=0, keepdims=True)

    def kernel_grad_start(layer, extra):
        extras = jnp.concatenate(extra + [jnp.zeros((8 - len(extra), 128), F32)], axis=0)
        for g in range(16):
            rows = [dka[8 * g:8 * g + 8, tap * 128:(tap + 1) * 128] for tap in range(9)]
            dks[layer, g] = jnp.concatenate(rows + [extras], axis=0).astype(BF16)
        for d in range(1, 16):
            other, where = group_a(d)
            send(dks.at[layer, other], dkr.at[layer, mine], dksem.at[layer, 0], dksem.at[layer, 1], where)
        dkr[layer, mine] = dks[layer, mine]

    def fifteen(ref, sem):
        finish(ref.at[pl.ds(0, 15)], sem)

    def sum16(ref, layer):
        def step(n, acc):
            return acc + ref[layer, n].astype(F32)

        return lax.fori_loop(1, 16, step, ref[layer, 0].astype(F32))

    def kernel_grad_second(layer):
        fifteen(dkr.at[layer], dksem.at[layer, 1])
        fifteen(dks.at[layer], dksem.at[layer, 0])
        dkacc[0:80, :] = sum16(dkr, layer)
        dkacc[80:88, :] = jnp.zeros((8, 128), F32)
        for n in range(16):
            dkbs[layer, n] = dkacc[5 * n:5 * n + 8, :]
        for d in range(1, 16):
            other, where = group_b(d)
            send(dkbs.at[layer, other], dkbr.at[layer, t], dkbsem.at[layer, 0], dkbsem.at[layer, 1], where)
        dkbr[layer, t] = dkbs[layer, t]

    def kernel_grad_middle(layer):
        fifteen(dkbr.at[layer], dkbsem.at[layer, 1])
        fifteen(dkbr.at[layer], dkbsem.at[layer, 0])
        dkms[layer] = sum16(dkbr, layer)
        for d in range(1, 16):
            send(dkms.at[layer], dkmr.at[layer, t], dkmsem.at[layer, 0], dkmsem.at[layer, 1], group_b(d)[1])
        dkmr[layer, t] = dkms[layer]

    def kernel_grad_third(layer):
        fifteen(dkmr.at[layer], dkmsem.at[layer, 1])
        fifteen(dkmr.at[layer], dkmsem.at[layer, 0])
        for n in range(16):
            dkacc[5 * n:5 * n + 5, :] = dkmr[layer, n, 0:5, :]
        dkcs[layer] = dkacc[0:80, :].astype(BF16)
        for d in range(1, 16):
            send(dkcs.at[layer], dkcr.at[layer, mine], dkcsem.at[layer, 0], dkcsem.at[layer, 1], group_a(d)[1])
        dkcr[layer, mine] = dkcs[layer]

    def kernel_grad_finish(layer):
        fifteen(dkcr.at[layer], dkcsem.at[layer, 1])
        fifteen(dkcr.at[layer], dkcsem.at[layer, 0])
        for g in range(16):
            got = dkcr[layer, g].astype(F32)
            dkf[g] = got[:72]
            if g == 0:
                bias_ref[layer * 8:layer * 8 + 8, :] = got[72:80]
        for tap in range(9):
            dk_ref[layer, tap * 128:(tap + 1) * 128, :] = (
                dkf[:, 8 * tap:8 * tap + 8, :].reshape(128, 128).astype(BF16)
            )

    objects = range(2)
    theirs = lax.rem(obj + 2, 4) * 4 + y

    def to_planes(slot):
        for d in range(1, 4):
            send(xg.at[slot], xg.at[slot], xsem.at[2], xsem.at[3], {"plane": lax.rem(y + d, 4)})

    for o in objects:
        pool_first(0, o, hid)
    to_planes(mine)
    for o in objects:
        pool_second(0, o)
    partner = {"obj": lax.rem(obj + 2, 4)}
    send(xg.at[mine], xg.at[mine], xsem.at[0], xsem.at[1], partner)
    for o in objects:
        pool_third(0, o)
        add_bands(pre0, o, hid)
        per_image(o, silu0)
        halo_start(1, o, nat)
    for o in objects:
        halo_start(0, o, grad)
    for o in objects:
        halo_finish(1, o, nat)
        per_image(o, forward)
        pool_first(1, o, hid)
    finish(xg.at[mine], xsem.at[1])
    to_planes(theirs)
    halo_finish(0, 0, grad)
    per_image(0, act_grad(1))
    pool_second(1, 0)
    pool_second(1, 1)
    halo_finish(0, 1, grad)
    per_image(1, act_grad(1))
    for o in objects:
        pool_third(1, o)
        add_bands(pre1, o, hid)
        per_image(o, pre_grad1)
        pool_first(2, o, dzed)
    kernel_grad(act1)
    kernel_grad_start(1, [total(grad)])
    for o in objects:
        pool_second(2, o)
    for o in objects:
        pool_third(2, o)
        add_bands(grad, o, grad, dzed)
        per_image(o, rounded)
        halo_start(2, o, nat)
    finish(xg.at[pl.ds(0, 6)], xsem.at[3])
    finish(xg.at[pl.ds(0, 6)], xsem.at[2])
    sibling = {"obj": obj + 1 - 2 * lax.rem(obj, 2)}
    core = lax.rem(obj, 2)
    for half in range(2):
        held = xg.at[pl.ds(pl.multiple_of((core + 2 * half) * 4, 4), 4)]
        send(held, held, xsem.at[4], xsem.at[5], sibling)
    kernel_grad_second(1)
    sum_grad = total(grad)
    for o in objects:
        halo_finish(2, o, nat)
        per_image(o, act_grad(0))
        per_image(o, pre_grad0)
        pool_first(3, o, dzed)
    kernel_grad(act0)
    kernel_grad_start(0, [sum_grad, sum_grad + 3.0 * total(dzed)])
    for o in objects:
        pool_second(3, o)
    kernel_grad_middle(1)
    pool_third(3, 0)
    add_bands(grad, 0, grad, dzed)
    kernel_grad_second(0)
    pool_third(3, 1)
    add_bands(grad, 1, grad, dzed)
    for a in range(4):
        for b in range(4):
            for j in range(2):
                tg[a * 4 + b, j * 48:(j + 1) * 48, :] = grad[
                    pl.ds(a * 8 + 4 * j + b, 48, stride=32), :
                ].astype(BF16)
    for d in range(1, 16):
        other, where = group_a(d)
        send(tg.at[other], gg.at[mine], tsem.at[0], tsem.at[1], where)
    gg[mine] = tg[mine]
    kernel_grad_third(1)
    taps = jnp.concatenate([tg[n] for n in range(16)], axis=1)
    for part in range(4):
        dtok_ref[:, part * 256:(part + 1) * 256] = lax.dot_general(
            taps, w_ref[part * 256:(part + 1) * 256, :], (((1,), (1,)), ((), ())),
            preferred_element_type=F32,
        ).astype(BF16)
    kernel_grad_middle(0)
    finish(xg.at[mine], xsem.at[0])
    finish(xg.at[pl.ds(0, 8)], xsem.at[5])
    finish(xg.at[pl.ds(0, 8)], xsem.at[4])
    fifteen(gg, tsem.at[1])
    fifteen(tg, tsem.at[0])
    taken = gg[...].reshape(1536, 128)
    for part in range(4):
        product = lax.dot_general(
            taken, xg[:, :, part * 256:(part + 1) * 256].reshape(1536, 256),
            (((0,), (0,)), ((), ())), preferred_element_type=F32,
        )
        dwk[part * 256:(part + 1) * 256, :] = product.T
    for other in range(16):
        dws[other] = jnp.concatenate(
            [dwk[pl.ds(other * 4 + r, 16, stride=64), :] for r in range(4)], axis=0
        ).astype(BF16)
    for d in range(1, 16):
        other, where = group_b(d)
        send(dws.at[other], dwr.at[t], dwsem.at[0], dwsem.at[1], where)
    dwr[t] = dws[t]
    kernel_grad_third(0)
    kernel_grad_finish(1)
    fifteen(dwr, dwsem.at[1])
    fifteen(dws, dwsem.at[0])
    fin[...] = lax.fori_loop(
        1, 16, lambda n, acc: acc + dwr[n].astype(F32), dwr[0].astype(F32)
    )
    for other in range(16):
        fins[other, 0:4, :] = fin[pl.ds(other, 4, stride=16), :]
        fins[other, 4:8, :] = jnp.zeros((4, 128), F32)
    for d in range(1, 16):
        other, where = group_a(d)
        send(fins.at[other], finr.at[mine], finsem.at[0], finsem.at[1], where)
    finr[mine] = fins[mine]
    kernel_grad_finish(0)
    fifteen(finr, finsem.at[1])
    fifteen(fins, finsem.at[0])
    for n in range(16):
        dw_ref[:, n * 128:(n + 1) * 128] = finr[n, 0:4, :]


def scratch():
    dma = pltpu.SemaphoreType.DMA
    vmem = pltpu.VMEM
    full = (TOTAL, 128)
    padded = (IMAGES * PADDED, 128)
    return [
        vmem((1024, 2048), BF16), dma((4,)),
        vmem(full, F32), vmem(full, F32), vmem(full, F32), vmem(full, BF16), vmem(full, BF16),
        vmem(full, F32), vmem(full, F32), vmem(full, F32), vmem((2, 128, 1152), BF16), vmem((IMAGES, CELLS, 1152), BF16),
        vmem(padded, F32), vmem(padded, F32), vmem(padded, F32),
        vmem((192, 128), F32), vmem((48, 128), F32), vmem((192, 128), F32), vmem((48, 128), F32),
        vmem((128, 128), F32), vmem((64, 128), F32),
        vmem((8, 3, 80, 128), BF16), vmem((8, 3, 80, 128), BF16),
        vmem((8, 64, 128), BF16), vmem((8, 3, 64, 128), BF16),
        vmem((8, 16, 128), BF16), vmem((8, 3, 16, 128), BF16),
        vmem((8, 32, 128), BF16), vmem((8, 4, 32, 128), BF16),
        vmem((8, 16, 128), BF16), vmem((8, 4, 16, 128), BF16),
        dma((8, 2)), dma((8, 2)), dma((8, 2)), dma((8, 4)), dma((8, 4)), dma((8, 4)), dma((8, 4)),
        vmem((6, 2, 32, 128), BF16), vmem((6, 2, 96, 128), BF16),
        vmem((6, 2, 32, 128), BF16), vmem((6, 2, 96, 128), BF16), vmem((6, 4, 32, 128), BF16),
        dma((6, 8)), dma((6, 8)),
        vmem((16, 96, 1024), BF16), dma((6,)),
        vmem((16, 96, 128), BF16), vmem((16, 96, 128), BF16), dma((2,)),
        vmem((1024, 128), F32), vmem((16, 64, 128), BF16), vmem((16, 64, 128), BF16), dma((2,)),
        vmem((64, 128), F32), vmem((16, 8, 128), F32), vmem((16, 8, 128), F32), dma((2,)),
        vmem((16, 72, 128), F32), vmem((88, 128), F32), vmem((128, 1152), F32), vmem((2, 16, 80, 128), BF16), vmem((2, 16, 80, 128), BF16), dma((2, 2)),
        vmem((2, 16, 8, 128), F32), vmem((2, 16, 8, 128), F32), dma((2, 2)),
        vmem((2, 8, 128), F32), vmem((2, 16, 8, 128), F32), dma((2, 2)),
        vmem((2, 80, 128), BF16), vmem((2, 16, 80, 128), BF16), dma((2, 2)),
    ]


def results(dw_ref, dk_ref, bias_ref, dw_out, dk_out, db_out, cb_out):
    dw_out[...] = dw_ref[...]
    dk_out[...] = dk_ref[...].astype(F32)
    db_out[...] = bias_ref[1:2, :]
    cb_out[0:1, :] = bias_ref[0:1, :]
    cb_out[1:2, :] = bias_ref[8:9, :]


def per_device(tokens, gout, deconv_weight, deconv_bias, conv_kernels, conv_biases):
    flat = tokens.reshape(48, 2, 1024).transpose(1, 0, 2).reshape(96, 1024)
    here = pl.BlockSpec(memory_space=pltpu.VMEM)
    tok_grad, weight_grad, kernel_grads, biases = pl.pallas_call(
        kernel,
        out_shape=(
            jax.ShapeDtypeStruct((96, 1024), BF16),
            jax.ShapeDtypeStruct((4, 2048), F32),
            jax.ShapeDtypeStruct((2, 1152, 128), BF16),
            jax.ShapeDtypeStruct((16, 128), F32),
        ),
        in_specs=[here, here, pl.BlockSpec(memory_space=pl.ANY), here, here, here],
        out_specs=(here,) * 4,
        scratch_shapes=scratch(),
        compiler_params=pltpu.CompilerParams(
            collective_id=0, has_side_effects=True, vmem_limit_bytes=56 * 1024 * 1024
        ),
        name="triplane",
    )(
        flat, gout.reshape(TOTAL, 128), deconv_weight, deconv_bias.reshape(1, 128),
        conv_kernels, conv_biases.reshape(2, 1, 128),
    )
    tok_out = tok_grad.reshape(2, 48, 1024).transpose(1, 0, 2).reshape(tokens.shape)
    weight_out, kernel_out, bias_out, conv_bias_out = pl.pallas_call(
        results,
        out_shape=(
            jax.ShapeDtypeStruct((4, 2048), F32),
            jax.ShapeDtypeStruct((2, 1152, 128), F32),
            jax.ShapeDtypeStruct((1, 128), F32),
            jax.ShapeDtypeStruct((2, 128), F32),
        ),
        in_specs=[here] * 3,
        out_specs=(here,) * 4,
        name="results",
    )(weight_grad, kernel_grads, biases)
    return (tok_out, weight_out, bias_out.reshape(128), kernel_out, conv_bias_out)


def solution(mesh):
    split = P("obj", None, "plane", "tile", None)
    return jax.shard_map(
        per_device,
        mesh=mesh,
        in_specs=(split, split, P(), P(), P(), P()),
        out_specs=(split, P(("obj", "plane", "tile"), None), P(), P(), P()),
        check_vma=False,
    )
```

```python
import jax
import jax.numpy as jnp
from jax import lax
from jax.experimental import pallas as pl
from jax.experimental.pallas import tpu as pltpu
from jax.sharding import PartitionSpec as P

MESH = pl.DeviceIdType.MESH
F32 = jnp.float32
BF16 = jnp.bfloat16
IMAGES = 6
ROWS = 32
COLS = 8
CELLS = ROWS * COLS
TOTAL = IMAGES * CELLS
PADDED = (ROWS + 2) * COLS
HALF = 3 * CELLS

HALO = (
    (-1, 0, ("row", 0), ("row", 1)),
    (1, 0, ("row", 1), ("row", 0)),
    (0, -1, ("col", 0), ("col", 1)),
    (0, 1, ("col", 1), ("col", 0)),
    (-1, -1, ("row", 0), ("corner", 3)),
    (-1, 1, ("row", 0), ("corner", 2)),
    (1, -1, ("row", 1), ("corner", 1)),
    (1, 1, ("row", 1), ("corner", 0)),
)


def both(first, second):
    return jnp.logical_and(first, second)


def kernel(
    tok_ref, g_ref, w_hbm, db_ref, k_ref, cb_ref,
    dtok_ref, dw_ref, dk_ref, bias_ref,
    x_ref, w_ref, wsem, hid, pre0, pre1, act0, act1, grad, nat, dzed, kcat, col,
    centre, leftpad, rightpad, rowpart, colpart, rowband, colband,
    rowhalf, colzero,
    zs, zr, m1s, m1r, m2s, m2r, m3s, m3r, m4s, m4r,
    zsem, m1sem, m2sem, m3ss, m3rs, m4ss, m4rs,
    hsrow, hscol, hrrow, hrcol, hrcor, hss, hrs,
    xg, xsem, tg, gg, tsem, dwt, dwk, dws, dwr, dwsem, fin, fins, finr, finsem,
    dkf, dkacc, dka, dks, dkr, dksem, dkbs, dkbr, dkbsem, dkms, dkmr, dkmsem, dkcs, dkcr, dkcsem,
):
    obj, y, t = lax.axis_index("obj"), lax.axis_index("plane"), lax.axis_index("tile")
    x, z = t // 4, lax.rem(t, 4)
    mine = obj * 4 + y

    def group_a(d):
        other = lax.rem(mine + d, 16)
        return other, {"obj": other // 4, "plane": lax.rem(other, 4)}

    def group_b(d):
        other = lax.rem(t + d, 16)
        return other, {"tile": other}

    def send(src, dst, send_sem, recv_sem, where):
        copy = pltpu.make_async_remote_copy(
            src_ref=src, dst_ref=dst, send_sem=send_sem, recv_sem=recv_sem,
            device_id=where, device_id_type=MESH,
        )
        copy.start()

    def finish(ref, sem):
        pltpu.make_async_copy(ref, ref, sem).wait()

    def weight_part(part):
        at = slice(part * 512, (part + 1) * 512)
        return pltpu.make_async_copy(w_hbm.at[:, at], w_ref.at[:, at], wsem.at[part])

    for part in range(4):
        weight_part(part).start()
    hrrow[...] = jnp.zeros_like(hrrow)
    hrcol[...] = jnp.zeros_like(hrcol)
    hrcor[...] = jnp.zeros_like(hrcor)
    barrier = pltpu.get_barrier_semaphore()

    def greet(where):
        pl.semaphore_signal(barrier, inc=1, device_id=where, device_id_type=MESH)

    for d in range(1, 16):
        greet(group_a(d)[1])
        greet(group_b(d)[1])
    for dy in range(1, 4):
        for dx in range(1, 4):
            greet({"plane": lax.rem(y + dy, 4), "tile": lax.rem(x + dx, 4) * 4 + z})

    def inside(dy, dt):
        row_ok = both(y + dy >= 0, y + dy <= 3)
        return both(row_ok, both(t + dt >= 0, t + dt <= 15))

    diagonals = 0
    for dy, dt in ((-1, -1), (-1, 1), (1, -1), (1, 1)):
        ok = inside(dy, dt)

        @pl.when(ok)
        def _(dy=dy, dt=dt):
            greet({"plane": y + dy, "tile": t + dt})

        diagonals = diagonals + ok.astype(jnp.int32)

    for o in range(2):
        x_ref[48 * o:48 * o + 48, :] = jnp.concatenate(
            [tok_ref[24 * o:24 * o + 24, j, :].astype(F32) for j in range(2)], axis=0
        ).astype(BF16)
    for l in range(2):
        for tap in range(9):
            kcat[l, :, tap * 128:(tap + 1) * 128] = k_ref[l, tap * 128:(tap + 1) * 128, :]
    xg[mine] = x_ref[...]
    grad[...] = g_ref[...].astype(F32)

    for part in range(4):
        weight_part(part).wait()
        products = jnp.dot(
            x_ref[...], w_ref[:, part * 512:(part + 1) * 512], preferred_element_type=F32
        )
        for o in range(2):
            for j in range(2):
                for b in range(4):
                    at = pl.ds(o * HALF + part * 8 + 4 * j + b, 24, stride=32)
                    row = 48 * o + 24 * j
                    hid[at, :] = products[row:row + 24, b * 128:(b + 1) * 128] + db_ref[...]
    pl.semaphore_wait(barrier, 39 + diagonals)

    sources = {"row": hsrow, "col": hscol}
    targets = {"row": hrrow, "col": hrcol, "corner": hrcor}

    def halo_start(stage, o, ref):
        h = 2 * stage + o
        for side, at in ((0, 0), (1, CELLS - COLS)):
            edge = [ref[i * CELLS + at:i * CELLS + at + COLS, :] for i in range(3 * o, 3 * o + 3)]
            hsrow[h, side] = jnp.concatenate(edge + [jnp.zeros((8, 128), F32)], axis=0).astype(BF16)
        for side, at in ((0, 0), (1, COLS - 1)):
            hscol[h, side] = ref[pl.ds(o * HALF + at, 3 * ROWS, stride=COLS), :].astype(BF16)
        for n, (dy, dt, src, dst) in enumerate(HALO):

            @pl.when(inside(dy, dt))
            def _(n=n, dy=dy, dt=dt, src=src, dst=dst):
                send(
                    sources[src[0]].at[h, src[1]], targets[dst[0]].at[h, dst[1]],
                    hss.at[h, n], hrs.at[h, n], {"plane": y + dy, "tile": t + dt},
                )

    def halo_finish(stage, o, ref):
        h = 2 * stage + o
        for n, (dy, dt, src, dst) in enumerate(HALO):

            @pl.when(inside(-dy, -dt))
            def _(n=n, dst=dst):
                finish(targets[dst[0]].at[h, dst[1]], hrs.at[h, n])

            @pl.when(inside(dy, dt))
            def _(n=n, src=src):
                finish(sources[src[0]].at[h, src[1]], hss.at[h, n])

        top, bottom = hrrow[h, 0].astype(F32), hrrow[h, 1].astype(F32)
        left, right = hrcol[h, 0].astype(F32), hrcol[h, 1].astype(F32)
        corners = [hrcor[h, c].astype(F32) for c in range(4)]
        last = PADDED - COLS
        for p in range(3):
            i = 3 * o + p
            base = i * PADDED
            centre[base:base + COLS, :] = top[p * COLS:(p + 1) * COLS]
            centre[base + COLS:base + COLS + CELLS, :] = ref[i * CELLS:(i + 1) * CELLS, :]
            centre[base + last:base + PADDED, :] = bottom[p * COLS:(p + 1) * COLS]
            leftpad[pl.ds(base + COLS, ROWS, stride=COLS), :] = left[p * ROWS:(p + 1) * ROWS]
            rightpad[pl.ds(base + 2 * COLS - 1, ROWS, stride=COLS), :] = right[p * ROWS:(p + 1) * ROWS]
            first, final = p * COLS, (p + 1) * COLS - 1
            leftpad[base:base + 1, :] = corners[0][final:final + 1]
            leftpad[base + last:base + last + 1, :] = corners[2][final:final + 1]
            rightpad[base + COLS - 1:base + COLS, :] = corners[1][first:first + 1]
            rightpad[base + PADDED - 1:base + PADDED, :] = corners[3][first:first + 1]

    def shifted(i, flipped):
        base = pl.multiple_of(i * PADDED, 8)
        middle = centre[pl.ds(base, PADDED), :]
        place = lax.rem(lax.broadcasted_iota(jnp.int32, (PADDED, 128), 0), COLS)
        before = jnp.where(place == 0, leftpad[pl.ds(base, PADDED), :], pltpu.roll(middle, 1, 0))
        after = jnp.where(
            place == COLS - 1, rightpad[pl.ds(base, PADDED), :], pltpu.roll(middle, PADDED - 1, 0)
        )
        for tx, padded in enumerate((before, middle, after)):
            for ty in range(3):
                tap = (2 - ty) * 3 + (2 - tx) if flipped else ty * 3 + tx
                col[i, :, tap * 128:(tap + 1) * 128] = padded[ty * COLS:ty * COLS + CELLS].astype(BF16)

    same = x == y

    def pool_first(ph, o, ref):
        q = 2 * ph + o
        rows = ref[pl.ds(o * HALF, 3 * ROWS, stride=COLS), :]
        for v in range(1, COLS):
            rows = rows + ref[pl.ds(o * HALF + v, 3 * ROWS, stride=COLS), :]
        rowpart[o * 96:o * 96 + 96, :] = rows
        for i in range(3 * o, 3 * o + 3):
            colpart[i * COLS:(i + 1) * COLS, :] = jnp.sum(
                ref[i * CELLS:(i + 1) * CELLS, :].reshape(ROWS, COLS, 128), axis=0
            )
        common = jnp.concatenate([rows[0:64], colpart[24 * o:24 * o + 8, :]], axis=0)
        for d in range(1, 4):
            zd = lax.rem(z + d, 4)
            chunk = rowpart[pl.ds(pl.multiple_of(96 * o + 64 + 8 * zd, 8), 8), :]
            zs[q, d - 1] = jnp.concatenate([common, chunk], axis=0).astype(BF16)
            send(zs.at[q, d - 1], zr.at[q, d - 1], zsem.at[q, 0], zsem.at[q, 1], {"tile": x * 4 + zd})
        m2s[q] = colpart[24 * o + 8:24 * o + 24, :].astype(BF16)
        for d in range(1, 4):
            send(m2s.at[q], m2r.at[q, d - 1], m2sem.at[q, 0], m2sem.at[q, 1], {"plane": lax.rem(y + d, 4)})

    def pool_second(ph, o):
        q = 2 * ph + o
        finish(zr.at[q], zsem.at[q, 1])
        half = rowpart[o * 96:o * 96 + 64, :]
        two = rowpart[pl.ds(pl.multiple_of(96 * o + 64 + 8 * z, 8), 8), :]
        colzero[pl.ds(pl.multiple_of(32 * o + 8 * z, 8), 8), :] = colpart[24 * o:24 * o + 8, :]
        for d in range(1, 4):
            got = zr[q, d - 1].astype(F32)
            half = half + got[:64]
            two = two + got[72:80]
            source = lax.rem(z + 4 - d, 4)
            colzero[pl.ds(pl.multiple_of(32 * o + 8 * source, 8), 8), :] = got[64:72]
        rowhalf[o * 64:o * 64 + 64, :] = half
        m1s[q] = half.astype(BF16)
        m3s[q] = colzero[32 * o:32 * o + 32, :].astype(BF16)
        m4s[q] = jnp.concatenate([two, jnp.zeros((8, 128), F32)], axis=0).astype(BF16)
        for k in range(4):

            @pl.when(jnp.logical_not(both(same, x == k)))
            def _(k=k):
                send(m3s.at[q], m3r.at[q, y], m3ss.at[q, k], m3rs.at[q, y], {"plane": x, "tile": k * 4 + z})
                send(m4s.at[q], m4r.at[q, x], m4ss.at[q, k], m4rs.at[q, x], {"plane": k, "tile": y * 4 + z})

        for d in range(1, 4):
            send(m1s.at[q], m1r.at[q, d - 1], m1sem.at[q, 0], m1sem.at[q, 1], {"tile": lax.rem(x + d, 4) * 4 + z})

        @pl.when(same)
        def _():
            m3r[q, y] = m3s[q]
            m4r[q, x] = m4s[q]

    def pool_third(ph, o):
        q = 2 * ph + o
        finish(m2r.at[q], m2sem.at[q, 1])
        finish(m1r.at[q], m1sem.at[q, 1])
        for k in range(4):

            @pl.when(jnp.logical_not(both(same, x == k)))
            def _(k=k):
                finish(m3r.at[q, k], m3rs.at[q, k])
                finish(m4r.at[q, k], m4rs.at[q, k])
                finish(m3s.at[q], m3ss.at[q, k])
                finish(m4s.at[q], m4ss.at[q, k])

        finish(zs.at[q], zsem.at[q, 0])
        finish(m1r.at[q], m1sem.at[q, 0])
        finish(m2r.at[q], m2sem.at[q, 0])
        half = rowhalf[o * 64:o * 64 + 64, :]
        one = colpart[24 * o + 8:24 * o + 24, :]
        for d in range(3):
            half = half + m1r[q, d].astype(F32)
            one = one + m2r[q, d].astype(F32)
        zero = m3r[q, 0].astype(F32)
        two = m4r[q, 0].astype(F32)
        for k in range(1, 4):
            zero = zero + m3r[q, k].astype(F32)
            two = two + m4r[q, k].astype(F32)
        share = 1.0 / 128.0
        rowband[96 * o:96 * o + 32, :] = half[32:64] * share
        rowband[96 * o + 32:96 * o + 64, :] = half[0:32] * share
        rowband[96 * o + 64:96 * o + 96, :] = zero * share
        colband[24 * o:24 * o + 8, :] = two[0:8] * share
        colband[24 * o + 8:24 * o + 16, :] = one[8:16] * share
        colband[24 * o + 16:24 * o + 24, :] = one[0:8] * share

    def add_bands(dst, o, *srcs):
        for i in range(3 * o, 3 * o + 3):
            rb = rowband[i * ROWS:(i + 1) * ROWS, :]
            for v in range(COLS):
                at = pl.ds(i * CELLS + v, ROWS, stride=COLS)
                value = rb + colband[i * COLS + v:i * COLS + v + 1, :]
                for src in srcs:
                    value = value + src[at, :]
                dst[at, :] = value

    def per_image(o, body):
        def step(n, carry):
            i = n + 3 * o
            body(i, pl.ds(pl.multiple_of(i * CELLS, CELLS), CELLS))
            return carry

        lax.fori_loop(0, 3, step, 0)

    def silu0(i, at):
        value = pre0[at, :]
        rounded = (value * jax.nn.sigmoid(value)).astype(BF16)
        act0[at, :] = rounded
        nat[at, :] = rounded.astype(F32)

    def forward(i, at):
        shifted(i, False)
        out = jnp.dot(col[i], k_ref[0], preferred_element_type=F32)
        hid[at, :] = hid[at, :] + out + cb_ref[0]

    def act_grad(layer):
        def body(i, at):
            shifted(i, True)
            dzed[at, :] = lax.dot_general(
                col[i], kcat[layer], (((1,), (1,)), ((), ())), preferred_element_type=F32
            )

        return body

    def pre_grad1(i, at):
        value = pre1[at, :]
        s = jax.nn.sigmoid(value)
        act1[at, :] = (value * s).astype(BF16)
        dzed[at, :] = dzed[at, :] * s * (1.0 + value * (1.0 - s))

    def pre_grad0(i, at):
        value = pre0[at, :]
        s = jax.nn.sigmoid(value)
        dzed[at, :] = dzed[at, :] * s * (1.0 + value * (1.0 - s))

    def rounded(i, at):
        nat[at, :] = grad[at, :].astype(BF16).astype(F32)

    def kernel_grad(act):
        dka[...] = jnp.zeros_like(dka)

        def body(i, at):
            dka[...] += lax.dot_general(
                act[at, :], col[i], (((0,), (0,)), ((), ())), preferred_element_type=F32
            )

        for o in range(2):
            per_image(o, body)

    def total(ref):
        return jnp.sum(jnp.sum(ref[...].reshape(TOTAL // 8, 8, 128), axis=0), axis=0, keepdims=True)

    def kernel_grad_start(layer, extra):
        extras = jnp.concatenate(extra + [jnp.zeros((8 - len(extra), 128), F32)], axis=0)
        for g in range(16):
            rows = [dka[8 * g:8 * g + 8, tap * 128:(tap + 1) * 128] for tap in range(9)]
            dks[layer, g] = jnp.concatenate(rows + [extras], axis=0).astype(BF16)
        for d in range(1, 16):
            other, where = group_a(d)
            send(dks.at[layer, other], dkr.at[layer, mine], dksem.at[layer, 0], dksem.at[layer, 1], where)
        dkr[layer, mine] = dks[layer, mine]

    def fifteen(ref, sem):
        finish(ref.at[pl.ds(0, 15)], sem)

    def sum16(ref, layer):
        def step(n, acc):
            return acc + ref[layer, n].astype(F32)

        return lax.fori_loop(1, 16, step, ref[layer, 0].astype(F32))

    def kernel_grad_second(layer):
        fifteen(dkr.at[layer], dksem.at[layer, 1])
        fifteen(dks.at[layer], dksem.at[layer, 0])
        dkacc[0:80, :] = sum16(dkr, layer)
        dkacc[80:88, :] = jnp.zeros((8, 128), F32)
        for n in range(16):
            dkbs[layer, n] = dkacc[5 * n:5 * n + 8, :]
        for d in range(1, 16):
            other, where = group_b(d)
            send(dkbs.at[layer, other], dkbr.at[layer, t], dkbsem.at[layer, 0], dkbsem.at[layer, 1], where)
        dkbr[layer, t] = dkbs[layer, t]

    def kernel_grad_middle(layer):
        fifteen(dkbr.at[layer], dkbsem.at[layer, 1])
        fifteen(dkbr.at[layer], dkbsem.at[layer, 0])
        dkms[layer] = sum16(dkbr, layer)
        for d in range(1, 16):
            send(dkms.at[layer], dkmr.at[layer, t], dkmsem.at[layer, 0], dkmsem.at[layer, 1], group_b(d)[1])
        dkmr[layer, t] = dkms[layer]

    def kernel_grad_third(layer):
        fifteen(dkmr.at[layer], dkmsem.at[layer, 1])
        fifteen(dkmr.at[layer], dkmsem.at[layer, 0])
        for n in range(16):
            dkacc[5 * n:5 * n + 5, :] = dkmr[layer, n, 0:5, :]
        dkcs[layer] = dkacc[0:80, :].astype(BF16)
        for d in range(1, 16):
            send(dkcs.at[layer], dkcr.at[layer, mine], dkcsem.at[layer, 0], dkcsem.at[layer, 1], group_a(d)[1])
        dkcr[layer, mine] = dkcs[layer]

    def kernel_grad_finish(layer):
        fifteen(dkcr.at[layer], dkcsem.at[layer, 1])
        fifteen(dkcr.at[layer], dkcsem.at[layer, 0])
        for g in range(16):
            got = dkcr[layer, g].astype(F32)
            dkf[g] = got[:72]
            if g == 0:
                bias_ref[layer * 8:layer * 8 + 8, :] = got[72:80]
        for tap in range(9):
            dk_ref[layer, tap * 128:(tap + 1) * 128, :] = (
                dkf[:, 8 * tap:8 * tap + 8, :].reshape(128, 128).astype(BF16)
            )

    objects = range(2)
    theirs = lax.rem(obj + 2, 4) * 4 + y

    def to_planes(slot):
        for d in range(1, 4):
            send(xg.at[slot], xg.at[slot], xsem.at[2], xsem.at[3], {"plane": lax.rem(y + d, 4)})

    for o in objects:
        pool_first(0, o, hid)
    to_planes(mine)
    for o in objects:
        pool_second(0, o)
    partner = {"obj": lax.rem(obj + 2, 4)}
    send(xg.at[mine], xg.at[mine], xsem.at[0], xsem.at[1], partner)
    for o in objects:
        pool_third(0, o)
        add_bands(pre0, o, hid)
        per_image(o, silu0)
        halo_start(1, o, nat)
    for o in objects:
        halo_start(0, o, grad)
    for o in objects:
        halo_finish(1, o, nat)
        per_image(o, forward)
        pool_first(1, o, hid)
    finish(xg.at[mine], xsem.at[1])
    to_planes(theirs)
    halo_finish(0, 0, grad)
    per_image(0, act_grad(1))
    pool_second(1, 0)
    pool_second(1, 1)
    halo_finish(0, 1, grad)
    per_image(1, act_grad(1))
    for o in objects:
        pool_third(1, o)
        add_bands(pre1, o, hid)
        per_image(o, pre_grad1)
        pool_first(2, o, dzed)
    kernel_grad(act1)
    kernel_grad_start(1, [total(grad)])
    for o in objects:
        pool_second(2, o)
    for o in objects:
        pool_third(2, o)
        add_bands(grad, o, grad, dzed)
        per_image(o, rounded)
        halo_start(2, o, nat)
    finish(xg.at[pl.ds(0, 6)], xsem.at[3])
    finish(xg.at[pl.ds(0, 6)], xsem.at[2])
    sibling = {"obj": obj + 1 - 2 * lax.rem(obj, 2)}
    core = lax.rem(obj, 2)
    for half in range(2):
        held = xg.at[pl.ds(pl.multiple_of((core + 2 * half) * 4, 4), 4)]
        send(held, held, xsem.at[4], xsem.at[5], sibling)
    kernel_grad_second(1)
    sum_grad = total(grad)
    for o in objects:
        halo_finish(2, o, nat)
        per_image(o, act_grad(0))
        per_image(o, pre_grad0)
        pool_first(3, o, dzed)
    kernel_grad(act0)
    kernel_grad_start(0, [sum_grad, sum_grad + 3.0 * total(dzed)])
    for o in objects:
        pool_second(3, o)
    kernel_grad_middle(1)

    def send_taps(o):
        for a in range(4):
            for b in range(4):
                tg[o, a * 4 + b] = jnp.concatenate(
                    [grad[pl.ds(o * HALF + a * 8 + 4 * j + b, 24, stride=32), :] for j in range(2)], axis=0
                ).astype(BF16)
        for d in range(1, 16):
            other, where = group_a(d)
            send(tg.at[o, other], gg.at[o, mine], tsem.at[o, 0], tsem.at[o, 1], where)
        gg[o, mine] = tg[o, mine]

    pool_third(3, 0)
    add_bands(grad, 0, grad, dzed)
    send_taps(0)
    kernel_grad_second(0)
    pool_third(3, 1)
    add_bands(grad, 1, grad, dzed)
    send_taps(1)
    kernel_grad_third(1)
    taps = jnp.concatenate([tg[:, n].reshape(96, 128) for n in range(16)], axis=1)
    for part in range(4):
        at = slice(part * 256, (part + 1) * 256)
        tok_grad = lax.dot_general(
            taps, w_ref[at, :], (((1,), (1,)), ((), ())), preferred_element_type=F32
        )
        for o in range(2):
            for j in range(2):
                row = 48 * o + 24 * j
                dtok_ref[24 * o:24 * o + 24, j, at] = tok_grad[row:row + 24].astype(BF16)
    kernel_grad_middle(0)
    finish(xg.at[mine], xsem.at[0])
    finish(xg.at[pl.ds(0, 8)], xsem.at[5])
    finish(xg.at[pl.ds(0, 8)], xsem.at[4])
    for o in range(2):
        fifteen(gg.at[o], tsem.at[o, 1])
        fifteen(tg.at[o], tsem.at[o, 0])
        taken = gg[o].reshape(768, 128)
        for part in range(4):
            at = slice(part * 256, (part + 1) * 256)
            product = lax.dot_general(
                taken, xg[:, 48 * o:48 * o + 48, at].reshape(768, 256),
                (((0,), (0,)), ((), ())), preferred_element_type=F32,
            )
            if o == 0:
                dwt[:, at] = product
            else:
                dwk[at, :] = (dwt[:, at] + product).T
    for other in range(16):
        dws[other] = jnp.concatenate(
            [dwk[pl.ds(other * 4 + r, 16, stride=64), :] for r in range(4)], axis=0
        ).astype(BF16)
    for d in range(1, 16):
        other, where = group_b(d)
        send(dws.at[other], dwr.at[t], dwsem.at[0], dwsem.at[1], where)
    dwr[t] = dws[t]
    kernel_grad_third(0)
    kernel_grad_finish(1)
    fifteen(dwr, dwsem.at[1])
    fifteen(dws, dwsem.at[0])
    fin[...] = lax.fori_loop(
        1, 16, lambda n, acc: acc + dwr[n].astype(F32), dwr[0].astype(F32)
    )
    for other in range(16):
        fins[other, 0:4, :] = fin[pl.ds(other, 4, stride=16), :]
        fins[other, 4:8, :] = jnp.zeros((4, 128), F32)
    for d in range(1, 16):
        other, where = group_a(d)
        send(fins.at[other], finr.at[mine], finsem.at[0], finsem.at[1], where)
    finr[mine] = fins[mine]
    kernel_grad_finish(0)
    fifteen(finr, finsem.at[1])
    fifteen(fins, finsem.at[0])
    for n in range(16):
        dw_ref[:, n * 128:(n + 1) * 128] = finr[n, 0:4, :]


def scratch():
    dma = pltpu.SemaphoreType.DMA
    vmem = pltpu.VMEM
    full = (TOTAL, 128)
    padded = (IMAGES * PADDED, 128)
    return [
        vmem((96, 1024), BF16), vmem((1024, 2048), BF16), dma((4,)),
        vmem(full, F32), vmem(full, F32), vmem(full, F32), vmem(full, BF16), vmem(full, BF16),
        vmem(full, F32), vmem(full, F32), vmem(full, F32), vmem((2, 128, 1152), BF16), vmem((IMAGES, CELLS, 1152), BF16),
        vmem(padded, F32), vmem(padded, F32), vmem(padded, F32),
        vmem((192, 128), F32), vmem((48, 128), F32), vmem((192, 128), F32), vmem((48, 128), F32),
        vmem((128, 128), F32), vmem((64, 128), F32),
        vmem((8, 3, 80, 128), BF16), vmem((8, 3, 80, 128), BF16),
        vmem((8, 64, 128), BF16), vmem((8, 3, 64, 128), BF16),
        vmem((8, 16, 128), BF16), vmem((8, 3, 16, 128), BF16),
        vmem((8, 32, 128), BF16), vmem((8, 4, 32, 128), BF16),
        vmem((8, 16, 128), BF16), vmem((8, 4, 16, 128), BF16),
        dma((8, 2)), dma((8, 2)), dma((8, 2)), dma((8, 4)), dma((8, 4)), dma((8, 4)), dma((8, 4)),
        vmem((6, 2, 32, 128), BF16), vmem((6, 2, 96, 128), BF16),
        vmem((6, 2, 32, 128), BF16), vmem((6, 2, 96, 128), BF16), vmem((6, 4, 32, 128), BF16),
        dma((6, 8)), dma((6, 8)),
        vmem((16, 96, 1024), BF16), dma((6,)),
        vmem((2, 16, 48, 128), BF16), vmem((2, 16, 48, 128), BF16), dma((2, 2)), vmem((128, 1024), F32),
        vmem((1024, 128), F32), vmem((16, 64, 128), BF16), vmem((16, 64, 128), BF16), dma((2,)),
        vmem((64, 128), F32), vmem((16, 8, 128), F32), vmem((16, 8, 128), F32), dma((2,)),
        vmem((16, 72, 128), F32), vmem((88, 128), F32), vmem((128, 1152), F32), vmem((2, 16, 80, 128), BF16), vmem((2, 16, 80, 128), BF16), dma((2, 2)),
        vmem((2, 16, 8, 128), F32), vmem((2, 16, 8, 128), F32), dma((2, 2)),
        vmem((2, 8, 128), F32), vmem((2, 16, 8, 128), F32), dma((2, 2)),
        vmem((2, 80, 128), BF16), vmem((2, 16, 80, 128), BF16), dma((2, 2)),
    ]


def results(dtok_ref, dw_ref, dk_ref, bias_ref, dtok_out, dw_out, dk_out, db_out, cb_out, sem):
    copy = pltpu.make_async_copy(dtok_ref, dtok_out, sem)
    copy.start()
    dw_out[...] = dw_ref[...]
    dk_out[...] = dk_ref[...].astype(F32)
    db_out[...] = bias_ref[1:2, :]
    cb_out[0:1, :] = bias_ref[0:1, :]
    cb_out[1:2, :] = bias_ref[8:9, :]
    copy.wait()


def per_device(tokens, gout, deconv_weight, deconv_bias, conv_kernels, conv_biases):
    here = pl.BlockSpec(memory_space=pltpu.VMEM)
    tok_grad, weight_grad, kernel_grads, biases = pl.pallas_call(
        kernel,
        out_shape=(
            jax.ShapeDtypeStruct((48, 2, 1024), BF16),
            jax.ShapeDtypeStruct((4, 2048), F32),
            jax.ShapeDtypeStruct((2, 1152, 128), BF16),
            jax.ShapeDtypeStruct((16, 128), F32),
        ),
        in_specs=[here, here, pl.BlockSpec(memory_space=pl.ANY), here, here, here],
        out_specs=(here,) * 4,
        scratch_shapes=scratch(),
        compiler_params=pltpu.CompilerParams(
            collective_id=0, has_side_effects=True, vmem_limit_bytes=56 * 1024 * 1024
        ),
        name="triplane",
    )(
        tokens.reshape(48, 2, 1024), gout.reshape(TOTAL, 128), deconv_weight, deconv_bias.reshape(1, 128),
        conv_kernels, conv_biases.reshape(2, 1, 128),
    )
    anywhere = pl.BlockSpec(memory_space=pl.ANY)
    tok_out, weight_out, kernel_out, bias_out, conv_bias_out = pl.pallas_call(
        results,
        out_shape=(
            jax.ShapeDtypeStruct((48, 2, 1024), BF16),
            jax.ShapeDtypeStruct((4, 2048), F32),
            jax.ShapeDtypeStruct((2, 1152, 128), F32),
            jax.ShapeDtypeStruct((1, 128), F32),
            jax.ShapeDtypeStruct((2, 128), F32),
        ),
        in_specs=[anywhere] + [here] * 3,
        out_specs=(anywhere,) + (here,) * 4,
        scratch_shapes=[pltpu.SemaphoreType.DMA],
        name="results",
    )(tok_grad, weight_grad, kernel_grads, biases)
    return (tok_out.reshape(tokens.shape), weight_out, bias_out.reshape(128), kernel_out, conv_bias_out)


def solution(mesh):
    split = P("obj", None, "plane", "tile", None)
    return jax.shard_map(
        per_device,
        mesh=mesh,
        in_specs=(split, split, P(), P(), P(), P()),
        out_specs=(split, P(("obj", "plane", "tile"), None), P(), P(), P()),
        check_vma=False,
    )
```

```python
import jax
import jax.numpy as jnp
from jax import lax
from jax.experimental import pallas as pl
from jax.experimental.pallas import tpu as pltpu
from jax.sharding import PartitionSpec as P

MESH = pl.DeviceIdType.MESH
F32 = jnp.float32
BF16 = jnp.bfloat16
IMAGES = 6
ROWS = 32
COLS = 8
CELLS = ROWS * COLS
TOTAL = IMAGES * CELLS
PADDED = (ROWS + 2) * COLS
HALF = 3 * CELLS

HALO = (
    (-1, 0, ("row", 0), ("row", 1)),
    (1, 0, ("row", 1), ("row", 0)),
    (0, -1, ("col", 0), ("col", 1)),
    (0, 1, ("col", 1), ("col", 0)),
    (-1, -1, ("row", 0), ("corner", 3)),
    (-1, 1, ("row", 0), ("corner", 2)),
    (1, -1, ("row", 1), ("corner", 1)),
    (1, 1, ("row", 1), ("corner", 0)),
)


def both(first, second):
    return jnp.logical_and(first, second)


def kernel(
    tok_ref, g_hbm, w_hbm, db_ref, k_hbm, cb_ref,
    dtok_ref, dw_ref, dk_ref, bias_ref,
    g_ref, k_ref, insem, x_ref, w_ref, wsem, hid, pre0, pre1, act0, act1, grad, nat, dzed, kcat, col,
    centre, leftpad, rightpad, rowpart, colpart, rowband, colband,
    rowhalf, colzero,
    zs, zr, m1s, m1r, m2s, m2r, m3s, m3r, m4s, m4r,
    zsem, m1sem, m2sem, m3ss, m3rs, m4ss, m4rs,
    hsrow, hscol, hrrow, hrcol, hrcor, hss, hrs,
    xg, xsem, tg, gg, tsem, dwt, dwk, dws, dwr, dwsem, fin, fins, finr, finsem,
    dkf, dkacc, dka, dks, dkr, dksem, dkbs, dkbr, dkbsem, dkms, dkmr, dkmsem, dkcs, dkcr, dkcsem,
):
    obj, y, t = lax.axis_index("obj"), lax.axis_index("plane"), lax.axis_index("tile")
    x, z = t // 4, lax.rem(t, 4)
    mine = obj * 4 + y

    def group_a(d):
        other = lax.rem(mine + d, 16)
        return other, {"obj": other // 4, "plane": lax.rem(other, 4)}

    def group_b(d):
        other = lax.rem(t + d, 16)
        return other, {"tile": other}

    def send(src, dst, send_sem, recv_sem, where):
        copy = pltpu.make_async_remote_copy(
            src_ref=src, dst_ref=dst, send_sem=send_sem, recv_sem=recv_sem,
            device_id=where, device_id_type=MESH,
        )
        copy.start()

    def finish(ref, sem):
        pltpu.make_async_copy(ref, ref, sem).wait()

    def weight_part(part):
        at = slice(part * 512, (part + 1) * 512)
        return pltpu.make_async_copy(w_hbm.at[:, at], w_ref.at[:, at], wsem.at[part])

    arrivals = [
        pltpu.make_async_copy(src, dst, insem.at[n])
        for n, (src, dst) in enumerate(((g_hbm, g_ref), (k_hbm, k_ref)))
    ]
    for part in range(4):
        weight_part(part).start()
    arrivals[0].start()
    arrivals[1].start()
    hrrow[...] = jnp.zeros_like(hrrow)
    hrcol[...] = jnp.zeros_like(hrcol)
    hrcor[...] = jnp.zeros_like(hrcor)
    barrier = pltpu.get_barrier_semaphore()

    def greet(where):
        pl.semaphore_signal(barrier, inc=1, device_id=where, device_id_type=MESH)

    for d in range(1, 16):
        greet(group_a(d)[1])
        greet(group_b(d)[1])
    for dy in range(1, 4):
        for dx in range(1, 4):
            greet({"plane": lax.rem(y + dy, 4), "tile": lax.rem(x + dx, 4) * 4 + z})

    def inside(dy, dt):
        row_ok = both(y + dy >= 0, y + dy <= 3)
        return both(row_ok, both(t + dt >= 0, t + dt <= 15))

    diagonals = 0
    for dy, dt in ((-1, -1), (-1, 1), (1, -1), (1, 1)):
        ok = inside(dy, dt)

        @pl.when(ok)
        def _(dy=dy, dt=dt):
            greet({"plane": y + dy, "tile": t + dt})

        diagonals = diagonals + ok.astype(jnp.int32)

    for o in range(2):
        x_ref[48 * o:48 * o + 48, :] = jnp.concatenate(
            [tok_ref[24 * o:24 * o + 24, j, :].astype(F32) for j in range(2)], axis=0
        ).astype(BF16)
    xg[mine] = x_ref[...]
    for part in range(4):
        weight_part(part).wait()
        products = jnp.dot(
            x_ref[...], w_ref[:, part * 512:(part + 1) * 512], preferred_element_type=F32
        )
        for o in range(2):
            for j in range(2):
                for b in range(4):
                    at = pl.ds(o * HALF + part * 8 + 4 * j + b, 24, stride=32)
                    row = 48 * o + 24 * j
                    hid[at, :] = products[row:row + 24, b * 128:(b + 1) * 128] + db_ref[...]
    pl.semaphore_wait(barrier, 39 + diagonals)

    sources = {"row": hsrow, "col": hscol}
    targets = {"row": hrrow, "col": hrcol, "corner": hrcor}

    def halo_start(stage, o, ref):
        h = 2 * stage + o
        for side, at in ((0, 0), (1, CELLS - COLS)):
            edge = [ref[i * CELLS + at:i * CELLS + at + COLS, :] for i in range(3 * o, 3 * o + 3)]
            hsrow[h, side] = jnp.concatenate(edge + [jnp.zeros((8, 128), F32)], axis=0).astype(BF16)
        for side, at in ((0, 0), (1, COLS - 1)):
            hscol[h, side] = ref[pl.ds(o * HALF + at, 3 * ROWS, stride=COLS), :].astype(BF16)
        for n, (dy, dt, src, dst) in enumerate(HALO):

            @pl.when(inside(dy, dt))
            def _(n=n, dy=dy, dt=dt, src=src, dst=dst):
                send(
                    sources[src[0]].at[h, src[1]], targets[dst[0]].at[h, dst[1]],
                    hss.at[h, n], hrs.at[h, n], {"plane": y + dy, "tile": t + dt},
                )

    def halo_finish(stage, o, ref):
        h = 2 * stage + o
        for n, (dy, dt, src, dst) in enumerate(HALO):

            @pl.when(inside(-dy, -dt))
            def _(n=n, dst=dst):
                finish(targets[dst[0]].at[h, dst[1]], hrs.at[h, n])

            @pl.when(inside(dy, dt))
            def _(n=n, src=src):
                finish(sources[src[0]].at[h, src[1]], hss.at[h, n])

        top, bottom = hrrow[h, 0].astype(F32), hrrow[h, 1].astype(F32)
        left, right = hrcol[h, 0].astype(F32), hrcol[h, 1].astype(F32)
        corners = [hrcor[h, c].astype(F32) for c in range(4)]
        last = PADDED - COLS
        for p in range(3):
            i = 3 * o + p
            base = i * PADDED
            centre[base:base + COLS, :] = top[p * COLS:(p + 1) * COLS]
            centre[base + COLS:base + COLS + CELLS, :] = ref[i * CELLS:(i + 1) * CELLS, :]
            centre[base + last:base + PADDED, :] = bottom[p * COLS:(p + 1) * COLS]
            leftpad[pl.ds(base + COLS, ROWS, stride=COLS), :] = left[p * ROWS:(p + 1) * ROWS]
            rightpad[pl.ds(base + 2 * COLS - 1, ROWS, stride=COLS), :] = right[p * ROWS:(p + 1) * ROWS]
            first, final = p * COLS, (p + 1) * COLS - 1
            leftpad[base:base + 1, :] = corners[0][final:final + 1]
            leftpad[base + last:base + last + 1, :] = corners[2][final:final + 1]
            rightpad[base + COLS - 1:base + COLS, :] = corners[1][first:first + 1]
            rightpad[base + PADDED - 1:base + PADDED, :] = corners[3][first:first + 1]

    def shifted(i, flipped):
        base = pl.multiple_of(i * PADDED, 8)
        middle = centre[pl.ds(base, PADDED), :]
        place = lax.rem(lax.broadcasted_iota(jnp.int32, (PADDED, 128), 0), COLS)
        before = jnp.where(place == 0, leftpad[pl.ds(base, PADDED), :], pltpu.roll(middle, 1, 0))
        after = jnp.where(
            place == COLS - 1, rightpad[pl.ds(base, PADDED), :], pltpu.roll(middle, PADDED - 1, 0)
        )
        for tx, padded in enumerate((before, middle, after)):
            for ty in range(3):
                tap = (2 - ty) * 3 + (2 - tx) if flipped else ty * 3 + tx
                col[i, :, tap * 128:(tap + 1) * 128] = padded[ty * COLS:ty * COLS + CELLS].astype(BF16)

    same = x == y

    def pool_first(ph, o, ref):
        q = 2 * ph + o
        rows = ref[pl.ds(o * HALF, 3 * ROWS, stride=COLS), :]
        for v in range(1, COLS):
            rows = rows + ref[pl.ds(o * HALF + v, 3 * ROWS, stride=COLS), :]
        rowpart[o * 96:o * 96 + 96, :] = rows
        for i in range(3 * o, 3 * o + 3):
            colpart[i * COLS:(i + 1) * COLS, :] = jnp.sum(
                ref[i * CELLS:(i + 1) * CELLS, :].reshape(ROWS, COLS, 128), axis=0
            )
        common = jnp.concatenate([rows[0:64], colpart[24 * o:24 * o + 8, :]], axis=0)
        for d in range(1, 4):
            zd = lax.rem(z + d, 4)
            chunk = rowpart[pl.ds(pl.multiple_of(96 * o + 64 + 8 * zd, 8), 8), :]
            zs[q, d - 1] = jnp.concatenate([common, chunk], axis=0).astype(BF16)
            send(zs.at[q, d - 1], zr.at[q, d - 1], zsem.at[q, 0], zsem.at[q, 1], {"tile": x * 4 + zd})
        m2s[q] = colpart[24 * o + 8:24 * o + 24, :].astype(BF16)
        for d in range(1, 4):
            send(m2s.at[q], m2r.at[q, d - 1], m2sem.at[q, 0], m2sem.at[q, 1], {"plane": lax.rem(y + d, 4)})

    def pool_second(ph, o):
        q = 2 * ph + o
        finish(zr.at[q], zsem.at[q, 1])
        half = rowpart[o * 96:o * 96 + 64, :]
        two = rowpart[pl.ds(pl.multiple_of(96 * o + 64 + 8 * z, 8), 8), :]
        colzero[pl.ds(pl.multiple_of(32 * o + 8 * z, 8), 8), :] = colpart[24 * o:24 * o + 8, :]
        for d in range(1, 4):
            got = zr[q, d - 1].astype(F32)
            half = half + got[:64]
            two = two + got[72:80]
            source = lax.rem(z + 4 - d, 4)
            colzero[pl.ds(pl.multiple_of(32 * o + 8 * source, 8), 8), :] = got[64:72]
        rowhalf[o * 64:o * 64 + 64, :] = half
        m1s[q] = half.astype(BF16)
        m3s[q] = colzero[32 * o:32 * o + 32, :].astype(BF16)
        m4s[q] = jnp.concatenate([two, jnp.zeros((8, 128), F32)], axis=0).astype(BF16)
        for k in range(4):

            @pl.when(jnp.logical_not(both(same, x == k)))
            def _(k=k):
                send(m3s.at[q], m3r.at[q, y], m3ss.at[q, k], m3rs.at[q, y], {"plane": x, "tile": k * 4 + z})
                send(m4s.at[q], m4r.at[q, x], m4ss.at[q, k], m4rs.at[q, x], {"plane": k, "tile": y * 4 + z})

        for d in range(1, 4):
            send(m1s.at[q], m1r.at[q, d - 1], m1sem.at[q, 0], m1sem.at[q, 1], {"tile": lax.rem(x + d, 4) * 4 + z})

        @pl.when(same)
        def _():
            m3r[q, y] = m3s[q]
            m4r[q, x] = m4s[q]

    def pool_third(ph, o):
        q = 2 * ph + o
        finish(m2r.at[q], m2sem.at[q, 1])
        finish(m1r.at[q], m1sem.at[q, 1])
        for k in range(4):

            @pl.when(jnp.logical_not(both(same, x == k)))
            def _(k=k):
                finish(m3r.at[q, k], m3rs.at[q, k])
                finish(m4r.at[q, k], m4rs.at[q, k])
                finish(m3s.at[q], m3ss.at[q, k])
                finish(m4s.at[q], m4ss.at[q, k])

        finish(zs.at[q], zsem.at[q, 0])
        finish(m1r.at[q], m1sem.at[q, 0])
        finish(m2r.at[q], m2sem.at[q, 0])
        half = rowhalf[o * 64:o * 64 + 64, :]
        one = colpart[24 * o + 8:24 * o + 24, :]
        for d in range(3):
            half = half + m1r[q, d].astype(F32)
            one = one + m2r[q, d].astype(F32)
        zero = m3r[q, 0].astype(F32)
        two = m4r[q, 0].astype(F32)
        for k in range(1, 4):
            zero = zero + m3r[q, k].astype(F32)
            two = two + m4r[q, k].astype(F32)
        share = 1.0 / 128.0
        rowband[96 * o:96 * o + 32, :] = half[32:64] * share
        rowband[96 * o + 32:96 * o + 64, :] = half[0:32] * share
        rowband[96 * o + 64:96 * o + 96, :] = zero * share
        colband[24 * o:24 * o + 8, :] = two[0:8] * share
        colband[24 * o + 8:24 * o + 16, :] = one[8:16] * share
        colband[24 * o + 16:24 * o + 24, :] = one[0:8] * share

    def add_bands(dst, o, *srcs):
        for i in range(3 * o, 3 * o + 3):
            rb = rowband[i * ROWS:(i + 1) * ROWS, :]
            for v in range(COLS):
                at = pl.ds(i * CELLS + v, ROWS, stride=COLS)
                value = rb + colband[i * COLS + v:i * COLS + v + 1, :]
                for src in srcs:
                    value = value + src[at, :]
                dst[at, :] = value

    def per_image(o, body):
        def step(n, carry):
            i = n + 3 * o
            body(i, pl.ds(pl.multiple_of(i * CELLS, CELLS), CELLS))
            return carry

        lax.fori_loop(0, 3, step, 0)

    def silu0(i, at):
        value = pre0[at, :]
        rounded = (value * jax.nn.sigmoid(value)).astype(BF16)
        act0[at, :] = rounded
        nat[at, :] = rounded.astype(F32)

    def forward(i, at):
        shifted(i, False)
        out = jnp.dot(col[i], k_ref[0], preferred_element_type=F32)
        hid[at, :] = hid[at, :] + out + cb_ref[0]

    def act_grad(layer):
        def body(i, at):
            shifted(i, True)
            dzed[at, :] = lax.dot_general(
                col[i], kcat[layer], (((1,), (1,)), ((), ())), preferred_element_type=F32
            )

        return body

    def pre_grad1(i, at):
        value = pre1[at, :]
        s = jax.nn.sigmoid(value)
        act1[at, :] = (value * s).astype(BF16)
        dzed[at, :] = dzed[at, :] * s * (1.0 + value * (1.0 - s))

    def pre_grad0(i, at):
        value = pre0[at, :]
        s = jax.nn.sigmoid(value)
        dzed[at, :] = dzed[at, :] * s * (1.0 + value * (1.0 - s))

    def rounded(i, at):
        nat[at, :] = grad[at, :].astype(BF16).astype(F32)

    def kernel_grad(act):
        dka[...] = jnp.zeros_like(dka)

        def body(i, at):
            dka[...] += lax.dot_general(
                act[at, :], col[i], (((0,), (0,)), ((), ())), preferred_element_type=F32
            )

        for o in range(2):
            per_image(o, body)

    def total(ref):
        return jnp.sum(jnp.sum(ref[...].reshape(TOTAL // 8, 8, 128), axis=0), axis=0, keepdims=True)

    def kernel_grad_start(layer, extra):
        extras = jnp.concatenate(extra + [jnp.zeros((8 - len(extra), 128), F32)], axis=0)
        for g in range(16):
            rows = [dka[8 * g:8 * g + 8, tap * 128:(tap + 1) * 128] for tap in range(9)]
            dks[layer, g] = jnp.concatenate(rows + [extras], axis=0).astype(BF16)
        for d in range(1, 16):
            other, where = group_a(d)
            send(dks.at[layer, other], dkr.at[layer, mine], dksem.at[layer, 0], dksem.at[layer, 1], where)
        dkr[layer, mine] = dks[layer, mine]

    def fifteen(ref, sem):
        finish(ref.at[pl.ds(0, 15)], sem)

    def sum16(ref, layer):
        def step(n, acc):
            return acc + ref[layer, n].astype(F32)

        return lax.fori_loop(1, 16, step, ref[layer, 0].astype(F32))

    def kernel_grad_second(layer):
        fifteen(dkr.at[layer], dksem.at[layer, 1])
        fifteen(dks.at[layer], dksem.at[layer, 0])
        dkacc[0:80, :] = sum16(dkr, layer)
        dkacc[80:88, :] = jnp.zeros((8, 128), F32)
        for n in range(16):
            dkbs[layer, n] = dkacc[5 * n:5 * n + 8, :]
        for d in range(1, 16):
            other, where = group_b(d)
            send(dkbs.at[layer, other], dkbr.at[layer, t], dkbsem.at[layer, 0], dkbsem.at[layer, 1], where)
        dkbr[layer, t] = dkbs[layer, t]

    def kernel_grad_middle(layer):
        fifteen(dkbr.at[layer], dkbsem.at[layer, 1])
        fifteen(dkbr.at[layer], dkbsem.at[layer, 0])
        dkms[layer] = sum16(dkbr, layer)
        for d in range(1, 16):
            send(dkms.at[layer], dkmr.at[layer, t], dkmsem.at[layer, 0], dkmsem.at[layer, 1], group_b(d)[1])
        dkmr[layer, t] = dkms[layer]

    def kernel_grad_third(layer):
        fifteen(dkmr.at[layer], dkmsem.at[layer, 1])
        fifteen(dkmr.at[layer], dkmsem.at[layer, 0])
        for n in range(16):
            dkacc[5 * n:5 * n + 5, :] = dkmr[layer, n, 0:5, :]
        dkcs[layer] = dkacc[0:80, :].astype(BF16)
        for d in range(1, 16):
            send(dkcs.at[layer], dkcr.at[layer, mine], dkcsem.at[layer, 0], dkcsem.at[layer, 1], group_a(d)[1])
        dkcr[layer, mine] = dkcs[layer]

    def kernel_grad_finish(layer):
        fifteen(dkcr.at[layer], dkcsem.at[layer, 1])
        fifteen(dkcr.at[layer], dkcsem.at[layer, 0])
        for g in range(16):
            got = dkcr[layer, g].astype(F32)
            dkf[g] = got[:72]
            if g == 0:
                bias_ref[layer * 8:layer * 8 + 8, :] = got[72:80]
        for tap in range(9):
            dk_ref[layer, tap * 128:(tap + 1) * 128, :] = (
                dkf[:, 8 * tap:8 * tap + 8, :].reshape(128, 128).astype(BF16)
            )

    objects = range(2)
    theirs = lax.rem(obj + 2, 4) * 4 + y

    def to_planes(slot):
        for d in range(1, 4):
            send(xg.at[slot], xg.at[slot], xsem.at[2], xsem.at[3], {"plane": lax.rem(y + d, 4)})

    for o in objects:
        pool_first(0, o, hid)
    to_planes(mine)
    arrivals[0].wait()
    arrivals[1].wait()
    for l in range(2):
        for tap in range(9):
            kcat[l, :, tap * 128:(tap + 1) * 128] = k_ref[l, tap * 128:(tap + 1) * 128, :]
    grad[...] = g_ref[...].astype(F32)
    for o in objects:
        pool_second(0, o)
    partner = {"obj": lax.rem(obj + 2, 4)}
    send(xg.at[mine], xg.at[mine], xsem.at[0], xsem.at[1], partner)
    for o in objects:
        pool_third(0, o)
        add_bands(pre0, o, hid)
        per_image(o, silu0)
        halo_start(1, o, nat)
    for o in objects:
        halo_start(0, o, grad)
    for o in objects:
        halo_finish(1, o, nat)
        per_image(o, forward)
        pool_first(1, o, hid)
    finish(xg.at[mine], xsem.at[1])
    to_planes(theirs)
    halo_finish(0, 0, grad)
    per_image(0, act_grad(1))
    pool_second(1, 0)
    pool_second(1, 1)
    halo_finish(0, 1, grad)
    per_image(1, act_grad(1))
    for o in objects:
        pool_third(1, o)
        add_bands(pre1, o, hid)
        per_image(o, pre_grad1)
        pool_first(2, o, dzed)
    kernel_grad(act1)
    kernel_grad_start(1, [total(grad)])
    for o in objects:
        pool_second(2, o)
    for o in objects:
        pool_third(2, o)
        add_bands(grad, o, grad, dzed)
        per_image(o, rounded)
        halo_start(2, o, nat)
    finish(xg.at[pl.ds(0, 6)], xsem.at[3])
    finish(xg.at[pl.ds(0, 6)], xsem.at[2])
    sibling = {"obj": obj + 1 - 2 * lax.rem(obj, 2)}
    core = lax.rem(obj, 2)
    for half in range(2):
        held = xg.at[pl.ds(pl.multiple_of((core + 2 * half) * 4, 4), 4)]
        send(held, held, xsem.at[4], xsem.at[5], sibling)
    kernel_grad_second(1)
    sum_grad = total(grad)
    for o in objects:
        halo_finish(2, o, nat)
        per_image(o, act_grad(0))
        per_image(o, pre_grad0)
        pool_first(3, o, dzed)
    kernel_grad(act0)
    kernel_grad_start(0, [sum_grad, sum_grad + 3.0 * total(dzed)])
    for o in objects:
        pool_second(3, o)
    kernel_grad_middle(1)

    def send_taps(o):
        for a in range(4):
            for b in range(4):
                tg[o, a * 4 + b] = jnp.concatenate(
                    [grad[pl.ds(o * HALF + a * 8 + 4 * j + b, 24, stride=32), :] for j in range(2)], axis=0
                ).astype(BF16)
        for d in range(1, 16):
            other, where = group_a(d)
            send(tg.at[o, other], gg.at[o, mine], tsem.at[o, 0], tsem.at[o, 1], where)
        gg[o, mine] = tg[o, mine]

    pool_third(3, 0)
    add_bands(grad, 0, grad, dzed)
    send_taps(0)
    kernel_grad_second(0)
    pool_third(3, 1)
    add_bands(grad, 1, grad, dzed)
    send_taps(1)
    kernel_grad_third(1)
    taps = jnp.concatenate([tg[:, n].reshape(96, 128) for n in range(16)], axis=1)
    for part in range(4):
        at = slice(part * 256, (part + 1) * 256)
        tok_grad = lax.dot_general(
            taps, w_ref[at, :], (((1,), (1,)), ((), ())), preferred_element_type=F32
        )
        for o in range(2):
            for j in range(2):
                row = 48 * o + 24 * j
                dtok_ref[24 * o:24 * o + 24, j, at] = tok_grad[row:row + 24].astype(BF16)
    kernel_grad_middle(0)
    finish(xg.at[mine], xsem.at[0])
    finish(xg.at[pl.ds(0, 8)], xsem.at[5])
    finish(xg.at[pl.ds(0, 8)], xsem.at[4])
    for o in range(2):
        fifteen(gg.at[o], tsem.at[o, 1])
        fifteen(tg.at[o], tsem.at[o, 0])
        taken = gg[o].reshape(768, 128)
        for part in range(4):
            at = slice(part * 256, (part + 1) * 256)
            product = lax.dot_general(
                taken, xg[:, 48 * o:48 * o + 48, at].reshape(768, 256),
                (((0,), (0,)), ((), ())), preferred_element_type=F32,
            )
            if o == 0:
                dwt[:, at] = product
            else:
                dwk[at, :] = (dwt[:, at] + product).T
            if o == 1 and part % 2 == 1:
                half = part // 2
                for other in range(16):
                    dws[half, other] = jnp.concatenate(
                        [dwk[pl.ds(512 * half + other * 4 + r, 8, stride=64), :] for r in range(4)], axis=0
                    ).astype(BF16)
                for d in range(1, 16):
                    other, where = group_b(d)
                    send(dws.at[half, other], dwr.at[half, t], dwsem.at[half, 0], dwsem.at[half, 1], where)
                dwr[half, t] = dws[half, t]
    kernel_grad_third(0)
    kernel_grad_finish(1)
    for half in range(2):
        fifteen(dwr.at[half], dwsem.at[half, 1])
        fifteen(dws.at[half], dwsem.at[half, 0])
        fin[...] = sum16(dwr, half)
        for n in range(8):
            fins[8 * half + n, 0:4, :] = fin[pl.ds(n, 4, stride=8), :]
            fins[8 * half + n, 4:8, :] = jnp.zeros((4, 128), F32)
    for d in range(1, 16):
        other, where = group_a(d)
        send(fins.at[other], finr.at[mine], finsem.at[0], finsem.at[1], where)
    finr[mine] = fins[mine]
    kernel_grad_finish(0)
    fifteen(finr, finsem.at[1])
    fifteen(fins, finsem.at[0])
    for n in range(16):
        dw_ref[:, n * 128:(n + 1) * 128] = finr[n, 0:4, :]


def scratch():
    dma = pltpu.SemaphoreType.DMA
    vmem = pltpu.VMEM
    full = (TOTAL, 128)
    padded = (IMAGES * PADDED, 128)
    return [
        vmem(full, BF16), vmem((2, 1152, 128), BF16), dma((2,)),
        vmem((96, 1024), BF16), vmem((1024, 2048), BF16), dma((4,)),
        vmem(full, F32), vmem(full, F32), vmem(full, F32), vmem(full, BF16), vmem(full, BF16),
        vmem(full, F32), vmem(full, F32), vmem(full, F32), vmem((2, 128, 1152), BF16), vmem((IMAGES, CELLS, 1152), BF16),
        vmem(padded, F32), vmem(padded, F32), vmem(padded, F32),
        vmem((192, 128), F32), vmem((48, 128), F32), vmem((192, 128), F32), vmem((48, 128), F32),
        vmem((128, 128), F32), vmem((64, 128), F32),
        vmem((8, 3, 80, 128), BF16), vmem((8, 3, 80, 128), BF16),
        vmem((8, 64, 128), BF16), vmem((8, 3, 64, 128), BF16),
        vmem((8, 16, 128), BF16), vmem((8, 3, 16, 128), BF16),
        vmem((8, 32, 128), BF16), vmem((8, 4, 32, 128), BF16),
        vmem((8, 16, 128), BF16), vmem((8, 4, 16, 128), BF16),
        dma((8, 2)), dma((8, 2)), dma((8, 2)), dma((8, 4)), dma((8, 4)), dma((8, 4)), dma((8, 4)),
        vmem((6, 2, 32, 128), BF16), vmem((6, 2, 96, 128), BF16),
        vmem((6, 2, 32, 128), BF16), vmem((6, 2, 96, 128), BF16), vmem((6, 4, 32, 128), BF16),
        dma((6, 8)), dma((6, 8)),
        vmem((16, 96, 1024), BF16), dma((6,)),
        vmem((2, 16, 48, 128), BF16), vmem((2, 16, 48, 128), BF16), dma((2, 2)), vmem((128, 1024), F32),
        vmem((1024, 128), F32), vmem((2, 16, 32, 128), BF16), vmem((2, 16, 32, 128), BF16), dma((2, 2)),
        vmem((32, 128), F32), vmem((16, 8, 128), F32), vmem((16, 8, 128), F32), dma((2,)),
        vmem((16, 72, 128), F32), vmem((88, 128), F32), vmem((128, 1152), F32), vmem((2, 16, 80, 128), BF16), vmem((2, 16, 80, 128), BF16), dma((2, 2)),
        vmem((2, 16, 8, 128), F32), vmem((2, 16, 8, 128), F32), dma((2, 2)),
        vmem((2, 8, 128), F32), vmem((2, 16, 8, 128), F32), dma((2, 2)),
        vmem((2, 80, 128), BF16), vmem((2, 16, 80, 128), BF16), dma((2, 2)),
    ]


def results(dtok_ref, dw_ref, dk_ref, bias_ref, dtok_out, dw_out, dk_out, db_out, cb_out):
    dtok_out[...] = dtok_ref[...]
    dw_out[...] = dw_ref[...]
    dk_out[...] = dk_ref[...].astype(F32)
    db_out[...] = bias_ref[1:2, :]
    cb_out[0:1, :] = bias_ref[0:1, :]
    cb_out[1:2, :] = bias_ref[8:9, :]


def per_device(tokens, gout, deconv_weight, deconv_bias, conv_kernels, conv_biases):
    here = pl.BlockSpec(memory_space=pltpu.VMEM)
    anywhere = pl.BlockSpec(memory_space=pl.ANY)
    tok_grad, weight_grad, kernel_grads, biases = pl.pallas_call(
        kernel,
        out_shape=(
            jax.ShapeDtypeStruct((48, 2, 1024), BF16),
            jax.ShapeDtypeStruct((4, 2048), F32),
            jax.ShapeDtypeStruct((2, 1152, 128), BF16),
            jax.ShapeDtypeStruct((16, 128), F32),
        ),
        in_specs=[here, anywhere, anywhere, here, anywhere, here],
        out_specs=(here,) * 4,
        scratch_shapes=scratch(),
        compiler_params=pltpu.CompilerParams(
            collective_id=0, has_side_effects=True, vmem_limit_bytes=56 * 1024 * 1024
        ),
        name="triplane",
    )(
        tokens.reshape(48, 2, 1024), gout.reshape(TOTAL, 128), deconv_weight, deconv_bias.reshape(1, 128),
        conv_kernels, conv_biases.reshape(2, 1, 128),
    )
    tok_out, weight_out, kernel_out, bias_out, conv_bias_out = pl.pallas_call(
        results,
        out_shape=(
            jax.ShapeDtypeStruct((48, 2, 1024), BF16),
            jax.ShapeDtypeStruct((4, 2048), F32),
            jax.ShapeDtypeStruct((2, 1152, 128), F32),
            jax.ShapeDtypeStruct((1, 128), F32),
            jax.ShapeDtypeStruct((2, 128), F32),
        ),
        in_specs=[here] * 4,
        out_specs=(here,) * 5,
        name="results",
    )(tok_grad, weight_grad, kernel_grads, biases)
    return (tok_out.reshape(tokens.shape), weight_out, bias_out.reshape(128), kernel_out, conv_bias_out)


def solution(mesh):
    split = P("obj", None, "plane", "tile", None)
    return jax.shard_map(
        per_device,
        mesh=mesh,
        in_specs=(split, split, P(), P(), P(), P()),
        out_specs=(split, P(("obj", "plane", "tile"), None), P(), P(), P()),
        check_vma=False,
    )
```

```python
import jax
import jax.numpy as jnp
from jax import lax
from jax.experimental import pallas as pl
from jax.experimental.pallas import tpu as pltpu
from jax.sharding import PartitionSpec as P

MESH = pl.DeviceIdType.MESH
F32 = jnp.float32
BF16 = jnp.bfloat16
IMAGES = 6
ROWS = 32
COLS = 8
CELLS = ROWS * COLS
TOTAL = IMAGES * CELLS
PADDED = (ROWS + 2) * COLS
HALF = 3 * CELLS

HALO = (
    (-1, 0, ("row", 0), ("row", 1)),
    (1, 0, ("row", 1), ("row", 0)),
    (0, -1, ("col", 0), ("col", 1)),
    (0, 1, ("col", 1), ("col", 0)),
    (-1, -1, ("row", 0), ("corner", 3)),
    (-1, 1, ("row", 0), ("corner", 2)),
    (1, -1, ("row", 1), ("corner", 1)),
    (1, 1, ("row", 1), ("corner", 0)),
)


STEPS = [(m, n) for m in range(4) for n in range(4) if m or n]
FAR_A = sorted(STEPS, key=lambda s: -(3 * min(s[1], 4 - s[1]) + min(s[0], 1) * (3 if s[0] == 2 else 2)))
FAR_B = sorted(STEPS, key=lambda s: -(min(s[0], 4 - s[0]) + 2 * min(s[1], 4 - s[1])))


def both(first, second):
    return jnp.logical_and(first, second)


def kernel(
    tok_ref, g_hbm, w_hbm, db_ref, k_hbm, cb_ref,
    dtok_ref, dw_ref, dk_ref, bias_ref,
    g_ref, k_ref, insem, x_ref, w_ref, wsem, hid, pre0, pre1, act0, act1, grad, nat, dzed, kcat, col,
    centre, leftpad, rightpad, rowpart, colpart, rowband, colband,
    rowhalf, colzero,
    zs, zr, m1s, m1r, m2s, m2r, m3s, m3r, m4s, m4r,
    zsem, m1sem, m2sem, m3ss, m3rs, m4ss, m4rs,
    hsrow, hscol, hrrow, hrcol, hrcor, hss, hrs,
    xg, xsem, tg, gg, tsem, dwt, dwk, dws, dwr, dwsem, fin, fins, finr, finsem,
    dkf, dkacc, dka, dks, dkr, dksem, dkbs, dkbr, dkbsem, dkms, dkmr, dkmsem, dkcs, dkcr, dkcsem,
):
    obj, y, t = lax.axis_index("obj"), lax.axis_index("plane"), lax.axis_index("tile")
    x, z = t // 4, lax.rem(t, 4)
    mine = obj * 4 + y

    def group_a(d):
        step_obj, step_y = FAR_A[d - 1]
        there, row = lax.rem(obj + step_obj, 4), lax.rem(y + step_y, 4)
        return there * 4 + row, {"obj": there, "plane": row}

    def group_b(d):
        step_x, step_z = FAR_B[d - 1]
        other = lax.rem(x + step_x, 4) * 4 + lax.rem(z + step_z, 4)
        return other, {"tile": other}

    def send(src, dst, send_sem, recv_sem, where):
        copy = pltpu.make_async_remote_copy(
            src_ref=src, dst_ref=dst, send_sem=send_sem, recv_sem=recv_sem,
            device_id=where, device_id_type=MESH,
        )
        copy.start()

    def finish(ref, sem):
        pltpu.make_async_copy(ref, ref, sem).wait()

    def weight_part(part):
        at = slice(part * 512, (part + 1) * 512)
        return pltpu.make_async_copy(w_hbm.at[:, at], w_ref.at[:, at], wsem.at[part])

    arrivals = [
        pltpu.make_async_copy(src, dst, insem.at[n])
        for n, (src, dst) in enumerate(((g_hbm, g_ref), (k_hbm, k_ref)))
    ]
    for part in range(4):
        weight_part(part).start()
    arrivals[0].start()
    arrivals[1].start()
    hrrow[...] = jnp.zeros_like(hrrow)
    hrcol[...] = jnp.zeros_like(hrcol)
    hrcor[...] = jnp.zeros_like(hrcor)
    barrier = pltpu.get_barrier_semaphore()

    def greet(where):
        pl.semaphore_signal(barrier, inc=1, device_id=where, device_id_type=MESH)

    for d in range(1, 16):
        greet(group_a(d)[1])
        greet(group_b(d)[1])
    for dy in range(1, 4):
        for dx in range(1, 4):
            greet({"plane": lax.rem(y + dy, 4), "tile": lax.rem(x + dx, 4) * 4 + z})

    def inside(dy, dt):
        row_ok = both(y + dy >= 0, y + dy <= 3)
        return both(row_ok, both(t + dt >= 0, t + dt <= 15))

    diagonals = 0
    for dy, dt in ((-1, -1), (-1, 1), (1, -1), (1, 1)):
        ok = inside(dy, dt)

        @pl.when(ok)
        def _(dy=dy, dt=dt):
            greet({"plane": y + dy, "tile": t + dt})

        diagonals = diagonals + ok.astype(jnp.int32)

    for o in range(2):
        x_ref[48 * o:48 * o + 48, :] = jnp.concatenate(
            [tok_ref[24 * o:24 * o + 24, j, :].astype(F32) for j in range(2)], axis=0
        ).astype(BF16)
    xg[mine] = x_ref[...]
    for part in range(4):
        weight_part(part).wait()
        products = jnp.dot(
            x_ref[...], w_ref[:, part * 512:(part + 1) * 512], preferred_element_type=F32
        )
        for o in range(2):
            for j in range(2):
                for b in range(4):
                    at = pl.ds(o * HALF + part * 8 + 4 * j + b, 24, stride=32)
                    row = 48 * o + 24 * j
                    hid[at, :] = products[row:row + 24, b * 128:(b + 1) * 128] + db_ref[...]
    pl.semaphore_wait(barrier, 39 + diagonals)

    sources = {"row": hsrow, "col": hscol}
    targets = {"row": hrrow, "col": hrcol, "corner": hrcor}

    def halo_start(stage, o, ref):
        h = 2 * stage + o
        for side, at in ((0, 0), (1, CELLS - COLS)):
            edge = [ref[i * CELLS + at:i * CELLS + at + COLS, :] for i in range(3 * o, 3 * o + 3)]
            hsrow[h, side] = jnp.concatenate(edge + [jnp.zeros((8, 128), F32)], axis=0).astype(BF16)
        for side, at in ((0, 0), (1, COLS - 1)):
            hscol[h, side] = ref[pl.ds(o * HALF + at, 3 * ROWS, stride=COLS), :].astype(BF16)
        for n, (dy, dt, src, dst) in enumerate(HALO):

            @pl.when(inside(dy, dt))
            def _(n=n, dy=dy, dt=dt, src=src, dst=dst):
                send(
                    sources[src[0]].at[h, src[1]], targets[dst[0]].at[h, dst[1]],
                    hss.at[h, n], hrs.at[h, n], {"plane": y + dy, "tile": t + dt},
                )

    def halo_finish(stage, o, ref):
        h = 2 * stage + o
        for n, (dy, dt, src, dst) in enumerate(HALO):

            @pl.when(inside(-dy, -dt))
            def _(n=n, dst=dst):
                finish(targets[dst[0]].at[h, dst[1]], hrs.at[h, n])

            @pl.when(inside(dy, dt))
            def _(n=n, src=src):
                finish(sources[src[0]].at[h, src[1]], hss.at[h, n])

        top, bottom = hrrow[h, 0].astype(F32), hrrow[h, 1].astype(F32)
        left, right = hrcol[h, 0].astype(F32), hrcol[h, 1].astype(F32)
        corners = [hrcor[h, c].astype(F32) for c in range(4)]
        last = PADDED - COLS
        for p in range(3):
            i = 3 * o + p
            base = i * PADDED
            centre[base:base + COLS, :] = top[p * COLS:(p + 1) * COLS]
            centre[base + COLS:base + COLS + CELLS, :] = ref[i * CELLS:(i + 1) * CELLS, :]
            centre[base + last:base + PADDED, :] = bottom[p * COLS:(p + 1) * COLS]
            leftpad[pl.ds(base + COLS, ROWS, stride=COLS), :] = left[p * ROWS:(p + 1) * ROWS]
            rightpad[pl.ds(base + 2 * COLS - 1, ROWS, stride=COLS), :] = right[p * ROWS:(p + 1) * ROWS]
            first, final = p * COLS, (p + 1) * COLS - 1
            leftpad[base:base + 1, :] = corners[0][final:final + 1]
            leftpad[base + last:base + last + 1, :] = corners[2][final:final + 1]
            rightpad[base + COLS - 1:base + COLS, :] = corners[1][first:first + 1]
            rightpad[base + PADDED - 1:base + PADDED, :] = corners[3][first:first + 1]

    def shifted(i, flipped):
        base = pl.multiple_of(i * PADDED, 8)
        middle = centre[pl.ds(base, PADDED), :]
        place = lax.rem(lax.broadcasted_iota(jnp.int32, (PADDED, 128), 0), COLS)
        before = jnp.where(place == 0, leftpad[pl.ds(base, PADDED), :], pltpu.roll(middle, 1, 0))
        after = jnp.where(
            place == COLS - 1, rightpad[pl.ds(base, PADDED), :], pltpu.roll(middle, PADDED - 1, 0)
        )
        for tx, padded in enumerate((before, middle, after)):
            for ty in range(3):
                tap = (2 - ty) * 3 + (2 - tx) if flipped else ty * 3 + tx
                col[i, :, tap * 128:(tap + 1) * 128] = padded[ty * COLS:ty * COLS + CELLS].astype(BF16)

    same = x == y

    def pool_first(ph, o, ref):
        q = 2 * ph + o
        rows = ref[pl.ds(o * HALF, 3 * ROWS, stride=COLS), :]
        for v in range(1, COLS):
            rows = rows + ref[pl.ds(o * HALF + v, 3 * ROWS, stride=COLS), :]
        rowpart[o * 96:o * 96 + 96, :] = rows
        for i in range(3 * o, 3 * o + 3):
            colpart[i * COLS:(i + 1) * COLS, :] = jnp.sum(
                ref[i * CELLS:(i + 1) * CELLS, :].reshape(ROWS, COLS, 128), axis=0
            )
        common = jnp.concatenate([rows[0:64], colpart[24 * o:24 * o + 8, :]], axis=0)
        for d in range(1, 4):
            zd = lax.rem(z + d, 4)
            chunk = rowpart[pl.ds(pl.multiple_of(96 * o + 64 + 8 * zd, 8), 8), :]
            zs[q, d - 1] = jnp.concatenate([common, chunk], axis=0).astype(BF16)
            send(zs.at[q, d - 1], zr.at[q, d - 1], zsem.at[q, 0], zsem.at[q, 1], {"tile": x * 4 + zd})
        m2s[q] = colpart[24 * o + 8:24 * o + 24, :].astype(BF16)
        for d in range(1, 4):
            send(m2s.at[q], m2r.at[q, d - 1], m2sem.at[q, 0], m2sem.at[q, 1], {"plane": lax.rem(y + d, 4)})

    def pool_second(ph, o):
        q = 2 * ph + o
        finish(zr.at[q], zsem.at[q, 1])
        half = rowpart[o * 96:o * 96 + 64, :]
        two = rowpart[pl.ds(pl.multiple_of(96 * o + 64 + 8 * z, 8), 8), :]
        colzero[pl.ds(pl.multiple_of(32 * o + 8 * z, 8), 8), :] = colpart[24 * o:24 * o + 8, :]
        for d in range(1, 4):
            got = zr[q, d - 1].astype(F32)
            half = half + got[:64]
            two = two + got[72:80]
            source = lax.rem(z + 4 - d, 4)
            colzero[pl.ds(pl.multiple_of(32 * o + 8 * source, 8), 8), :] = got[64:72]
        rowhalf[o * 64:o * 64 + 64, :] = half
        m1s[q] = half.astype(BF16)
        m3s[q] = colzero[32 * o:32 * o + 32, :].astype(BF16)
        m4s[q] = jnp.concatenate([two, jnp.zeros((8, 128), F32)], axis=0).astype(BF16)
        for k in range(4):

            @pl.when(jnp.logical_not(both(same, x == k)))
            def _(k=k):
                send(m3s.at[q], m3r.at[q, y], m3ss.at[q, k], m3rs.at[q, y], {"plane": x, "tile": k * 4 + z})
                send(m4s.at[q], m4r.at[q, x], m4ss.at[q, k], m4rs.at[q, x], {"plane": k, "tile": y * 4 + z})

        for d in range(1, 4):
            send(m1s.at[q], m1r.at[q, d - 1], m1sem.at[q, 0], m1sem.at[q, 1], {"tile": lax.rem(x + d, 4) * 4 + z})

        @pl.when(same)
        def _():
            m3r[q, y] = m3s[q]
            m4r[q, x] = m4s[q]

    def pool_third(ph, o):
        q = 2 * ph + o
        finish(m2r.at[q], m2sem.at[q, 1])
        finish(m1r.at[q], m1sem.at[q, 1])
        for k in range(4):

            @pl.when(jnp.logical_not(both(same, x == k)))
            def _(k=k):
                finish(m3r.at[q, k], m3rs.at[q, k])
                finish(m4r.at[q, k], m4rs.at[q, k])
                finish(m3s.at[q], m3ss.at[q, k])
                finish(m4s.at[q], m4ss.at[q, k])

        finish(zs.at[q], zsem.at[q, 0])
        finish(m1r.at[q], m1sem.at[q, 0])
        finish(m2r.at[q], m2sem.at[q, 0])
        half = rowhalf[o * 64:o * 64 + 64, :]
        one = colpart[24 * o + 8:24 * o + 24, :]
        for d in range(3):
            half = half + m1r[q, d].astype(F32)
            one = one + m2r[q, d].astype(F32)
        zero = m3r[q, 0].astype(F32)
        two = m4r[q, 0].astype(F32)
        for k in range(1, 4):
            zero = zero + m3r[q, k].astype(F32)
            two = two + m4r[q, k].astype(F32)
        share = 1.0 / 128.0
        rowband[96 * o:96 * o + 32, :] = half[32:64] * share
        rowband[96 * o + 32:96 * o + 64, :] = half[0:32] * share
        rowband[96 * o + 64:96 * o + 96, :] = zero * share
        colband[24 * o:24 * o + 8, :] = two[0:8] * share
        colband[24 * o + 8:24 * o + 16, :] = one[8:16] * share
        colband[24 * o + 16:24 * o + 24, :] = one[0:8] * share

    def add_bands(dst, o, *srcs):
        for i in range(3 * o, 3 * o + 3):
            rb = rowband[i * ROWS:(i + 1) * ROWS, :]
            for v in range(COLS):
                at = pl.ds(i * CELLS + v, ROWS, stride=COLS)
                value = rb + colband[i * COLS + v:i * COLS + v + 1, :]
                for src in srcs:
                    value = value + src[at, :]
                dst[at, :] = value

    def per_image(o, body):
        def step(n, carry):
            i = n + 3 * o
            body(i, pl.ds(pl.multiple_of(i * CELLS, CELLS), CELLS))
            return carry

        lax.fori_loop(0, 3, step, 0)

    def silu0(i, at):
        value = pre0[at, :]
        rounded = (value * jax.nn.sigmoid(value)).astype(BF16)
        act0[at, :] = rounded
        nat[at, :] = rounded.astype(F32)

    def forward(i, at):
        shifted(i, False)
        out = jnp.dot(col[i], k_ref[0], preferred_element_type=F32)
        hid[at, :] = hid[at, :] + out + cb_ref[0]

    def act_grad(layer):
        def body(i, at):
            shifted(i, True)
            dzed[at, :] = lax.dot_general(
                col[i], kcat[layer], (((1,), (1,)), ((), ())), preferred_element_type=F32
            )

        return body

    def pre_grad1(i, at):
        value = pre1[at, :]
        s = jax.nn.sigmoid(value)
        act1[at, :] = (value * s).astype(BF16)
        dzed[at, :] = dzed[at, :] * s * (1.0 + value * (1.0 - s))

    def pre_grad0(i, at):
        value = pre0[at, :]
        s = jax.nn.sigmoid(value)
        dzed[at, :] = dzed[at, :] * s * (1.0 + value * (1.0 - s))

    def rounded(i, at):
        nat[at, :] = grad[at, :].astype(BF16).astype(F32)

    def kernel_grad(act):
        dka[...] = jnp.zeros_like(dka)

        def body(i, at):
            dka[...] += lax.dot_general(
                act[at, :], col[i], (((0,), (0,)), ((), ())), preferred_element_type=F32
            )

        for o in range(2):
            per_image(o, body)

    def total(ref):
        return jnp.sum(jnp.sum(ref[...].reshape(TOTAL // 8, 8, 128), axis=0), axis=0, keepdims=True)

    def kernel_grad_start(layer, extra):
        extras = jnp.concatenate(extra + [jnp.zeros((8 - len(extra), 128), F32)], axis=0)
        for g in range(16):
            rows = [dka[8 * g:8 * g + 8, tap * 128:(tap + 1) * 128] for tap in range(9)]
            dks[layer, g] = jnp.concatenate(rows + [extras], axis=0).astype(BF16)
        for d in range(1, 16):
            other, where = group_a(d)
            send(dks.at[layer, other], dkr.at[layer, mine], dksem.at[layer, 0], dksem.at[layer, 1], where)
        dkr[layer, mine] = dks[layer, mine]

    def fifteen(ref, sem):
        finish(ref.at[pl.ds(0, 15)], sem)

    def sum16(ref, layer):
        def step(n, acc):
            return acc + ref[layer, n].astype(F32)

        return lax.fori_loop(1, 16, step, ref[layer, 0].astype(F32))

    def kernel_grad_second(layer):
        fifteen(dkr.at[layer], dksem.at[layer, 1])
        fifteen(dks.at[layer], dksem.at[layer, 0])
        dkacc[0:80, :] = sum16(dkr, layer)
        dkacc[80:88, :] = jnp.zeros((8, 128), F32)
        for n in range(16):
            dkbs[layer, n] = dkacc[5 * n:5 * n + 8, :]
        for d in range(1, 16):
            other, where = group_b(d)
            send(dkbs.at[layer, other], dkbr.at[layer, t], dkbsem.at[layer, 0], dkbsem.at[layer, 1], where)
        dkbr[layer, t] = dkbs[layer, t]

    def kernel_grad_middle(layer):
        fifteen(dkbr.at[layer], dkbsem.at[layer, 1])
        fifteen(dkbr.at[layer], dkbsem.at[layer, 0])
        dkms[layer] = sum16(dkbr, layer)
        for d in range(1, 16):
            send(dkms.at[layer], dkmr.at[layer, t], dkmsem.at[layer, 0], dkmsem.at[layer, 1], group_b(d)[1])
        dkmr[layer, t] = dkms[layer]

    def kernel_grad_third(layer):
        fifteen(dkmr.at[layer], dkmsem.at[layer, 1])
        fifteen(dkmr.at[layer], dkmsem.at[layer, 0])
        for n in range(16):
            dkacc[5 * n:5 * n + 5, :] = dkmr[layer, n, 0:5, :]
        dkcs[layer] = dkacc[0:80, :].astype(BF16)
        for d in range(1, 16):
            send(dkcs.at[layer], dkcr.at[layer, mine], dkcsem.at[layer, 0], dkcsem.at[layer, 1], group_a(d)[1])
        dkcr[layer, mine] = dkcs[layer]

    def kernel_grad_finish(layer):
        fifteen(dkcr.at[layer], dkcsem.at[layer, 1])
        fifteen(dkcr.at[layer], dkcsem.at[layer, 0])
        for g in range(16):
            got = dkcr[layer, g].astype(F32)
            dkf[g] = got[:72]
            if g == 0:
                bias_ref[layer * 8:layer * 8 + 8, :] = got[72:80]
        for tap in range(9):
            dk_ref[layer, tap * 128:(tap + 1) * 128, :] = (
                dkf[:, 8 * tap:8 * tap + 8, :].reshape(128, 128).astype(BF16)
            )

    objects = range(2)
    theirs = lax.rem(obj + 2, 4) * 4 + y

    def to_planes(slot):
        for d in range(1, 4):
            send(xg.at[slot], xg.at[slot], xsem.at[2], xsem.at[3], {"plane": lax.rem(y + d, 4)})

    for o in objects:
        pool_first(0, o, hid)
    to_planes(mine)
    arrivals[0].wait()
    arrivals[1].wait()
    for l in range(2):
        for tap in range(9):
            kcat[l, :, tap * 128:(tap + 1) * 128] = k_ref[l, tap * 128:(tap + 1) * 128, :]
    grad[...] = g_ref[...].astype(F32)
    for o in objects:
        pool_second(0, o)
    partner = {"obj": lax.rem(obj + 2, 4)}
    send(xg.at[mine], xg.at[mine], xsem.at[0], xsem.at[1], partner)
    for o in objects:
        pool_third(0, o)
        add_bands(pre0, o, hid)
        per_image(o, silu0)
        halo_start(1, o, nat)
    for o in objects:
        halo_start(0, o, grad)
    for o in objects:
        halo_finish(1, o, nat)
        per_image(o, forward)
        pool_first(1, o, hid)
    finish(xg.at[mine], xsem.at[1])
    to_planes(theirs)
    halo_finish(0, 0, grad)
    per_image(0, act_grad(1))
    pool_second(1, 0)
    pool_second(1, 1)
    halo_finish(0, 1, grad)
    per_image(1, act_grad(1))
    for o in objects:
        pool_third(1, o)
        add_bands(pre1, o, hid)
        per_image(o, pre_grad1)
        pool_first(2, o, dzed)
    kernel_grad(act1)
    kernel_grad_start(1, [total(grad)])
    for o in objects:
        pool_second(2, o)
    for o in objects:
        pool_third(2, o)
        add_bands(grad, o, grad, dzed)
        per_image(o, rounded)
        halo_start(2, o, nat)
    finish(xg.at[pl.ds(0, 6)], xsem.at[3])
    finish(xg.at[pl.ds(0, 6)], xsem.at[2])
    sibling = {"obj": obj + 1 - 2 * lax.rem(obj, 2)}
    core = lax.rem(obj, 2)
    for half in range(2):
        held = xg.at[pl.ds(pl.multiple_of((core + 2 * half) * 4, 4), 4)]
        send(held, held, xsem.at[4], xsem.at[5], sibling)
    kernel_grad_second(1)
    sum_grad = total(grad)
    for o in objects:
        halo_finish(2, o, nat)
        per_image(o, act_grad(0))
        per_image(o, pre_grad0)
        pool_first(3, o, dzed)
    kernel_grad(act0)
    kernel_grad_start(0, [sum_grad, sum_grad + 3.0 * total(dzed)])
    for o in objects:
        pool_second(3, o)
    kernel_grad_middle(1)

    def send_taps(o):
        for a in range(4):
            for b in range(4):
                tg[o, a * 4 + b] = jnp.concatenate(
                    [grad[pl.ds(o * HALF + a * 8 + 4 * j + b, 24, stride=32), :] for j in range(2)], axis=0
                ).astype(BF16)
        for d in range(1, 16):
            other, where = group_a(d)
            send(tg.at[o, other], gg.at[o, mine], tsem.at[o, 0], tsem.at[o, 1], where)
        gg[o, mine] = tg[o, mine]

    pool_third(3, 0)
    add_bands(grad, 0, grad, dzed)
    send_taps(0)
    kernel_grad_second(0)
    pool_third(3, 1)
    add_bands(grad, 1, grad, dzed)
    send_taps(1)
    kernel_grad_third(1)
    kernel_grad_middle(0)
    finish(xg.at[mine], xsem.at[0])
    finish(xg.at[pl.ds(0, 8)], xsem.at[5])
    finish(xg.at[pl.ds(0, 8)], xsem.at[4])
    for o in range(2):
        fifteen(gg.at[o], tsem.at[o, 1])
        fifteen(tg.at[o], tsem.at[o, 0])
        taken = gg[o].reshape(768, 128)
        for part in range(4):
            at = slice(part * 256, (part + 1) * 256)
            product = lax.dot_general(
                taken, xg[:, 48 * o:48 * o + 48, at].reshape(768, 256),
                (((0,), (0,)), ((), ())), preferred_element_type=F32,
            )
            if o == 0:
                dwt[:, at] = product
            else:
                dwk[at, :] = (dwt[:, at] + product).T
            if o == 1 and part % 2 == 1:
                half = part // 2
                for other in range(16):
                    dws[half, other] = jnp.concatenate(
                        [dwk[pl.ds(512 * half + other * 4 + r, 8, stride=64), :] for r in range(4)], axis=0
                    ).astype(BF16)
                for d in range(1, 16):
                    other, where = group_b(d)
                    send(dws.at[half, other], dwr.at[half, t], dwsem.at[half, 0], dwsem.at[half, 1], where)
                dwr[half, t] = dws[half, t]
    taps = jnp.concatenate([tg[:, n].reshape(96, 128) for n in range(16)], axis=1)
    for part in range(4):
        at = slice(part * 256, (part + 1) * 256)
        tok_grad = lax.dot_general(
            taps, w_ref[at, :], (((1,), (1,)), ((), ())), preferred_element_type=F32
        )
        for o in range(2):
            for j in range(2):
                row = 48 * o + 24 * j
                dtok_ref[24 * o:24 * o + 24, j, at] = tok_grad[row:row + 24].astype(BF16)
    kernel_grad_third(0)
    kernel_grad_finish(1)
    for half in range(2):
        fifteen(dwr.at[half], dwsem.at[half, 1])
        fifteen(dws.at[half], dwsem.at[half, 0])
        fin[...] = sum16(dwr, half)
        for n in range(8):
            fins[8 * half + n, 0:4, :] = fin[pl.ds(n, 4, stride=8), :]
            fins[8 * half + n, 4:8, :] = jnp.zeros((4, 128), F32)
    for d in range(1, 16):
        other, where = group_a(d)
        send(fins.at[other], finr.at[mine], finsem.at[0], finsem.at[1], where)
    finr[mine] = fins[mine]
    kernel_grad_finish(0)
    fifteen(finr, finsem.at[1])
    fifteen(fins, finsem.at[0])
    for n in range(16):
        dw_ref[:, n * 128:(n + 1) * 128] = finr[n, 0:4, :]


def scratch():
    dma = pltpu.SemaphoreType.DMA
    vmem = pltpu.VMEM
    full = (TOTAL, 128)
    padded = (IMAGES * PADDED, 128)
    return [
        vmem(full, BF16), vmem((2, 1152, 128), BF16), dma((2,)),
        vmem((96, 1024), BF16), vmem((1024, 2048), BF16), dma((4,)),
        vmem(full, F32), vmem(full, F32), vmem(full, F32), vmem(full, BF16), vmem(full, BF16),
        vmem(full, F32), vmem(full, F32), vmem(full, F32), vmem((2, 128, 1152), BF16), vmem((IMAGES, CELLS, 1152), BF16),
        vmem(padded, F32), vmem(padded, F32), vmem(padded, F32),
        vmem((192, 128), F32), vmem((48, 128), F32), vmem((192, 128), F32), vmem((48, 128), F32),
        vmem((128, 128), F32), vmem((64, 128), F32),
        vmem((8, 3, 80, 128), BF16), vmem((8, 3, 80, 128), BF16),
        vmem((8, 64, 128), BF16), vmem((8, 3, 64, 128), BF16),
        vmem((8, 16, 128), BF16), vmem((8, 3, 16, 128), BF16),
        vmem((8, 32, 128), BF16), vmem((8, 4, 32, 128), BF16),
        vmem((8, 16, 128), BF16), vmem((8, 4, 16, 128), BF16),
        dma((8, 2)), dma((8, 2)), dma((8, 2)), dma((8, 4)), dma((8, 4)), dma((8, 4)), dma((8, 4)),
        vmem((6, 2, 32, 128), BF16), vmem((6, 2, 96, 128), BF16),
        vmem((6, 2, 32, 128), BF16), vmem((6, 2, 96, 128), BF16), vmem((6, 4, 32, 128), BF16),
        dma((6, 8)), dma((6, 8)),
        vmem((16, 96, 1024), BF16), dma((6,)),
        vmem((2, 16, 48, 128), BF16), vmem((2, 16, 48, 128), BF16), dma((2, 2)), vmem((128, 1024), F32),
        vmem((1024, 128), F32), vmem((2, 16, 32, 128), BF16), vmem((2, 16, 32, 128), BF16), dma((2, 2)),
        vmem((32, 128), F32), vmem((16, 8, 128), F32), vmem((16, 8, 128), F32), dma((2,)),
        vmem((16, 72, 128), F32), vmem((88, 128), F32), vmem((128, 1152), F32), vmem((2, 16, 80, 128), BF16), vmem((2, 16, 80, 128), BF16), dma((2, 2)),
        vmem((2, 16, 8, 128), F32), vmem((2, 16, 8, 128), F32), dma((2, 2)),
        vmem((2, 8, 128), F32), vmem((2, 16, 8, 128), F32), dma((2, 2)),
        vmem((2, 80, 128), BF16), vmem((2, 16, 80, 128), BF16), dma((2, 2)),
    ]


def results(dtok_ref, dw_ref, dk_ref, bias_ref, dtok_out, dw_out, dk_out, db_out, cb_out):
    dtok_out[...] = dtok_ref[...]
    dw_out[...] = dw_ref[...]
    dk_out[...] = dk_ref[...].astype(F32)
    db_out[...] = bias_ref[1:2, :]
    cb_out[0:1, :] = bias_ref[0:1, :]
    cb_out[1:2, :] = bias_ref[8:9, :]


def per_device(tokens, gout, deconv_weight, deconv_bias, conv_kernels, conv_biases):
    here = pl.BlockSpec(memory_space=pltpu.VMEM)
    anywhere = pl.BlockSpec(memory_space=pl.ANY)
    tok_grad, weight_grad, kernel_grads, biases = pl.pallas_call(
        kernel,
        out_shape=(
            jax.ShapeDtypeStruct((48, 2, 1024), BF16),
            jax.ShapeDtypeStruct((4, 2048), F32),
            jax.ShapeDtypeStruct((2, 1152, 128), BF16),
            jax.ShapeDtypeStruct((16, 128), F32),
        ),
        in_specs=[here, anywhere, anywhere, here, anywhere, here],
        out_specs=(here,) * 4,
        scratch_shapes=scratch(),
        compiler_params=pltpu.CompilerParams(
            collective_id=0, has_side_effects=True, vmem_limit_bytes=56 * 1024 * 1024
        ),
        name="triplane",
    )(
        tokens.reshape(48, 2, 1024), gout.reshape(TOTAL, 128), deconv_weight, deconv_bias.reshape(1, 128),
        conv_kernels, conv_biases.reshape(2, 1, 128),
    )
    tok_out, weight_out, kernel_out, bias_out, conv_bias_out = pl.pallas_call(
        results,
        out_shape=(
            jax.ShapeDtypeStruct((48, 2, 1024), BF16),
            jax.ShapeDtypeStruct((4, 2048), F32),
            jax.ShapeDtypeStruct((2, 1152, 128), F32),
            jax.ShapeDtypeStruct((1, 128), F32),
            jax.ShapeDtypeStruct((2, 128), F32),
        ),
        in_specs=[here] * 4,
        out_specs=(here,) * 5,
        name="results",
    )(tok_grad, weight_grad, kernel_grads, biases)
    return (tok_out.reshape(tokens.shape), weight_out, bias_out.reshape(128), kernel_out, conv_bias_out)


def solution(mesh):
    split = P("obj", None, "plane", "tile", None)
    return jax.shard_map(
        per_device,
        mesh=mesh,
        in_specs=(split, split, P(), P(), P(), P()),
        out_specs=(split, P(("obj", "plane", "tile"), None), P(), P(), P()),
        check_vma=False,
    )
```

```python
import jax
import jax.numpy as jnp
from jax import lax
from jax.experimental import pallas as pl
from jax.experimental.pallas import tpu as pltpu
from jax.sharding import PartitionSpec as P

MESH = pl.DeviceIdType.MESH
F32 = jnp.float32
BF16 = jnp.bfloat16
IMAGES = 6
ROWS = 32
COLS = 8
CELLS = ROWS * COLS
TOTAL = IMAGES * CELLS
PADDED = (ROWS + 2) * COLS
HALF = 3 * CELLS

HALO = (
    (-1, -1, ("row", 0), ("corner", 3)),
    (-1, 1, ("row", 0), ("corner", 2)),
    (1, -1, ("row", 1), ("corner", 1)),
    (1, 1, ("row", 1), ("corner", 0)),
    (0, -1, ("col", 0), ("col", 1)),
    (0, 1, ("col", 1), ("col", 0)),
    (-1, 0, ("row", 0), ("row", 1)),
    (1, 0, ("row", 1), ("row", 0)),
)


STEPS = [(m, n) for m in range(4) for n in range(4) if m or n]
FAR_A = sorted(STEPS, key=lambda s: -(3 * min(s[1], 4 - s[1]) + min(s[0], 1) * (3 if s[0] == 2 else 2)))
FAR_B = sorted(STEPS, key=lambda s: -(min(s[0], 4 - s[0]) + 2 * min(s[1], 4 - s[1])))


def both(first, second):
    return jnp.logical_and(first, second)


def kernel(
    tok_ref, g_hbm, w_hbm, db_ref, k_hbm, cb_ref,
    dtok_ref, dw_ref, dk_ref, bias_ref,
    g_ref, k_ref, insem, x_ref, w_ref, wsem, hid, pre0, pre1, act0, act1, grad, nat, dzed, kcat, col,
    centre, leftpad, rightpad, rowpart, colpart, rowband, colband,
    rowhalf, colzero,
    zs, zr, m1s, m1r, m2s, m2r, m3s, m3r, m4s, m4r,
    zsem, m1sem, m2sem, m3ss, m3rs, m4ss, m4rs,
    hsrow, hscol, hrrow, hrcol, hrcor, hss, hrs,
    xg, xsem, tg, gg, tsem, dwt, dwk, dws, dwr, dwsem, fin, fins, finr, finsem,
    dkf, dkacc, dka, dks, dkr, dksem, dkbs, dkbr, dkbsem, dkms, dkmr, dkmsem, dkcs, dkcr, dkcsem,
):
    obj, y, t = lax.axis_index("obj"), lax.axis_index("plane"), lax.axis_index("tile")
    x, z = t // 4, lax.rem(t, 4)
    mine = obj * 4 + y

    def group_a(d):
        step_obj, step_y = FAR_A[d - 1]
        there, row = lax.rem(obj + step_obj, 4), lax.rem(y + step_y, 4)
        return there * 4 + row, {"obj": there, "plane": row}

    def group_b(d):
        step_x, step_z = FAR_B[d - 1]
        other = lax.rem(x + step_x, 4) * 4 + lax.rem(z + step_z, 4)
        return other, {"tile": other}

    def send(src, dst, send_sem, recv_sem, where):
        copy = pltpu.make_async_remote_copy(
            src_ref=src, dst_ref=dst, send_sem=send_sem, recv_sem=recv_sem,
            device_id=where, device_id_type=MESH,
        )
        copy.start()

    def finish(ref, sem):
        pltpu.make_async_copy(ref, ref, sem).wait()

    def weight_part(part):
        at = slice(part * 512, (part + 1) * 512)
        return pltpu.make_async_copy(w_hbm.at[:, at], w_ref.at[:, at], wsem.at[part])

    arrivals = [
        pltpu.make_async_copy(src, dst, insem.at[n])
        for n, (src, dst) in enumerate(((g_hbm, g_ref), (k_hbm, k_ref)))
    ]
    for part in range(4):
        weight_part(part).start()
    arrivals[0].start()
    arrivals[1].start()
    hrrow[...] = jnp.zeros_like(hrrow)
    hrcol[...] = jnp.zeros_like(hrcol)
    hrcor[...] = jnp.zeros_like(hrcor)
    barrier = pltpu.get_barrier_semaphore()

    def greet(where):
        pl.semaphore_signal(barrier, inc=1, device_id=where, device_id_type=MESH)

    for d in range(1, 16):
        greet(group_a(d)[1])
        greet(group_b(d)[1])
    for dy in range(1, 4):
        for dx in range(1, 4):
            greet({"plane": lax.rem(y + dy, 4), "tile": lax.rem(x + dx, 4) * 4 + z})

    def inside(dy, dt):
        row_ok = both(y + dy >= 0, y + dy <= 3)
        return both(row_ok, both(t + dt >= 0, t + dt <= 15))

    diagonals = 0
    for dy, dt in ((-1, -1), (-1, 1), (1, -1), (1, 1)):
        ok = inside(dy, dt)

        @pl.when(ok)
        def _(dy=dy, dt=dt):
            greet({"plane": y + dy, "tile": t + dt})

        diagonals = diagonals + ok.astype(jnp.int32)

    for o in range(2):
        x_ref[48 * o:48 * o + 48, :] = jnp.concatenate(
            [tok_ref[24 * o:24 * o + 24, j, :].astype(F32) for j in range(2)], axis=0
        ).astype(BF16)
    xg[mine] = x_ref[...]
    for part in range(4):
        weight_part(part).wait()
        products = jnp.dot(
            x_ref[...], w_ref[:, part * 512:(part + 1) * 512], preferred_element_type=F32
        )
        for o in range(2):
            for j in range(2):
                for b in range(4):
                    at = pl.ds(o * HALF + part * 8 + 4 * j + b, 24, stride=32)
                    row = 48 * o + 24 * j
                    hid[at, :] = products[row:row + 24, b * 128:(b + 1) * 128] + db_ref[...]
    pl.semaphore_wait(barrier, 39 + diagonals)

    sources = {"row": hsrow, "col": hscol}
    targets = {"row": hrrow, "col": hrcol, "corner": hrcor}

    def halo_start(stage, o, ref):
        h = 2 * stage + o
        for side, at in ((0, 0), (1, CELLS - COLS)):
            edge = [ref[i * CELLS + at:i * CELLS + at + COLS, :] for i in range(3 * o, 3 * o + 3)]
            hsrow[h, side] = jnp.concatenate(edge + [jnp.zeros((8, 128), F32)], axis=0).astype(BF16)
        for side, at in ((0, 0), (1, COLS - 1)):
            hscol[h, side] = ref[pl.ds(o * HALF + at, 3 * ROWS, stride=COLS), :].astype(BF16)
        for n, (dy, dt, src, dst) in enumerate(HALO):

            @pl.when(inside(dy, dt))
            def _(n=n, dy=dy, dt=dt, src=src, dst=dst):
                send(
                    sources[src[0]].at[h, src[1]], targets[dst[0]].at[h, dst[1]],
                    hss.at[h, n], hrs.at[h, n], {"plane": y + dy, "tile": t + dt},
                )

    def halo_finish(stage, o, ref):
        h = 2 * stage + o
        for n, (dy, dt, src, dst) in enumerate(HALO):

            @pl.when(inside(-dy, -dt))
            def _(n=n, dst=dst):
                finish(targets[dst[0]].at[h, dst[1]], hrs.at[h, n])

            @pl.when(inside(dy, dt))
            def _(n=n, src=src):
                finish(sources[src[0]].at[h, src[1]], hss.at[h, n])

        top, bottom = hrrow[h, 0].astype(F32), hrrow[h, 1].astype(F32)
        left, right = hrcol[h, 0].astype(F32), hrcol[h, 1].astype(F32)
        corners = [hrcor[h, c].astype(F32) for c in range(4)]
        last = PADDED - COLS
        for p in range(3):
            i = 3 * o + p
            base = i * PADDED
            centre[base:base + COLS, :] = top[p * COLS:(p + 1) * COLS]
            centre[base + COLS:base + COLS + CELLS, :] = ref[i * CELLS:(i + 1) * CELLS, :]
            centre[base + last:base + PADDED, :] = bottom[p * COLS:(p + 1) * COLS]
            leftpad[pl.ds(base + COLS, ROWS, stride=COLS), :] = left[p * ROWS:(p + 1) * ROWS]
            rightpad[pl.ds(base + 2 * COLS - 1, ROWS, stride=COLS), :] = right[p * ROWS:(p + 1) * ROWS]
            first, final = p * COLS, (p + 1) * COLS - 1
            leftpad[base:base + 1, :] = corners[0][final:final + 1]
            leftpad[base + last:base + last + 1, :] = corners[2][final:final + 1]
            rightpad[base + COLS - 1:base + COLS, :] = corners[1][first:first + 1]
            rightpad[base + PADDED - 1:base + PADDED, :] = corners[3][first:first + 1]

    def shifted(i, flipped):
        base = pl.multiple_of(i * PADDED, 8)
        middle = centre[pl.ds(base, PADDED), :]
        place = lax.rem(lax.broadcasted_iota(jnp.int32, (PADDED, 128), 0), COLS)
        before = jnp.where(place == 0, leftpad[pl.ds(base, PADDED), :], pltpu.roll(middle, 1, 0))
        after = jnp.where(
            place == COLS - 1, rightpad[pl.ds(base, PADDED), :], pltpu.roll(middle, PADDED - 1, 0)
        )
        for tx, padded in enumerate((before, middle, after)):
            for ty in range(3):
                tap = (2 - ty) * 3 + (2 - tx) if flipped else ty * 3 + tx
                col[i, :, tap * 128:(tap + 1) * 128] = padded[ty * COLS:ty * COLS + CELLS].astype(BF16)

    same = x == y

    def pool_first(ph, o, ref):
        q = 2 * ph + o
        rows = ref[pl.ds(o * HALF, 3 * ROWS, stride=COLS), :]
        for v in range(1, COLS):
            rows = rows + ref[pl.ds(o * HALF + v, 3 * ROWS, stride=COLS), :]
        rowpart[o * 96:o * 96 + 96, :] = rows
        for i in range(3 * o, 3 * o + 3):
            colpart[i * COLS:(i + 1) * COLS, :] = jnp.sum(
                ref[i * CELLS:(i + 1) * CELLS, :].reshape(ROWS, COLS, 128), axis=0
            )
        common = jnp.concatenate([rows[0:64], colpart[24 * o:24 * o + 8, :]], axis=0)
        for d in (2, 1, 3):
            zd = lax.rem(z + d, 4)
            chunk = rowpart[pl.ds(pl.multiple_of(96 * o + 64 + 8 * zd, 8), 8), :]
            zs[q, d - 1] = jnp.concatenate([common, chunk], axis=0).astype(BF16)
            send(zs.at[q, d - 1], zr.at[q, d - 1], zsem.at[q, 0], zsem.at[q, 1], {"tile": x * 4 + zd})
        m2s[q] = colpart[24 * o + 8:24 * o + 24, :].astype(BF16)
        for d in (2, 1, 3):
            send(m2s.at[q], m2r.at[q, d - 1], m2sem.at[q, 0], m2sem.at[q, 1], {"plane": lax.rem(y + d, 4)})

    def pool_second(ph, o):
        q = 2 * ph + o
        finish(zr.at[q], zsem.at[q, 1])
        half = rowpart[o * 96:o * 96 + 64, :]
        two = rowpart[pl.ds(pl.multiple_of(96 * o + 64 + 8 * z, 8), 8), :]
        colzero[pl.ds(pl.multiple_of(32 * o + 8 * z, 8), 8), :] = colpart[24 * o:24 * o + 8, :]
        for d in range(1, 4):
            got = zr[q, d - 1].astype(F32)
            half = half + got[:64]
            two = two + got[72:80]
            source = lax.rem(z + 4 - d, 4)
            colzero[pl.ds(pl.multiple_of(32 * o + 8 * source, 8), 8), :] = got[64:72]
        rowhalf[o * 64:o * 64 + 64, :] = half
        m1s[q] = half.astype(BF16)
        m3s[q] = colzero[32 * o:32 * o + 32, :].astype(BF16)
        m4s[q] = jnp.concatenate([two, jnp.zeros((8, 128), F32)], axis=0).astype(BF16)
        for k in range(4):

            @pl.when(jnp.logical_not(both(same, x == k)))
            def _(k=k):
                send(m3s.at[q], m3r.at[q, y], m3ss.at[q, k], m3rs.at[q, y], {"plane": x, "tile": k * 4 + z})
                send(m4s.at[q], m4r.at[q, x], m4ss.at[q, k], m4rs.at[q, x], {"plane": k, "tile": y * 4 + z})

        for d in (2, 1, 3):
            send(m1s.at[q], m1r.at[q, d - 1], m1sem.at[q, 0], m1sem.at[q, 1], {"tile": lax.rem(x + d, 4) * 4 + z})

        @pl.when(same)
        def _():
            m3r[q, y] = m3s[q]
            m4r[q, x] = m4s[q]

    def pool_third(ph, o):
        q = 2 * ph + o
        finish(m2r.at[q], m2sem.at[q, 1])
        finish(m1r.at[q], m1sem.at[q, 1])
        for k in range(4):

            @pl.when(jnp.logical_not(both(same, x == k)))
            def _(k=k):
                finish(m3r.at[q, k], m3rs.at[q, k])
                finish(m4r.at[q, k], m4rs.at[q, k])
                finish(m3s.at[q], m3ss.at[q, k])
                finish(m4s.at[q], m4ss.at[q, k])

        finish(zs.at[q], zsem.at[q, 0])
        finish(m1r.at[q], m1sem.at[q, 0])
        finish(m2r.at[q], m2sem.at[q, 0])
        half = rowhalf[o * 64:o * 64 + 64, :]
        one = colpart[24 * o + 8:24 * o + 24, :]
        for d in range(3):
            half = half + m1r[q, d].astype(F32)
            one = one + m2r[q, d].astype(F32)
        zero = m3r[q, 0].astype(F32)
        two = m4r[q, 0].astype(F32)
        for k in range(1, 4):
            zero = zero + m3r[q, k].astype(F32)
            two = two + m4r[q, k].astype(F32)
        share = 1.0 / 128.0
        rowband[96 * o:96 * o + 32, :] = half[32:64] * share
        rowband[96 * o + 32:96 * o + 64, :] = half[0:32] * share
        rowband[96 * o + 64:96 * o + 96, :] = zero * share
        colband[24 * o:24 * o + 8, :] = two[0:8] * share
        colband[24 * o + 8:24 * o + 16, :] = one[8:16] * share
        colband[24 * o + 16:24 * o + 24, :] = one[0:8] * share

    def add_bands(dst, o, *srcs):
        for i in range(3 * o, 3 * o + 3):
            rb = rowband[i * ROWS:(i + 1) * ROWS, :]
            for v in range(COLS):
                at = pl.ds(i * CELLS + v, ROWS, stride=COLS)
                value = rb + colband[i * COLS + v:i * COLS + v + 1, :]
                for src in srcs:
                    value = value + src[at, :]
                dst[at, :] = value

    def per_image(o, body):
        def step(n, carry):
            i = n + 3 * o
            body(i, pl.ds(pl.multiple_of(i * CELLS, CELLS), CELLS))
            return carry

        lax.fori_loop(0, 3, step, 0)

    def silu0(i, at):
        value = pre0[at, :]
        rounded = (value * jax.nn.sigmoid(value)).astype(BF16)
        act0[at, :] = rounded
        nat[at, :] = rounded.astype(F32)

    def forward(i, at):
        shifted(i, False)
        out = jnp.dot(col[i], k_ref[0], preferred_element_type=F32)
        hid[at, :] = hid[at, :] + out + cb_ref[0]

    def act_grad(layer):
        def body(i, at):
            shifted(i, True)
            dzed[at, :] = lax.dot_general(
                col[i], kcat[layer], (((1,), (1,)), ((), ())), preferred_element_type=F32
            )

        return body

    def pre_grad1(i, at):
        value = pre1[at, :]
        s = jax.nn.sigmoid(value)
        act1[at, :] = (value * s).astype(BF16)
        dzed[at, :] = dzed[at, :] * s * (1.0 + value * (1.0 - s))

    def pre_grad0(i, at):
        value = pre0[at, :]
        s = jax.nn.sigmoid(value)
        dzed[at, :] = dzed[at, :] * s * (1.0 + value * (1.0 - s))

    def rounded(i, at):
        nat[at, :] = grad[at, :].astype(BF16).astype(F32)

    def kernel_grad(act):
        dka[...] = jnp.zeros_like(dka)

        def body(i, at):
            dka[...] += lax.dot_general(
                act[at, :], col[i], (((0,), (0,)), ((), ())), preferred_element_type=F32
            )

        for o in range(2):
            per_image(o, body)

    def total(ref):
        return jnp.sum(jnp.sum(ref[...].reshape(TOTAL // 8, 8, 128), axis=0), axis=0, keepdims=True)

    def kernel_grad_start(layer, extra):
        extras = jnp.concatenate(extra + [jnp.zeros((8 - len(extra), 128), F32)], axis=0)
        for g in range(16):
            rows = [dka[8 * g:8 * g + 8, tap * 128:(tap + 1) * 128] for tap in range(9)]
            dks[layer, g] = jnp.concatenate(rows + [extras], axis=0).astype(BF16)
        for d in range(1, 16):
            other, where = group_a(d)
            send(dks.at[layer, other], dkr.at[layer, mine], dksem.at[layer, 0], dksem.at[layer, 1], where)
        dkr[layer, mine] = dks[layer, mine]

    def fifteen(ref, sem):
        finish(ref.at[pl.ds(0, 15)], sem)

    def sum16(ref, layer):
        def step(n, acc):
            return acc + ref[layer, n].astype(F32)

        return lax.fori_loop(1, 16, step, ref[layer, 0].astype(F32))

    def kernel_grad_second(layer):
        fifteen(dkr.at[layer], dksem.at[layer, 1])
        fifteen(dks.at[layer], dksem.at[layer, 0])
        dkacc[0:80, :] = sum16(dkr, layer)
        dkacc[80:88, :] = jnp.zeros((8, 128), F32)
        for n in range(16):
            dkbs[layer, n] = dkacc[5 * n:5 * n + 8, :]
        for d in range(1, 16):
            other, where = group_b(d)
            send(dkbs.at[layer, other], dkbr.at[layer, t], dkbsem.at[layer, 0], dkbsem.at[layer, 1], where)
        dkbr[layer, t] = dkbs[layer, t]

    def kernel_grad_middle(layer):
        fifteen(dkbr.at[layer], dkbsem.at[layer, 1])
        fifteen(dkbr.at[layer], dkbsem.at[layer, 0])
        dkms[layer] = sum16(dkbr, layer)
        for d in range(1, 16):
            send(dkms.at[layer], dkmr.at[layer, t], dkmsem.at[layer, 0], dkmsem.at[layer, 1], group_b(d)[1])
        dkmr[layer, t] = dkms[layer]

    def kernel_grad_third(layer):
        fifteen(dkmr.at[layer], dkmsem.at[layer, 1])
        fifteen(dkmr.at[layer], dkmsem.at[layer, 0])
        for n in range(16):
            dkacc[5 * n:5 * n + 5, :] = dkmr[layer, n, 0:5, :]
        dkcs[layer] = dkacc[0:80, :].astype(BF16)
        for d in range(1, 16):
            send(dkcs.at[layer], dkcr.at[layer, mine], dkcsem.at[layer, 0], dkcsem.at[layer, 1], group_a(d)[1])
        dkcr[layer, mine] = dkcs[layer]

    def kernel_grad_finish(layer):
        fifteen(dkcr.at[layer], dkcsem.at[layer, 1])
        fifteen(dkcr.at[layer], dkcsem.at[layer, 0])
        for g in range(16):
            got = dkcr[layer, g].astype(F32)
            dkf[g] = got[:72]
            if g == 0:
                bias_ref[layer * 8:layer * 8 + 8, :] = got[72:80]
        for tap in range(9):
            dk_ref[layer, tap * 128:(tap + 1) * 128, :] = (
                dkf[:, 8 * tap:8 * tap + 8, :].reshape(128, 128).astype(BF16)
            )

    objects = range(2)
    theirs = lax.rem(obj + 2, 4) * 4 + y

    def to_planes(slot):
        for d in range(1, 4):
            send(xg.at[slot], xg.at[slot], xsem.at[2], xsem.at[3], {"plane": lax.rem(y + d, 4)})

    for o in objects:
        pool_first(0, o, hid)
    to_planes(mine)
    arrivals[0].wait()
    arrivals[1].wait()
    for l in range(2):
        for tap in range(9):
            kcat[l, :, tap * 128:(tap + 1) * 128] = k_ref[l, tap * 128:(tap + 1) * 128, :]
    grad[...] = g_ref[...].astype(F32)
    for o in objects:
        pool_second(0, o)
    partner = {"obj": lax.rem(obj + 2, 4)}
    send(xg.at[mine], xg.at[mine], xsem.at[0], xsem.at[1], partner)
    for o in objects:
        pool_third(0, o)
        add_bands(pre0, o, hid)
        per_image(o, silu0)
        halo_start(1, o, nat)
    for o in objects:
        halo_start(0, o, grad)
    for o in objects:
        halo_finish(1, o, nat)
        per_image(o, forward)
        pool_first(1, o, hid)
    finish(xg.at[mine], xsem.at[1])
    to_planes(theirs)
    halo_finish(0, 0, grad)
    per_image(0, act_grad(1))
    pool_second(1, 0)
    pool_second(1, 1)
    halo_finish(0, 1, grad)
    per_image(1, act_grad(1))
    for o in objects:
        pool_third(1, o)
        add_bands(pre1, o, hid)
        per_image(o, pre_grad1)
        pool_first(2, o, dzed)
    kernel_grad(act1)
    kernel_grad_start(1, [total(grad)])
    for o in objects:
        pool_second(2, o)
    for o in objects:
        pool_third(2, o)
        add_bands(grad, o, grad, dzed)
        per_image(o, rounded)
        halo_start(2, o, nat)
    finish(xg.at[pl.ds(0, 6)], xsem.at[3])
    finish(xg.at[pl.ds(0, 6)], xsem.at[2])
    sibling = {"obj": obj + 1 - 2 * lax.rem(obj, 2)}
    core = lax.rem(obj, 2)
    for half in range(2):
        held = xg.at[pl.ds(pl.multiple_of((core + 2 * half) * 4, 4), 4)]
        send(held, held, xsem.at[4], xsem.at[5], sibling)
    kernel_grad_second(1)
    sum_grad = total(grad)
    for o in objects:
        halo_finish(2, o, nat)
        per_image(o, act_grad(0))
        per_image(o, pre_grad0)
        pool_first(3, o, dzed)
    kernel_grad(act0)
    kernel_grad_start(0, [sum_grad, sum_grad + 3.0 * total(dzed)])
    for o in objects:
        pool_second(3, o)
    kernel_grad_middle(1)

    def send_taps(o):
        for a in range(4):
            for b in range(4):
                tg[o, a * 4 + b] = jnp.concatenate(
                    [grad[pl.ds(o * HALF + a * 8 + 4 * j + b, 24, stride=32), :] for j in range(2)], axis=0
                ).astype(BF16)
        for d in range(1, 16):
            other, where = group_a(d)
            send(tg.at[o, other], gg.at[o, mine], tsem.at[o, 0], tsem.at[o, 1], where)
        gg[o, mine] = tg[o, mine]

    pool_third(3, 0)
    add_bands(grad, 0, grad, dzed)
    send_taps(0)
    kernel_grad_second(0)
    pool_third(3, 1)
    add_bands(grad, 1, grad, dzed)
    send_taps(1)
    kernel_grad_third(1)
    kernel_grad_middle(0)
    finish(xg.at[mine], xsem.at[0])
    finish(xg.at[pl.ds(0, 8)], xsem.at[5])
    finish(xg.at[pl.ds(0, 8)], xsem.at[4])
    for o in range(2):
        fifteen(gg.at[o], tsem.at[o, 1])
        fifteen(tg.at[o], tsem.at[o, 0])
        taken = gg[o].reshape(768, 128)
        for part in range(4):
            at = slice(part * 256, (part + 1) * 256)
            product = lax.dot_general(
                taken, xg[:, 48 * o:48 * o + 48, at].reshape(768, 256),
                (((0,), (0,)), ((), ())), preferred_element_type=F32,
            )
            if o == 0:
                dwt[:, at] = product
            else:
                dwk[at, :] = (dwt[:, at] + product).T
            if o == 1 and part % 2 == 1:
                half = part // 2
                for other in range(16):
                    dws[half, other] = jnp.concatenate(
                        [dwk[pl.ds(512 * half + other * 4 + r, 8, stride=64), :] for r in range(4)], axis=0
                    ).astype(BF16)
                for d in range(1, 16):
                    other, where = group_b(d)
                    send(dws.at[half, other], dwr.at[half, t], dwsem.at[half, 0], dwsem.at[half, 1], where)
                dwr[half, t] = dws[half, t]
    taps = jnp.concatenate([tg[:, n].reshape(96, 128) for n in range(16)], axis=1)
    for part in range(4):
        at = slice(part * 256, (part + 1) * 256)
        tok_grad = lax.dot_general(
            taps, w_ref[at, :], (((1,), (1,)), ((), ())), preferred_element_type=F32
        )
        for o in range(2):
            for j in range(2):
                row = 48 * o + 24 * j
                dtok_ref[24 * o:24 * o + 24, j, at] = tok_grad[row:row + 24].astype(BF16)
    kernel_grad_third(0)
    kernel_grad_finish(1)
    for half in range(2):
        fifteen(dwr.at[half], dwsem.at[half, 1])
        fifteen(dws.at[half], dwsem.at[half, 0])
        fin[...] = sum16(dwr, half)
        for n in range(8):
            fins[8 * half + n, 0:4, :] = fin[pl.ds(n, 4, stride=8), :]
            fins[8 * half + n, 4:8, :] = jnp.zeros((4, 128), F32)
    for d in range(1, 16):
        other, where = group_a(d)
        send(fins.at[other], finr.at[mine], finsem.at[0], finsem.at[1], where)
    finr[mine] = fins[mine]
    kernel_grad_finish(0)
    fifteen(finr, finsem.at[1])
    fifteen(fins, finsem.at[0])
    for n in range(16):
        dw_ref[:, n * 128:(n + 1) * 128] = finr[n, 0:4, :]


def scratch():
    dma = pltpu.SemaphoreType.DMA
    vmem = pltpu.VMEM
    full = (TOTAL, 128)
    padded = (IMAGES * PADDED, 128)
    return [
        vmem(full, BF16), vmem((2, 1152, 128), BF16), dma((2,)),
        vmem((96, 1024), BF16), vmem((1024, 2048), BF16), dma((4,)),
        vmem(full, F32), vmem(full, F32), vmem(full, F32), vmem(full, BF16), vmem(full, BF16),
        vmem(full, F32), vmem(full, F32), vmem(full, F32), vmem((2, 128, 1152), BF16), vmem((IMAGES, CELLS, 1152), BF16),
        vmem(padded, F32), vmem(padded, F32), vmem(padded, F32),
        vmem((192, 128), F32), vmem((48, 128), F32), vmem((192, 128), F32), vmem((48, 128), F32),
        vmem((128, 128), F32), vmem((64, 128), F32),
        vmem((8, 3, 80, 128), BF16), vmem((8, 3, 80, 128), BF16),
        vmem((8, 64, 128), BF16), vmem((8, 3, 64, 128), BF16),
        vmem((8, 16, 128), BF16), vmem((8, 3, 16, 128), BF16),
        vmem((8, 32, 128), BF16), vmem((8, 4, 32, 128), BF16),
        vmem((8, 16, 128), BF16), vmem((8, 4, 16, 128), BF16),
        dma((8, 2)), dma((8, 2)), dma((8, 2)), dma((8, 4)), dma((8, 4)), dma((8, 4)), dma((8, 4)),
        vmem((6, 2, 32, 128), BF16), vmem((6, 2, 96, 128), BF16),
        vmem((6, 2, 32, 128), BF16), vmem((6, 2, 96, 128), BF16), vmem((6, 4, 32, 128), BF16),
        dma((6, 8)), dma((6, 8)),
        vmem((16, 96, 1024), BF16), dma((6,)),
        vmem((2, 16, 48, 128), BF16), vmem((2, 16, 48, 128), BF16), dma((2, 2)), vmem((128, 1024), F32),
        vmem((1024, 128), F32), vmem((2, 16, 32, 128), BF16), vmem((2, 16, 32, 128), BF16), dma((2, 2)),
        vmem((32, 128), F32), vmem((16, 8, 128), F32), vmem((16, 8, 128), F32), dma((2,)),
        vmem((16, 72, 128), F32), vmem((88, 128), F32), vmem((128, 1152), F32), vmem((2, 16, 80, 128), BF16), vmem((2, 16, 80, 128), BF16), dma((2, 2)),
        vmem((2, 16, 8, 128), F32), vmem((2, 16, 8, 128), F32), dma((2, 2)),
        vmem((2, 8, 128), F32), vmem((2, 16, 8, 128), F32), dma((2, 2)),
        vmem((2, 80, 128), BF16), vmem((2, 16, 80, 128), BF16), dma((2, 2)),
    ]


def results(dtok_ref, dw_ref, dk_ref, bias_ref, dtok_out, dw_out, dk_out, db_out, cb_out):
    dtok_out[...] = dtok_ref[...]
    dw_out[...] = dw_ref[...]
    dk_out[...] = dk_ref[...].astype(F32)
    db_out[...] = bias_ref[1:2, :]
    cb_out[0:1, :] = bias_ref[0:1, :]
    cb_out[1:2, :] = bias_ref[8:9, :]


def per_device(tokens, gout, deconv_weight, deconv_bias, conv_kernels, conv_biases):
    here = pl.BlockSpec(memory_space=pltpu.VMEM)
    anywhere = pl.BlockSpec(memory_space=pl.ANY)
    tok_grad, weight_grad, kernel_grads, biases = pl.pallas_call(
        kernel,
        out_shape=(
            jax.ShapeDtypeStruct((48, 2, 1024), BF16),
            jax.ShapeDtypeStruct((4, 2048), F32),
            jax.ShapeDtypeStruct((2, 1152, 128), BF16),
            jax.ShapeDtypeStruct((16, 128), F32),
        ),
        in_specs=[here, anywhere, anywhere, here, anywhere, here],
        out_specs=(here,) * 4,
        scratch_shapes=scratch(),
        compiler_params=pltpu.CompilerParams(
            collective_id=0, has_side_effects=True, vmem_limit_bytes=56 * 1024 * 1024
        ),
        name="triplane",
    )(
        tokens.reshape(48, 2, 1024), gout.reshape(TOTAL, 128), deconv_weight, deconv_bias.reshape(1, 128),
        conv_kernels, conv_biases.reshape(2, 1, 128),
    )
    tok_out, weight_out, kernel_out, bias_out, conv_bias_out = pl.pallas_call(
        results,
        out_shape=(
            jax.ShapeDtypeStruct((48, 2, 1024), BF16),
            jax.ShapeDtypeStruct((4, 2048), F32),
            jax.ShapeDtypeStruct((2, 1152, 128), F32),
            jax.ShapeDtypeStruct((1, 128), F32),
            jax.ShapeDtypeStruct((2, 128), F32),
        ),
        in_specs=[here] * 4,
        out_specs=(here,) * 5,
        name="results",
    )(tok_grad, weight_grad, kernel_grads, biases)
    return (tok_out.reshape(tokens.shape), weight_out, bias_out.reshape(128), kernel_out, conv_bias_out)


def solution(mesh):
    split = P("obj", None, "plane", "tile", None)
    return jax.shard_map(
        per_device,
        mesh=mesh,
        in_specs=(split, split, P(), P(), P(), P()),
        out_specs=(split, P(("obj", "plane", "tile"), None), P(), P(), P()),
        check_vma=False,
    )
```
